32 devices in a mesh: dp: 8 (over z, x), tensor: 4 (over y, core).
Axes of the slice: x: 2, y: 2, z: 4, core: 2. Of those that a mesh axis runs over, the one named last changes fastest.
Arguments:
- inputs: bfloat16 [8192, 2048], P(('dp', 'tensor')), may hold values from -6 to 6
- segment_ids: int32 [8192], P('dp'), may hold values from 0 to 127, never falling along the last dimension, each value on 1 to 1024 neighbouring positions
- gain_mixer: bfloat16 [2048], P('dp'), may hold values from 0.5 to 1.5
- branch_weight: bfloat16 [2048, 2560], P('dp', 'tensor'), may hold values from -0.125 to 0.125
- input_weight: bfloat16 [2048, 2560], P('dp', 'tensor'), may hold values from -0.125 to 0.125
- conv_weight: bfloat16 [4, 16, 160], P(None, 'tensor', 'dp'), may hold values from -3 to 3
- conv_bias: bfloat16 [16, 160], P('tensor', 'dp'), may hold values from -1.5 to 1.5
- rate_weight: bfloat16 [16, 160, 160], P('tensor', 'dp'), may hold values from -0.5 to 0.5
- rate_bias: bfloat16 [16, 160], P('tensor', 'dp'), may hold values from -3 to 3
- entry_weight: bfloat16 [16, 160, 160], P('tensor', 'dp'), may hold values from -0.5 to 0.5
- entry_bias: bfloat16 [16, 160], P('tensor', 'dp'), may hold values from -3 to 3
- decay_param: bfloat16 [16, 160], P('tensor', 'dp'), may hold values from 2 to 6
- output_weight: bfloat16 [2560, 2048], P('tensor', 'dp'), may hold values from -0.5 to 0.5
- gain_mlp: bfloat16 [2048], P('dp'), may hold values from 0.5 to 1.5
- gate_weight: bfloat16 [2048, 6144], P('dp', 'tensor'), may hold values from -0.125 to 0.125
- up_weight: bfloat16 [2048, 6144], P('dp', 'tensor'), may hold values from -0.125 to 0.125
- down_weight: bfloat16 [6144, 2048], P('tensor', 'dp'), may hold values from -0.15625 to 0.15625
- cotangent: bfloat16 [8192, 2048], P(('dp', 'tensor')), may hold values from -6 to 6
Outputs:
- layer_out: bfloat16 [8192, 2048], P(('dp', 'tensor'))
- inputs_grad: bfloat16 [8192, 2048], P(('dp', 'tensor'))
- gain_mixer_grad: float32 [2048], P('dp')
- branch_weight_grad: float32 [2048, 2560], P('dp', 'tensor')
- input_weight_grad: float32 [2048, 2560], P('dp', 'tensor')
- conv_weight_grad: float32 [4, 16, 160], P(None, 'tensor', 'dp')
- conv_bias_grad: float32 [16, 160], P('tensor', 'dp')
- rate_weight_grad: float32 [16, 160, 160], P('tensor', 'dp')
- rate_bias_grad: float32 [16, 160], P('tensor', 'dp')
- entry_weight_grad: float32 [16, 160, 160], P('tensor', 'dp')
- entry_bias_grad: float32 [16, 160], P('tensor', 'dp')
- decay_param_grad: float32 [16, 160], P('tensor', 'dp')
- output_weight_grad: float32 [2560, 2048], P('tensor', 'dp')
- gain_mlp_grad: float32 [2048], P('dp')
- gate_weight_grad: float32 [2048, 6144], P('dp', 'tensor')
- up_weight_grad: float32 [2048, 6144], P('dp', 'tensor')
- down_weight_grad: float32 [6144, 2048], P('tensor', 'dp')
The draws below stay inside these ranges and needn't reach their ends.
Inputs may be any that keep to these rules, and one draw needn't show every extreme that they name: `segment_ids`: ids never fall along the tokens; each document holds 1 to 1024 tokens, and a document that crosses a sequence's end restarts there.
All inputs are finite; a program needn't handle non-finite values.
Results may differ from the reference program's by a relative error of at most 0.023.
Values may be sent and summed in bfloat16 or wider, within the bound.
No kernel may reach another device: no remote copies, remote signals or barrier semaphores. Data moves between devices by JAX's collectives and lax.ppermute only.
A program may use at most 256 MiB of HBM per device.

```python
import math
import jax
import jax.numpy as jnp
import numpy as np
from jax import lax

D = 2048
H = 16
BW = 160
FF = 6144
CW = 4
R = 2560
SEQ = 1024
TOKENS = 8192
NDOCS = 128


def spiked(values, own_key, source, target, blocks, factor):
    def block_of(position):
        return (jnp.arange(values.shape[position]) // (values.shape[position] // blocks)).reshape((-1,) + (1,) * (values.ndim - 1 - position))

    one_side = jax.random.permutation(own_key, blocks)[block_of(target)]
    far = (block_of(target) + blocks // 2) % blocks
    return jnp.where((block_of(source) == one_side) | (block_of(source) == far), factor * values, values)


def block_levels(own_key, dims, pieces, low, high):
    factor_of = 1.0
    for position, blocks in pieces:
        heights = jax.random.uniform(jax.random.fold_in(jax.random.fold_in(own_key, 6), position), (blocks,), jnp.float32, low / len(pieces), high / len(pieces))
        factor_of = factor_of * jnp.repeat(jnp.exp(heights), dims[position] // blocks).reshape((-1,) + (1,) * (len(dims) - 1 - position))
    return factor_of


def profile(amount, total, limit, slope):
    loads = [(1 << 20) // math.isqrt(rank ** slope) + 1 for rank in range(2, amount + 1)]
    rest, counts = total - limit - (amount - 1), [1] * (amount - 1)
    while rest > 0:
        candidates = [i for i in range(amount - 1) if counts[i] < limit]
        pool, budget = sum([loads[i] for i in candidates]), rest
        for i in candidates:
            extra = min(limit - counts[i], max(1, budget * loads[i] // pool), rest)
            counts[i] = counts[i] + extra
            rest = rest - extra
    return np.array([limit] + counts)


def uneven(key, number_of, total, limit, skew):
    if number_of == 2:
        one = jax.random.randint(key, (), max(1, total - limit), min(limit, total - 1) + 1)
        return jnp.stack([one, total - one])
    sizes = jnp.asarray(profile(number_of, total, limit, skew), jnp.int32)
    pairs = (number_of - 1) // 2
    donor, receiver = sizes[1:1 + 2 * pairs:2], sizes[2:2 + 2 * pairs:2]
    margin = jnp.minimum(donor - 1, limit - receiver)
    passed = jax.random.randint(jax.random.fold_in(key, 1), (pairs,), 0, 1 << 20) % (margin + 1)
    sizes = sizes.at[1:1 + 2 * pairs:2].set(donor - passed).at[2:2 + 2 * pairs:2].set(receiver + passed)
    return sizes[jax.random.permutation(jax.random.fold_in(key, 2), number_of)]


def noise(rng, dims, scale, reach, cuts=(), kind=jnp.bfloat16):
    level = block_levels(rng, dims, cuts, -0.22, 0.18) if cuts else 1.0
    result = jax.random.normal(rng, dims, jnp.float32) * scale * level
    return jnp.minimum(jnp.maximum(result, -reach), reach).astype(kind)


def gaussian_with(rng, extent, scale, bound, cuts, heavy, kind=jnp.bfloat16):
    result = scale * jax.random.normal(rng, extent, jnp.float32)
    if cuts:
        result = result * block_levels(rng, extent, cuts, -0.22, 0.18)
    return jnp.clip(spiked(result, jax.random.fold_in(rng, 3), *heavy), -bound, bound).astype(kind)


def setup_inputs(seed: int = 0) -> dict:
    key_of = jax.random.split(jax.random.key(seed), 19)
    return {
        "inputs": noise(key_of[0], (TOKENS, D), 1.0, 6.0, ((0, 32),)),
        "segment_ids": jnp.searchsorted(jnp.cumsum(uneven(key_of[1], NDOCS, TOKENS, SEQ, 2)), jnp.arange(TOKENS), side="right").astype(jnp.int32),
        "gain_mixer": jnp.clip(1.0 + 0.1 * jax.random.normal(key_of[2], (D,), jnp.float32), 0.5, 1.5).astype(jnp.bfloat16),
        "branch_weight": noise(key_of[3], (D, R), D ** -0.5, 0.125, ((0, 8), (1, 4))),
        "input_weight": noise(key_of[4], (D, R), D ** -0.5, 0.125, ((0, 8), (1, 4))),
        "conv_weight": noise(key_of[5], (CW, H, BW), CW ** -0.5, 3.0, ((1, 4), (2, 8))),
        "conv_bias": noise(key_of[6], (H, BW), 0.3, 1.5, ((0, 4), (1, 8))),
        "rate_weight": noise(key_of[7], (H, BW, BW), BW ** -0.5, 0.5, ((0, 4), (1, 8))),
        "rate_bias": noise(key_of[8], (H, BW), 0.5, 3.0, ((0, 4), (1, 8))),
        "entry_weight": noise(key_of[9], (H, BW, BW), BW ** -0.5, 0.5, ((0, 4), (1, 8))),
        "entry_bias": noise(key_of[10], (H, BW), 0.5, 3.0, ((0, 4), (1, 8))),
        "decay_param": jnp.clip(2.0 + 4.0 * jax.random.uniform(key_of[11], (H, BW), jnp.float32) ** block_levels(key_of[11], (H, BW), ((0, 4), (1, 8)), -0.2, 0.2), 2.0, 6.0).astype(jnp.bfloat16),
        "output_weight": noise(key_of[12], (R, D), (R // 16) ** -0.5, 0.5, ((0, 4), (1, 8))),
        "gain_mlp": jnp.clip(1.0 + 0.1 * jax.random.normal(key_of[13], (D,), jnp.float32), 0.5, 1.5).astype(jnp.bfloat16),
        "gate_weight": noise(key_of[14], (D, FF), D ** -0.5, 0.125, ((0, 8), (1, 4))),
        "up_weight": noise(key_of[15], (D, FF), D ** -0.5, 0.125, ((0, 8), (1, 4))),
        "down_weight": noise(key_of[16], (FF, D), (FF // 4) ** -0.5, 0.15625, ((0, 4), (1, 8))),
        "cotangent": gaussian_with(key_of[17], (TOKENS, D), 1.0, 6.0, ((0, 32),), (0, 1, 32, 2.75)),
    }


epsilon = 1e-06
lru_scale = 8.0

@jax.custom_vjp
def low(v):
    return lax.optimization_barrier(v.astype(jnp.bfloat16)).astype(jnp.float32)

@jax.custom_vjp
def low_back(v):
    return v

def low_keep(v):
    return (low(v), None)

def low_pass(kept, grad):
    return (grad,)

def back_keep(v):
    return (v, None)

def back_low(kept, grad):
    return (low(grad),)
low.defvjp(low_keep, low_pass)
low_back.defvjp(back_keep, back_low)

def rms_norm(values, gain):
    scale = lax.rsqrt(lax.optimization_barrier(jnp.mean(values * values, axis=-1, keepdims=True)) + epsilon)
    return values * scale * gain

def shifted(values, offset, fill):
    head = jnp.full((offset,) + values.shape[1:], fill, values.dtype)
    return jnp.concatenate([head, values[:values.shape[0] - offset]], axis=0)

def combine(first, second):
    return (first[0] * second[0], second[0] * first[1] + second[1])

def recurrent_core(branch_pre, entry_pre, conv_weight, conv_bias, rate_weight, rate_bias, entry_weight, entry_bias, decay_param, segment_ids):
    length, width = entry_pre.shape
    blocks = rate_weight.shape[0]
    block_width = rate_weight.shape[1]
    taps = conv_weight.shape[0]
    kernel = conv_weight.reshape(taps, width)
    mixed = entry_pre * kernel[0] + conv_bias.reshape(width)
    for offset in range(1, taps):
        earlier = shifted(segment_ids, offset, -1)
        same = (earlier == segment_ids).astype(entry_pre.dtype)[:, None]
        mixed = mixed + shifted(entry_pre, offset, 0.0) * same * kernel[offset]
    grouped = mixed.reshape(length, blocks, block_width)
    highest = lax.Precision.HIGHEST
    rate_pre = jnp.einsum('lhi,hij->lhj', grouped, rate_weight, precision=highest) + rate_bias
    entry_gate_pre = jnp.einsum('lhi,hij->lhj', grouped, entry_weight, precision=highest) + entry_bias
    rate = jax.nn.sigmoid(rate_pre).reshape(length, width)
    entry = jax.nn.sigmoid(entry_gate_pre).reshape(length, width)
    log_decay = -lru_scale * rate * jax.nn.softplus(-decay_param.reshape(width))
    start = (shifted(segment_ids, 1, -1) != segment_ids)[:, None]
    decay = jnp.where(start, 0.0, jnp.exp(log_decay))
    factor = jnp.where(start, 1.0, jnp.sqrt(-jnp.expm1(2.0 * log_decay)))
    drive = factor * entry * mixed
    carried, state = lax.associative_scan(combine, (decay, drive), axis=0)
    return jax.nn.gelu(branch_pre) * state

def layer(tokens, segments, params):
    gain_mixer, branch_weight, input_weight, conv_weight, conv_bias, rate_weight, rate_bias, entry_weight, entry_bias, decay_param, output_weight, gain_mlp, gate_weight, up_weight, down_weight = params
    highest = lax.Precision.HIGHEST
    mixer_in = low(rms_norm(tokens, gain_mixer))
    branch_pre = low_back(jnp.dot(mixer_in, branch_weight, precision=highest))
    entry_pre = low_back(jnp.dot(mixer_in, input_weight, precision=highest))
    mixer_out = low(recurrent_core(branch_pre, entry_pre, conv_weight, conv_bias, rate_weight, rate_bias, entry_weight, entry_bias, decay_param, segments))
    middle = tokens + low_back(jnp.dot(mixer_out, output_weight, precision=highest))
    mlp_in = low(rms_norm(middle, gain_mlp))
    gate_pre = low_back(jnp.dot(mlp_in, gate_weight, precision=highest))
    up_pre = low_back(jnp.dot(mlp_in, up_weight, precision=highest))
    hidden = low(jax.nn.gelu(gate_pre) * up_pre)
    return middle + jnp.dot(hidden, down_weight, precision=highest)

def reference(inputs, segment_ids, gain_mixer, branch_weight, input_weight, conv_weight, conv_bias, rate_weight, rate_bias, entry_weight, entry_bias, decay_param, output_weight, gain_mlp, gate_weight, up_weight, down_weight, cotangent):
    params = tuple((item.astype(jnp.float32) for item in (gain_mixer, branch_weight, input_weight, conv_weight, conv_bias, rate_weight, rate_bias, entry_weight, entry_bias, decay_param, output_weight, gain_mlp, gate_weight, up_weight, down_weight)))
    sequences = inputs.shape[0] // SEQ
    tokens = inputs.astype(jnp.float32).reshape(sequences, SEQ, D)
    segments = segment_ids.reshape(sequences, SEQ)

    def forward(token_set, param_set):

        def one_sequence(pair):
            return layer(pair[0], pair[1], param_set)
        return lax.map(jax.checkpoint(one_sequence), (token_set, segments))
    outputs, backward = jax.vjp(forward, tokens, params)
    token_grad, grads = backward(cotangent.astype(jnp.float32).reshape(sequences, SEQ, D))
    gain_mixer_grad, branch_weight_grad, input_weight_grad, conv_weight_grad, conv_bias_grad, rate_weight_grad, rate_bias_grad, entry_weight_grad, entry_bias_grad, decay_param_grad, output_weight_grad, gain_mlp_grad, gate_weight_grad, up_weight_grad, down_weight_grad = grads
    layer_out = outputs.reshape(sequences * SEQ, D).astype(jnp.bfloat16)
    inputs_grad = token_grad.reshape(sequences * SEQ, D).astype(jnp.bfloat16)
    return (layer_out, inputs_grad, gain_mixer_grad, branch_weight_grad, input_weight_grad, conv_weight_grad, conv_bias_grad, rate_weight_grad, rate_bias_grad, entry_weight_grad, entry_bias_grad, decay_param_grad, output_weight_grad, gain_mlp_grad, gate_weight_grad, up_weight_grad, down_weight_grad)
```

```python
import functools

import jax
import jax.numpy as jnp
from jax import lax
from jax.experimental import pallas as pl
from jax.experimental.pallas import tpu as pltpu
from jax.sharding import PartitionSpec as P

epsilon = 1e-06
lru_scale = 8.0
root = 0.7978845608028654
cubic = 0.044715
f32 = jnp.float32
bf16 = jnp.bfloat16
vmem_bytes = 60 * 1024 * 1024


def gelu_both(value):
    square = value * value
    th = jnp.tanh(root * value * (1.0 + cubic * square))
    half = 0.5 * (1.0 + th)
    slope = half + 0.5 * value * (1.0 - th * th) * (root * (1.0 + 3.0 * cubic * square))
    return value * half, slope


def gelu(value):
    return value * (0.5 * (1.0 + jnp.tanh(root * value * (1.0 + cubic * value * value))))


def one_minus_exp(x, exp_x):
    series = 1.0 + x * (1.0 / 7.0)
    for order in (6.0, 5.0, 4.0, 3.0, 2.0):
        series = 1.0 + x * (1.0 / order) * series
    return jnp.where(x > -0.5, -x * series, 1.0 - exp_x)


def decay_terms(rate, slope, keep):
    log_decay = slope * rate
    expo = jnp.exp(log_decay)
    square = expo * expo
    factor = jnp.where(keep > 0.0, jnp.sqrt(one_minus_exp(2.0 * log_decay, square)), 1.0)
    return expo * keep, square, factor


def row_index(width):
    return lax.broadcasted_iota(jnp.int32, (8, width), 0)


def down_by(current, before, offset, rows):
    if offset == 0:
        return current
    return jnp.where(
        rows < offset, pltpu.roll(before, offset, 0), pltpu.roll(current, offset, 0)
    )


def up_by(current, after, offset, rows):
    if offset == 0:
        return current
    return jnp.where(
        rows < 8 - offset,
        pltpu.roll(current, 8 - offset, 0),
        pltpu.roll(after, 8 - offset, 0),
    )


def core_forward_kernel(
    place, branch, entry_pre, masks, gates, small, out, mixed_out, rate_out, entry_out, state_out,
    mixed_low, pre, last_entry, last_state,
):
    length, width = entry_pre.shape
    rows = row_index(width)

    @pl.when(pl.program_id(0) == 0)
    def _():
        last_entry[...] = jnp.zeros_like(last_entry)
        last_state[...] = jnp.zeros_like(last_state)

    taps = [small[k : k + 1, :] for k in range(4)]
    conv_bias = small[4:5, :]

    def convolve(step, before):
        parts = []
        for half in range(2):
            at = pl.ds(pl.multiple_of(step * 16 + half * 8, 8), 8)
            here = entry_pre[at, :]
            mask = masks[at, :]
            mixed = here * taps[0] + conv_bias
            for k in range(1, 4):
                mixed += down_by(here, before, k, rows) * mask[:, k : k + 1] * taps[k]
            mixed_out[at, :] = mixed
            parts.append(mixed)
            before = here
        mixed_low[pl.ds(pl.multiple_of(step * 16, 16), 16), :] = jnp.concatenate(
            parts, axis=0
        ).astype(bf16)
        return before

    last_entry[...] = lax.fori_loop(0, length // 16, convolve, last_entry[...])
    pre[...] = jnp.dot(mixed_low[...], gates[...], preferred_element_type=f32)
    rate_bias = small[5:6, :]
    entry_bias = small[6:7, :]
    slope = small[7:8, :]

    def scan(step, carry):
        parts = []
        for half in range(2):
            at = pl.ds(pl.multiple_of(step * 16 + half * 8, 8), 8)
            keep = masks[at, :][:, 0:1]
            rate = jax.nn.sigmoid(pre[at, :width] + rate_bias)
            entry = jax.nn.sigmoid(pre[at, width:] + entry_bias)
            decay, _, factor = decay_terms(rate, slope, keep)
            drive = factor * entry * mixed_out[at, :]
            for shift in (1, 2, 4):
                inside = rows >= shift
                drive += decay * jnp.where(inside, pltpu.roll(drive, shift, 0), 0.0)
                decay = decay * jnp.where(inside, pltpu.roll(decay, shift, 0), 1.0)
            state = drive + decay * carry
            carry = jnp.broadcast_to(state[7:8, :], state.shape)
            rate_out[at, :] = rate
            entry_out[at, :] = entry
            state_out[at, :] = state
            parts.append(gelu(branch[at, :]) * state)
        out[pl.ds(pl.multiple_of(step * 16, 16), 16), :] = jnp.concatenate(parts, axis=0).astype(
            bf16
        )
        return carry

    last_state[...] = lax.fori_loop(0, length // 16, scan, last_state[...])


def core_backward_kernel(
    place, grad, branch, entry_pre, mixed_in, rate_in, entry_in, state_in, state_tail, entry_tail,
    masks, gates, small, low, gate_grads, small_grads,
    state_long, entry_long, gate_low, mixed_grad, sums, next_decay, next_carried, next_mixed,
):
    length, width = entry_pre.shape
    rows = row_index(width)

    @pl.when(pl.program_id(0) == 0)
    def _():
        next_decay[...] = jnp.zeros_like(next_decay)
        next_carried[...] = jnp.zeros_like(next_carried)
        next_mixed[...] = jnp.zeros_like(next_mixed)
        sums[...] = jnp.zeros_like(sums)
        gate_grads[...] = jnp.zeros_like(gate_grads)

    state_long[0:8, :] = state_tail[...]
    state_long[8:, :] = state_in[...]
    entry_long[0:8, :] = entry_tail[...]
    entry_long[8:, :] = entry_pre[...]
    slope = small[7:8, :]

    def reverse(step, carry):
        after_decay, carried_after = carry
        step = length // 16 - 1 - step
        branch_parts, rate_parts, entry_parts = [], [], []
        for half in (1, 0):
            start = pl.multiple_of(step * 16 + half * 8, 8)
            at = pl.ds(start, 8)
            keep = masks[at, :][:, 0:1]
            rate = rate_in[at, :]
            entry = entry_in[at, :]
            mixed = mixed_in[at, :]
            decay, square, factor = decay_terms(rate, slope, keep)
            up = grad[at, :]
            act, act_slope = gelu_both(branch[at, :])
            state = state_in[at, :]
            branch_parts.append(up * state * act_slope)
            value = up * act
            ahead = up_by(decay, after_decay, 1, rows)
            after_decay = decay
            for shift in (1, 2, 4):
                inside = rows < 8 - shift
                value += ahead * jnp.where(inside, pltpu.roll(value, 8 - shift, 0), 0.0)
                ahead = ahead * jnp.where(inside, pltpu.roll(ahead, 8 - shift, 0), 1.0)
            carried = value + ahead * carried_after
            carried_after = jnp.broadcast_to(carried[0:1, :], carried.shape)
            earlier = down_by(state, state_long[at, :], 1, rows)
            driven = carried * entry
            log_grad = keep * (carried * earlier * decay - driven * mixed * square / factor)
            scaled = log_grad * rate
            rate_pre_grad = slope * scaled * (1.0 - rate)
            entry_pre_grad = driven * factor * mixed * (1.0 - entry)
            mixed_grad[at, :] = driven * factor
            sums[40:48, :] += rate_pre_grad
            sums[48:56, :] += entry_pre_grad
            sums[56:64, :] += scaled
            rate_parts.append(rate_pre_grad)
            entry_parts.append(entry_pre_grad)
        both = pl.ds(pl.multiple_of(step * 16, 16), 16)
        low[both, :width] = jnp.concatenate(branch_parts[::-1], axis=0).astype(bf16)
        gate_low[both, :width] = jnp.concatenate(rate_parts[::-1], axis=0).astype(bf16)
        gate_low[both, width:] = jnp.concatenate(entry_parts[::-1], axis=0).astype(bf16)
        return after_decay, carried_after

    after_decay, carried_after = lax.fori_loop(
        0, length // 16, reverse, (next_decay[...], next_carried[...])
    )
    next_decay[...] = after_decay
    next_carried[...] = carried_after
    mixed_grad[...] += lax.dot_general(
        gate_low[...], gates[...], (((1,), (1,)), ((), ())), preferred_element_type=f32
    )
    gate_grads[...] += lax.dot_general(
        mixed_in[...].astype(bf16),
        gate_low[...],
        (((0,), (0,)), ((), ())),
        preferred_element_type=f32,
    )
    taps = [small[k : k + 1, :] for k in range(4)]

    def convolve(step, after):
        step = length // 16 - 1 - step
        parts = []
        for half in (1, 0):
            start = pl.multiple_of(step * 16 + half * 8, 8)
            at = pl.ds(start, 8)
            mask = masks[at, :]
            here = mixed_grad[at, :]
            value = entry_pre[at, :]
            before = entry_long[at, :]
            sums[32:40, :] += here
            sums[0:8, :] += here * value
            total = here * taps[0]
            masked = [here * mask[:, k : k + 1] for k in range(1, 4)]
            for k in range(1, 4):
                sums[8 * k : 8 * k + 8, :] += masked[k - 1] * down_by(value, before, k, rows)
                total += up_by(masked[k - 1], after[k - 1], k, rows) * taps[k]
            after = masked
            parts.append(total)
        low[pl.ds(pl.multiple_of(step * 16, 16), 16), width:] = jnp.concatenate(
            parts[::-1], axis=0
        ).astype(bf16)
        return after

    after = lax.fori_loop(
        0,
        length // 16,
        convolve,
        [next_mixed[8 * k : 8 * k + 8, :] for k in range(3)],
    )
    for k in range(3):
        next_mixed[8 * k : 8 * k + 8, :] = after[k]

    @pl.when(pl.program_id(0) == pl.num_programs(0) - 1)
    def _():
        for k in range(8):
            small_grads[k : k + 1, :] = jnp.sum(sums[8 * k : 8 * k + 8, :], axis=0, keepdims=True)


def core_forward(place, pre, masks, gates, small, blocks):
    total, width = pre.shape[0], pre.shape[1] // 2
    length = total // blocks
    wide = lambda column: pl.BlockSpec((length, width), lambda b, t: (b ^ t[0], column))
    whole = lambda shape: pl.BlockSpec(shape, lambda b, t: (0, 0))
    kept = jax.ShapeDtypeStruct((total, width), f32)
    return pl.pallas_call(
        core_forward_kernel,
        grid_spec=pltpu.PrefetchScalarGridSpec(
            num_scalar_prefetch=1,
            grid=(blocks,),
            in_specs=[
                wide(0),
                wide(1),
                pl.BlockSpec((length, 128), lambda b, t: (b, 0)),
                whole(gates.shape),
                whole(small.shape),
            ],
            out_specs=[wide(0)] * 5,
            scratch_shapes=[
                pltpu.VMEM((length, width), bf16),
                pltpu.VMEM((length, 2 * width), f32),
                pltpu.VMEM((8, width), f32),
                pltpu.VMEM((8, width), f32),
            ],
        ),
        out_shape=[jax.ShapeDtypeStruct((total, width), bf16)] + [kept] * 4,
        compiler_params=pltpu.CompilerParams(vmem_limit_bytes=vmem_bytes),
        cost_estimate=pl.CostEstimate(
            flops=4 * total * width * width, bytes_accessed=32 * total * width, transcendentals=0
        ),
        name="core_forward",
    )(place, pre, pre, masks, gates, small)


def core_backward(place, grad, pre, mixed, rate, entry, state, masks, gates, small, blocks):
    total, width = grad.shape
    length = total // blocks
    back = lambda g: blocks - 1 - g
    wide = lambda column: pl.BlockSpec((length, width), lambda g, t: (back(g) ^ t[0], column))
    whole = lambda shape: pl.BlockSpec(shape, lambda g, t: (0, 0))

    def tail(column):
        def at(g, t):
            block = jnp.maximum(back(g) - 1, 0) ^ t[0]
            return (block * (length // 8) + length // 8 - 1, column)

        return pl.BlockSpec((8, width), at)

    return pl.pallas_call(
        core_backward_kernel,
        grid_spec=pltpu.PrefetchScalarGridSpec(
            num_scalar_prefetch=1,
            grid=(blocks,),
            in_specs=[
                wide(0),
                wide(0),
                wide(1),
                wide(0),
                wide(0),
                wide(0),
                wide(0),
                tail(0),
                tail(1),
                pl.BlockSpec((length, 128), lambda g, t: (back(g), 0)),
                whole(gates.shape),
                whole(small.shape),
            ],
            out_specs=[
                pl.BlockSpec((length, 2 * width), lambda g, t: (back(g) ^ t[0], 0)),
                whole(gates.shape),
                whole((8, width)),
            ],
            scratch_shapes=[
                pltpu.VMEM((length + 8, width), f32),
                pltpu.VMEM((length + 8, width), f32),
                pltpu.VMEM((length, 2 * width), bf16),
                pltpu.VMEM((length, width), f32),
                pltpu.VMEM((64, width), f32),
                pltpu.VMEM((8, width), f32),
                pltpu.VMEM((8, width), f32),
                pltpu.VMEM((24, width), f32),
            ],
        ),
        out_shape=[
            jax.ShapeDtypeStruct((total, 2 * width), bf16),
            jax.ShapeDtypeStruct(gates.shape, f32),
            jax.ShapeDtypeStruct((8, width), f32),
        ],
        compiler_params=pltpu.CompilerParams(vmem_limit_bytes=vmem_bytes),
        cost_estimate=pl.CostEstimate(
            flops=8 * total * width * width, bytes_accessed=40 * total * width, transcendentals=0
        ),
        name="core_backward",
    )(place, grad, pre, pre, mixed, rate, entry, state, state, pre, masks, gates, small)


def dot(left, right):
    return jnp.dot(left, right, preferred_element_type=f32)


def dot_rows(left, right):
    return lax.dot_general(left, right, (((0,), (0,)), ((), ())), preferred_element_type=f32)


def dot_back(left, right):
    return lax.dot_general(left, right, (((1,), (1,)), ((), ())), preferred_element_type=f32)


class Ring:
    def __init__(self, count):
        self.count = count
        order = list(range(0, count, 2)) + list(range(1, count, 2))[::-1]
        self.order = order
        self.place_of = [order.index(index) for index in range(count)]
        self.ahead = [(order[(i + 1) % count], order[i]) for i in range(count)]
        self.behind = [(order[i], order[(i + 1) % count]) for i in range(count)]
        self.place = jnp.asarray(self.place_of, jnp.int32)[lax.axis_index("dp")]

    def reach(self, far):
        return self.count // 2 if far else (self.count - 1) // 2

    def gather(self, own, far):
        count = self.count
        blocks = [own] + [None] * (count - 1)
        reach = self.reach(far)
        for r in range(1, count):
            if r <= reach:
                blocks[r] = lax.ppermute(blocks[r - 1], "dp", self.ahead)
            if r <= count - 1 - reach:
                blocks[count - r] = lax.ppermute(blocks[(count - r + 1) % count], "dp", self.behind)
        return blocks

    def scatter(self, part, far):
        count = self.count
        reach = self.reach(far)
        steps = max(reach, count - 1 - reach)
        right = left = None
        right_sum = left_sum = None
        for r in range(steps, 0, -1):
            if r <= reach:
                value = part(r)
                if right is not None:
                    value = value + right.astype(f32)
                right = lax.ppermute(value.astype(bf16), "dp", self.behind)
            if r <= count - 1 - reach:
                value = part(count - r)
                if left is not None:
                    value = value + left.astype(f32)
                left = lax.ppermute(value.astype(bf16), "dp", self.ahead)
        return part(0) + right.astype(f32) + left.astype(f32)

    def scatter_direct(self, blocks):
        total = blocks[0]
        for r in range(1, self.count):
            pairs = [
                (self.order[i], self.order[(i + r) % self.count]) for i in range(self.count)
            ]
            total = total + lax.ppermute(blocks[r], "dp", pairs)
        return total

    def from_whole(self, whole, axis, size):
        ordered = [lax.slice_in_dim(whole, i * size, (i + 1) * size, axis=axis) for i in self.order]
        return lax.dynamic_slice_in_dim(
            jnp.concatenate(ordered + ordered, axis=axis),
            self.place * size,
            self.count * size,
            axis=axis,
        )

    def to_whole(self, ringed, axis, size):
        start = lax.rem(self.count - self.place, self.count) * size
        ordered = lax.dynamic_slice_in_dim(
            jnp.concatenate([ringed, ringed], axis=axis), start, self.count * size, axis=axis
        )
        return jnp.concatenate(
            [
                lax.slice_in_dim(ordered, i * size, (i + 1) * size, axis=axis)
                for i in self.place_of
            ],
            axis=axis,
        )


core_pairs = [(0, 1), (1, 0), (2, 3), (3, 2)]
chip_pairs = [(0, 2), (1, 3), (2, 0), (3, 1)]


def tensor_gather(own):
    sibling = lax.ppermute(own, "tensor", core_pairs)
    across = lax.ppermute(own, "tensor", chip_pairs)
    far = lax.ppermute(across, "tensor", core_pairs)
    return jnp.concatenate([own, sibling, across, far], axis=0)


def tensor_scatter(part):
    far = lax.ppermute(part(3).astype(bf16), "tensor", core_pairs)
    across = lax.ppermute((part(2) + far.astype(f32)).astype(bf16), "tensor", chip_pairs)
    sibling = lax.ppermute(part(1).astype(bf16), "tensor", core_pairs)
    return part(0) + sibling.astype(f32) + across.astype(f32)


def tensor_sum(value):
    value = value + lax.ppermute(value, "tensor", core_pairs)
    return value + lax.ppermute(value, "tensor", chip_pairs)


def norm_forward(values, gain):
    scale = lax.rsqrt(jnp.mean(values * values, axis=-1, keepdims=True) + epsilon)
    return scale, values * scale * gain


def norm_backward(values, scale, gain, grad):
    weighted = grad * gain
    inner = jnp.mean(weighted * values, axis=-1, keepdims=True)
    row_grad = scale * weighted - values * (scale * scale * scale * inner)
    return row_grad, jnp.sum(grad * values * scale, axis=0)


def body(
    inputs,
    segment_ids,
    gain_mixer,
    branch_weight,
    input_weight,
    conv_weight,
    conv_bias,
    rate_weight,
    rate_bias,
    entry_weight,
    entry_bias,
    decay_param,
    output_weight,
    gain_mlp,
    gate_weight,
    up_weight,
    down_weight,
    cotangent,
    *,
    dp,
    tensor,
):
    ring = Ring(dp)
    shard, width = branch_weight.shape
    features = inputs.shape[1]
    rows = inputs.shape[0]
    length = segment_ids.shape[0]
    gate_blocks, piece, block_width = rate_weight.shape
    taps = conv_weight.shape[0]
    place = lax.axis_index("tensor").astype(jnp.int32).reshape(1)

    columns = jnp.stack(
        [conv_weight[k] for k in range(taps)] + [conv_bias, rate_bias, entry_bias, decay_param],
        axis=-1,
    )
    table = jnp.concatenate([rate_weight, entry_weight, columns], axis=-1)
    table = table.reshape(gate_blocks * piece, table.shape[-1])
    table_rows, table_columns = table.shape
    wide = -(-table_columns // 128) * 128
    high = -(-(table_rows + 2) // 16) * 16
    gains = jnp.pad(jnp.stack([gain_mixer, gain_mlp]), ((0, 0), (0, wide - shard)))
    table = jnp.concatenate(
        [jnp.pad(table, ((0, 0), (0, wide - table_columns))), gains], axis=0
    )
    table = jnp.pad(table, ((0, high - table_rows - 2), (0, 0)))

    tables = jnp.stack(ring.gather(table, True))
    gain_one = tables[:, table_rows, :shard].reshape(features).astype(f32)
    gain_two = tables[:, table_rows + 1, :shard].reshape(features).astype(f32)
    whole_table = ring.to_whole(tables[:, :table_rows], 0, 1)
    whole_table = (
        whole_table.reshape(dp, gate_blocks, piece, wide)
        .transpose(1, 0, 2, 3)
        .reshape(width, wide)
    )
    channel_block = jnp.arange(width) // block_width
    same_block = channel_block[:, None] == channel_block[None, :]

    def spread(weights):
        return jnp.where(same_block, jnp.tile(weights, (1, gate_blocks)), jnp.zeros((), bf16))

    gates = jnp.concatenate(
        [
            spread(whole_table[:, :block_width]),
            spread(whole_table[:, block_width : 2 * block_width]),
        ],
        axis=1,
    )
    small = whole_table[:, 2 * block_width : 2 * block_width + 8].astype(f32).T
    decay_full = small[7]
    small = jnp.concatenate(
        [small[:7], -lru_scale * jax.nn.softplus(-decay_full)[None]], axis=0
    )

    masks = []
    for offset in range(1, taps):
        earlier = jnp.concatenate(
            [jnp.full((offset,), -1, segment_ids.dtype), segment_ids[: length - offset]]
        )
        masks.append((earlier == segment_ids).astype(f32))
    masks = jnp.stack([masks[0]] + masks, axis=1)
    masks = jnp.pad(masks, ((0, 0), (0, 128 - taps)))

    tokens = ring.from_whole(inputs, 1, shard).astype(f32)
    cotangent_own = ring.from_whole(cotangent, 1, shard)
    scale_one, mixer_in = norm_forward(tokens, gain_one)
    mixer_rows = tensor_gather(mixer_in.astype(bf16))
    pair_weight = jnp.concatenate(
        [
            jnp.concatenate(ring.gather(branch_weight, True), axis=0),
            jnp.concatenate(ring.gather(input_weight, False), axis=0),
        ],
        axis=1,
    )
    pre = dot(mixer_rows, pair_weight)
    mixer_low, mixed, rate, entry, state = core_forward(
        place, pre, masks, gates, small, tensor
    )
    output_full = jnp.concatenate(ring.gather(output_weight, True), axis=1)

    def block(array, j):
        return lax.slice_in_dim(array, j * rows, (j + 1) * rows, axis=0)

    middle = tokens + tensor_scatter(lambda j: dot(block(mixer_low, j), output_full))
    scale_two, mlp_in = norm_forward(middle, gain_two)
    mlp_rows = tensor_gather(mlp_in.astype(bf16))
    cotangent_rows = tensor_gather(cotangent_own)

    gate_full = jnp.concatenate(ring.gather(gate_weight, True), axis=0)
    up_full = jnp.concatenate(ring.gather(up_weight, False), axis=0)
    down_full = jnp.concatenate(ring.gather(down_weight, False), axis=1)
    gate_pre = dot(mlp_rows, gate_full)
    up_pre = dot(mlp_rows, up_full)
    act, act_slope = gelu_both(gate_pre)
    hidden_low = (act * up_pre).astype(bf16)

    def columns_of(array, r):
        return lax.slice_in_dim(array, r * shard, (r + 1) * shard, axis=1)

    down_grad = ring.scatter(lambda r: dot_rows(hidden_low, columns_of(cotangent_rows, r)), False)
    hidden_grad = dot_back(cotangent_rows, down_full)
    gate_low = (hidden_grad * up_pre * act_slope).astype(bf16)
    up_low = (hidden_grad * act).astype(bf16)
    mlp_in_grad = tensor_scatter(
        lambda j: dot_back(block(gate_low, j), gate_full) + dot_back(block(up_low, j), up_full)
    )
    gate_wgrad = ring.scatter(lambda r: dot_rows(columns_of(mlp_rows, r), gate_low), True)
    up_wgrad = ring.scatter(lambda r: dot_rows(columns_of(mlp_rows, r), up_low), False)
    middle_norm_grad, gain_two_part = norm_backward(middle, scale_two, gain_two, mlp_in_grad)
    middle_grad = cotangent_own.astype(f32) + middle_norm_grad
    residual_rows = tensor_gather(middle_grad.astype(bf16))

    mixer_grad = dot_back(residual_rows, output_full)
    pair_low, gate_grads, small_grads = core_backward(
        place, mixer_grad, pre, mixed, rate, entry, state, masks, gates, small, tensor
    )
    mixer_in_grad = tensor_scatter(lambda j: dot_back(block(pair_low, j), pair_weight))
    output_wgrad = ring.scatter(lambda r: dot_rows(mixer_low, columns_of(residual_rows, r)), True)
    branch_low = pair_low[:, :width]
    entry_low = pair_low[:, width:]
    branch_wgrad = ring.scatter(lambda r: dot_rows(columns_of(mixer_rows, r), branch_low), True)
    input_wgrad = ring.scatter(lambda r: dot_rows(columns_of(mixer_rows, r), entry_low), False)

    def folded(grads):
        kept = jnp.where(same_block, grads, 0.0).reshape(width, gate_blocks, block_width)
        return jnp.sum(kept, axis=1)

    decay_grad = lru_scale * small_grads[7:8] * jax.nn.sigmoid(-decay_full)[None]
    small_columns = jnp.concatenate([small_grads[:7], decay_grad], axis=0).T
    grad_table = jnp.concatenate(
        [folded(gate_grads[:, :width]), folded(gate_grads[:, width:]), small_columns], axis=1
    ).astype(bf16)
    grad_table = jnp.pad(grad_table, ((0, 0), (0, wide - table_columns)))
    grad_table = (
        grad_table.reshape(gate_blocks, dp, piece, wide)
        .transpose(1, 0, 2, 3)
        .reshape(dp, table_rows, wide)
    )
    grad_tables = ring.from_whole(grad_table, 0, 1)
    table_grad = ring.scatter(lambda r: grad_tables[r].astype(f32), True)
    table_grad = table_grad.reshape(gate_blocks, piece, wide)
    rate_wgrad = table_grad[:, :, :block_width]
    entry_wgrad = table_grad[:, :, block_width : 2 * block_width]
    singles = [table_grad[:, :, 2 * block_width + k] for k in range(taps + 4)]

    mlp_sum = tensor_scatter(lambda j: dot(block(hidden_low, j), down_full))
    layer_out = ring.to_whole((middle + mlp_sum).astype(bf16), 1, shard)
    tokens_norm_grad, gain_one_part = norm_backward(tokens, scale_one, gain_one, mixer_in_grad)
    inputs_grad = ring.to_whole((middle_grad + tokens_norm_grad).astype(bf16), 1, shard)
    gain_parts = tensor_sum(jnp.stack([gain_one_part, gain_two_part]))
    gain_sums = ring.scatter_direct([columns_of(gain_parts, r) for r in range(dp)])
    return (
        layer_out,
        inputs_grad,
        gain_sums[0],
        branch_wgrad,
        input_wgrad,
        jnp.stack(singles[:taps]),
        singles[taps],
        rate_wgrad,
        singles[taps + 1],
        entry_wgrad,
        singles[taps + 2],
        singles[taps + 3],
        output_wgrad,
        gain_sums[1],
        gate_wgrad,
        up_wgrad,
        down_grad,
    )


def solution(mesh):
    return jax.shard_map(
        functools.partial(body, dp=mesh.shape["dp"], tensor=mesh.shape["tensor"]),
        mesh=mesh,
        in_specs=(
            P(("dp", "tensor"), None),
            P("dp"),
            P("dp"),
            P("dp", "tensor"),
            P("dp", "tensor"),
            P(None, "tensor", "dp"),
            P("tensor", "dp"),
            P("tensor", "dp", None),
            P("tensor", "dp"),
            P("tensor", "dp", None),
            P("tensor", "dp"),
            P("tensor", "dp"),
            P("tensor", "dp"),
            P("dp"),
            P("dp", "tensor"),
            P("dp", "tensor"),
            P("tensor", "dp"),
            P(("dp", "tensor"), None),
        ),
        out_specs=(
            P(("dp", "tensor"), None),
            P(("dp", "tensor"), None),
            P("dp"),
            P("dp", "tensor"),
            P("dp", "tensor"),
            P(None, "tensor", "dp"),
            P("tensor", "dp"),
            P("tensor", "dp", None),
            P("tensor", "dp"),
            P("tensor", "dp", None),
            P("tensor", "dp"),
            P("tensor", "dp"),
            P("tensor", "dp"),
            P("dp"),
            P("dp", "tensor"),
            P("dp", "tensor"),
            P("tensor", "dp"),
        ),
        check_vma=False,
    )
```

```python
import functools

import jax
import jax.numpy as jnp
from jax import lax
from jax.experimental import pallas as pl
from jax.experimental.pallas import tpu as pltpu
from jax.sharding import PartitionSpec as P

epsilon = 1e-06
lru_scale = 8.0
root = 0.7978845608028654
cubic = 0.044715
f32 = jnp.float32
bf16 = jnp.bfloat16
vmem_bytes = 56 * 1024 * 1024
light = pl.CostEstimate(flops=1000, bytes_accessed=1000, transcendentals=0)


def gelu_both(value):
    square = value * value
    th = jnp.tanh(root * value * (1.0 + cubic * square))
    half = 0.5 * (1.0 + th)
    slope = half + 0.5 * value * (1.0 - th * th) * (root * (1.0 + 3.0 * cubic * square))
    return value * half, slope


def gelu(value):
    return value * (0.5 * (1.0 + jnp.tanh(root * value * (1.0 + cubic * value * value))))


def one_minus_exp(x, exp_x):
    series = 1.0 + x * (1.0 / 7.0)
    for order in (6.0, 5.0, 4.0, 3.0, 2.0):
        series = 1.0 + x * (1.0 / order) * series
    return jnp.where(x > -0.5, -x * series, 1.0 - exp_x)


def decay_terms(rate, slope, keep):
    log_decay = slope * rate
    expo = jnp.exp(log_decay)
    square = expo * expo
    factor = jnp.where(keep > 0.0, jnp.sqrt(one_minus_exp(2.0 * log_decay, square)), 1.0)
    return expo * keep, square, factor


def row_index(width):
    return lax.broadcasted_iota(jnp.int32, (8, width), 0)


def down_by(current, before, offset, rows):
    if offset == 0:
        return current
    return jnp.where(
        rows < offset, pltpu.roll(before, offset, 0), pltpu.roll(current, offset, 0)
    )


def up_by(current, after, offset, rows):
    if offset == 0:
        return current
    return jnp.where(
        rows < 8 - offset,
        pltpu.roll(current, 8 - offset, 0),
        pltpu.roll(after, 8 - offset, 0),
    )


def core_forward_kernel(
    place, branch, entry_pre, masks, gates, small, out, mixed_out, rate_out, entry_out, state_out,
    mixed_low, pre, last_entry, last_state,
):
    length, width = entry_pre.shape
    rows = row_index(width)

    @pl.when(pl.program_id(0) == 0)
    def _():
        last_entry[...] = jnp.zeros_like(last_entry)
        last_state[...] = jnp.zeros_like(last_state)

    taps = [small[k : k + 1, :] for k in range(4)]
    conv_bias = small[4:5, :]

    def convolve(step, before):
        parts = []
        for half in range(2):
            at = pl.ds(pl.multiple_of(step * 16 + half * 8, 8), 8)
            here = entry_pre[at, :]
            mask = masks[at, :]
            mixed = here * taps[0] + conv_bias
            for k in range(1, 4):
                mixed += down_by(here, before, k, rows) * mask[:, k : k + 1] * taps[k]
            mixed_out[at, :] = mixed
            parts.append(mixed)
            before = here
        mixed_low[pl.ds(pl.multiple_of(step * 16, 16), 16), :] = jnp.concatenate(
            parts, axis=0
        ).astype(bf16)
        return before

    last_entry[...] = lax.fori_loop(0, length // 16, convolve, last_entry[...])
    pre[...] = jnp.dot(mixed_low[...], gates[...], preferred_element_type=f32)
    rate_bias = small[5:6, :]
    entry_bias = small[6:7, :]
    slope = small[7:8, :]

    def scan(step, carry):
        parts = []
        for half in range(2):
            at = pl.ds(pl.multiple_of(step * 16 + half * 8, 8), 8)
            keep = masks[at, :][:, 0:1]
            rate = jax.nn.sigmoid(pre[at, :width] + rate_bias)
            entry = jax.nn.sigmoid(pre[at, width:] + entry_bias)
            decay, _, factor = decay_terms(rate, slope, keep)
            drive = factor * entry * mixed_out[at, :]
            for shift in (1, 2, 4):
                inside = rows >= shift
                drive += decay * jnp.where(inside, pltpu.roll(drive, shift, 0), 0.0)
                decay = decay * jnp.where(inside, pltpu.roll(decay, shift, 0), 1.0)
            state = drive + decay * carry
            carry = jnp.broadcast_to(state[7:8, :], state.shape)
            rate_out[at, :] = rate
            entry_out[at, :] = entry
            state_out[at, :] = state
            parts.append(gelu(branch[at, :]) * state)
        out[pl.ds(pl.multiple_of(step * 16, 16), 16), :] = jnp.concatenate(parts, axis=0).astype(
            bf16
        )
        return carry

    last_state[...] = lax.fori_loop(0, length // 16, scan, last_state[...])


def core_backward_kernel(
    place, grad, branch, entry_pre, mixed_in, rate_in, entry_in, state_in, state_tail, entry_tail,
    masks, gates, small, low, gate_grads, small_grads,
    state_long, entry_long, gate_low, mixed_grad, sums, next_decay, next_carried, next_mixed,
):
    length, width = entry_pre.shape
    rows = row_index(width)

    @pl.when(pl.program_id(0) == 0)
    def _():
        next_decay[...] = jnp.zeros_like(next_decay)
        next_carried[...] = jnp.zeros_like(next_carried)
        next_mixed[...] = jnp.zeros_like(next_mixed)
        sums[...] = jnp.zeros_like(sums)
        gate_grads[...] = jnp.zeros_like(gate_grads)

    state_long[0:8, :] = state_tail[...]
    state_long[8:, :] = state_in[...]
    entry_long[0:8, :] = entry_tail[...]
    entry_long[8:, :] = entry_pre[...]
    slope = small[7:8, :]

    def reverse(step, carry):
        after_decay, carried_after = carry
        step = length // 16 - 1 - step
        branch_parts, rate_parts, entry_parts = [], [], []
        for half in (1, 0):
            start = pl.multiple_of(step * 16 + half * 8, 8)
            at = pl.ds(start, 8)
            keep = masks[at, :][:, 0:1]
            rate = rate_in[at, :]
            entry = entry_in[at, :]
            mixed = mixed_in[at, :]
            decay, square, factor = decay_terms(rate, slope, keep)
            up = grad[at, :]
            act, act_slope = gelu_both(branch[at, :])
            state = state_in[at, :]
            branch_parts.append(up * state * act_slope)
            value = up * act
            ahead = up_by(decay, after_decay, 1, rows)
            after_decay = decay
            for shift in (1, 2, 4):
                inside = rows < 8 - shift
                value += ahead * jnp.where(inside, pltpu.roll(value, 8 - shift, 0), 0.0)
                ahead = ahead * jnp.where(inside, pltpu.roll(ahead, 8 - shift, 0), 1.0)
            carried = value + ahead * carried_after
            carried_after = jnp.broadcast_to(carried[0:1, :], carried.shape)
            earlier = down_by(state, state_long[at, :], 1, rows)
            driven = carried * entry
            log_grad = keep * (carried * earlier * decay - driven * mixed * square / factor)
            scaled = log_grad * rate
            rate_pre_grad = slope * scaled * (1.0 - rate)
            entry_pre_grad = driven * factor * mixed * (1.0 - entry)
            mixed_grad[at, :] = driven * factor
            sums[40:48, :] += rate_pre_grad
            sums[48:56, :] += entry_pre_grad
            sums[56:64, :] += scaled
            rate_parts.append(rate_pre_grad)
            entry_parts.append(entry_pre_grad)
        both = pl.ds(pl.multiple_of(step * 16, 16), 16)
        low[both, :width] = jnp.concatenate(branch_parts[::-1], axis=0).astype(bf16)
        gate_low[both, :width] = jnp.concatenate(rate_parts[::-1], axis=0).astype(bf16)
        gate_low[both, width:] = jnp.concatenate(entry_parts[::-1], axis=0).astype(bf16)
        return after_decay, carried_after

    after_decay, carried_after = lax.fori_loop(
        0, length // 16, reverse, (next_decay[...], next_carried[...])
    )
    next_decay[...] = after_decay
    next_carried[...] = carried_after
    mixed_grad[...] += lax.dot_general(
        gate_low[...], gates[...], (((1,), (1,)), ((), ())), preferred_element_type=f32
    )
    gate_grads[...] += lax.dot_general(
        mixed_in[...].astype(bf16),
        gate_low[...],
        (((0,), (0,)), ((), ())),
        preferred_element_type=f32,
    )
    taps = [small[k : k + 1, :] for k in range(4)]

    def convolve(step, after):
        step = length // 16 - 1 - step
        parts = []
        for half in (1, 0):
            start = pl.multiple_of(step * 16 + half * 8, 8)
            at = pl.ds(start, 8)
            mask = masks[at, :]
            here = mixed_grad[at, :]
            value = entry_pre[at, :]
            before = entry_long[at, :]
            sums[32:40, :] += here
            sums[0:8, :] += here * value
            total = here * taps[0]
            masked = [here * mask[:, k : k + 1] for k in range(1, 4)]
            for k in range(1, 4):
                sums[8 * k : 8 * k + 8, :] += masked[k - 1] * down_by(value, before, k, rows)
                total += up_by(masked[k - 1], after[k - 1], k, rows) * taps[k]
            after = masked
            parts.append(total)
        low[pl.ds(pl.multiple_of(step * 16, 16), 16), width:] = jnp.concatenate(
            parts[::-1], axis=0
        ).astype(bf16)
        return after

    after = lax.fori_loop(
        0,
        length // 16,
        convolve,
        [next_mixed[8 * k : 8 * k + 8, :] for k in range(3)],
    )
    for k in range(3):
        next_mixed[8 * k : 8 * k + 8, :] = after[k]

    @pl.when(pl.program_id(0) == pl.num_programs(0) - 1)
    def _():
        for k in range(8):
            small_grads[k : k + 1, :] = jnp.sum(sums[8 * k : 8 * k + 8, :], axis=0, keepdims=True)


def core_forward(place, pre, masks, gates, small, blocks):
    total, width = pre.shape[0], pre.shape[1] // 2
    length = total // blocks
    wide = lambda column: pl.BlockSpec((length, width), lambda b, t: (b ^ t[0], column))
    whole = lambda shape: pl.BlockSpec(shape, lambda b, t: (0, 0))
    kept = jax.ShapeDtypeStruct((total, width), f32)
    return pl.pallas_call(
        core_forward_kernel,
        grid_spec=pltpu.PrefetchScalarGridSpec(
            num_scalar_prefetch=1,
            grid=(blocks,),
            in_specs=[
                wide(0),
                wide(1),
                pl.BlockSpec((length, 128), lambda b, t: (b, 0)),
                whole(gates.shape),
                whole(small.shape),
            ],
            out_specs=[wide(0)] * 5,
            scratch_shapes=[
                pltpu.VMEM((length, width), bf16),
                pltpu.VMEM((length, 2 * width), f32),
                pltpu.VMEM((8, width), f32),
                pltpu.VMEM((8, width), f32),
            ],
        ),
        out_shape=[jax.ShapeDtypeStruct((total, width), bf16)] + [kept] * 4,
        compiler_params=pltpu.CompilerParams(vmem_limit_bytes=vmem_bytes),
        cost_estimate=light,
        name="core_forward",
    )(place, pre, pre, masks, gates, small)


def core_backward(place, grad, pre, mixed, rate, entry, state, masks, gates, small, blocks):
    total, width = grad.shape
    length = total // blocks
    back = lambda g: blocks - 1 - g
    wide = lambda column: pl.BlockSpec((length, width), lambda g, t: (back(g) ^ t[0], column))
    whole = lambda shape: pl.BlockSpec(shape, lambda g, t: (0, 0))

    def tail(column):
        def at(g, t):
            block = jnp.maximum(back(g) - 1, 0) ^ t[0]
            return (block * (length // 8) + length // 8 - 1, column)

        return pl.BlockSpec((8, width), at)

    return pl.pallas_call(
        core_backward_kernel,
        grid_spec=pltpu.PrefetchScalarGridSpec(
            num_scalar_prefetch=1,
            grid=(blocks,),
            in_specs=[
                wide(0),
                wide(0),
                wide(1),
                wide(0),
                wide(0),
                wide(0),
                wide(0),
                tail(0),
                tail(1),
                pl.BlockSpec((length, 128), lambda g, t: (back(g), 0)),
                whole(gates.shape),
                whole(small.shape),
            ],
            out_specs=[
                pl.BlockSpec((length, 2 * width), lambda g, t: (back(g) ^ t[0], 0)),
                whole(gates.shape),
                whole((8, width)),
            ],
            scratch_shapes=[
                pltpu.VMEM((length + 8, width), f32),
                pltpu.VMEM((length + 8, width), f32),
                pltpu.VMEM((length, 2 * width), bf16),
                pltpu.VMEM((length, width), f32),
                pltpu.VMEM((64, width), f32),
                pltpu.VMEM((8, width), f32),
                pltpu.VMEM((8, width), f32),
                pltpu.VMEM((24, width), f32),
            ],
        ),
        out_shape=[
            jax.ShapeDtypeStruct((total, 2 * width), bf16),
            jax.ShapeDtypeStruct(gates.shape, f32),
            jax.ShapeDtypeStruct((8, width), f32),
        ],
        compiler_params=pltpu.CompilerParams(vmem_limit_bytes=vmem_bytes),
        cost_estimate=light,
        name="core_backward",
    )(place, grad, pre, pre, mixed, rate, entry, state, state, pre, masks, gates, small)


def dot(left, right):
    return jnp.dot(left, right, preferred_element_type=f32)


def dot_rows(left, right):
    return lax.dot_general(left, right, (((0,), (0,)), ((), ())), preferred_element_type=f32)


def dot_back(left, right):
    return lax.dot_general(left, right, (((1,), (1,)), ((), ())), preferred_element_type=f32)


def fixed(shape):
    zeros = (0,) * len(shape)
    return pl.BlockSpec(shape, lambda *_: zeros)


def call(kernel, name, grid, in_specs, out_specs, out_shape, scratch=()):
    return pl.pallas_call(
        kernel,
        grid=grid,
        in_specs=in_specs,
        out_specs=out_specs,
        out_shape=out_shape,
        scratch_shapes=list(scratch),
        compiler_params=pltpu.CompilerParams(vmem_limit_bytes=vmem_bytes),
        cost_estimate=light,
        name=name,
    )


def spread(lefts, weights, first, count, transposed, name):
    rows = lefts[0][0].shape[0] // 4
    pieces = len(weights[0])
    product = dot_back if transposed else dot
    sizes = [w.shape[0 if transposed else 1] for w in weights[0]]
    widths = [w[0].shape[1 if transposed else 0] for w in weights]
    features = sum(sizes)
    terms = len(lefts)

    def kernel(*refs):
        left = [ref[...] for ref in refs[:terms]]
        flat = refs[terms : terms + terms * pieces]
        outs = refs[terms + terms * pieces : -1]
        total = refs[-1]
        at = 0
        for r in range(pieces):
            value = product(left[0], flat[r][...])
            for i in range(1, terms):
                value += product(left[i], flat[i * pieces + r][...])
            total[:, at : at + sizes[r]] = value.astype(bf16)
            at += sizes[r]
        for g in range(count):

            @pl.when(pl.program_id(0) == g)
            def _():
                outs[g][...] = total[...]

    def left_spec(width, column):
        return pl.BlockSpec((rows, width), lambda g: (first - g, column))

    return call(
        kernel,
        name,
        (count,),
        [left_spec(width, column) for width, (_, column) in zip(widths, lefts)]
        + [fixed(w.shape) for group in weights for w in group],
        [fixed((rows, features))] * count,
        [jax.ShapeDtypeStruct((rows, features), bf16)] * count,
        [pltpu.VMEM((rows, features), bf16)],
    )(*[left for left, _ in lefts], *[w for group in weights for w in group])


def collect(left, weights, transposed, name):
    total, features = left.shape
    rows = total // 4
    pieces = len(weights[0])
    product = dot_back if transposed else dot
    sizes = [w.shape[1 if transposed else 0] for w in weights[0]]
    widths = [w[0].shape[0 if transposed else 1] for w in weights]

    def kernel(*refs):
        out = refs[-1]
        column = 0
        for i, width in enumerate(widths):
            at = 0
            value = None
            for r in range(pieces):
                term = product(refs[0][:, at : at + sizes[r]], refs[1 + i * pieces + r][...])
                value = term if value is None else value + term
                at += sizes[r]
            out[:, column : column + width] = value
            column += width

    width = sum(widths)
    return call(
        kernel,
        name,
        (4,),
        [pl.BlockSpec((rows, features), lambda g: (g, 0))]
        + [fixed(w.shape) for group in weights for w in group],
        pl.BlockSpec((rows, width), lambda g: (g, 0)),
        jax.ShapeDtypeStruct((total, width), f32),
    )(left, *[w for group in weights for w in group])


def gated_forward(left, weights):
    total, features = left.shape
    rows = total // 4
    pieces = len(weights)
    size = features // pieces
    units = weights[0].shape[1] // 2
    step = units // 3

    def kernel(*refs):
        left_ref = refs[0]
        hidden, act_out, slope_out = refs[1 + pieces :]
        for c in range(3):
            at = slice(c * step, (c + 1) * step)
            after = slice(units + c * step, units + (c + 1) * step)
            gate = up = None
            for r in range(pieces):
                part = left_ref[:, r * size : (r + 1) * size]
                one = dot(part, refs[1 + r][:, at])
                two = dot(part, refs[1 + r][:, after])
                gate = one if gate is None else gate + one
                up = two if up is None else up + two
            act, slope = gelu_both(gate)
            hidden[:, at] = (act * up).astype(bf16)
            act_out[:, at] = act.astype(bf16)
            slope_out[:, at] = (up * slope).astype(bf16)

    block = pl.BlockSpec((rows, units), lambda g: (g, 0))
    return call(
        kernel,
        "gated_forward",
        (4,),
        [pl.BlockSpec((rows, features), lambda g: (g, 0))] + [fixed(w.shape) for w in weights],
        [block] * 3,
        [jax.ShapeDtypeStruct((total, units), bf16)] * 3,
    )(left, *weights)


def gated_backward(left, down_pieces, act, slope):
    total, features = left.shape
    rows = total // 4
    pieces = len(down_pieces)
    size = features // pieces
    units = down_pieces[0].shape[0]

    def kernel(*refs):
        left_ref = refs[0]
        act_ref, slope_ref, out = refs[1 + pieces :]
        grad = None
        for r in range(pieces):
            term = dot_back(left_ref[:, r * size : (r + 1) * size], refs[1 + r][...])
            grad = term if grad is None else grad + term
        out[:, :units] = (grad * slope_ref[...].astype(f32)).astype(bf16)
        out[:, units:] = (grad * act_ref[...].astype(f32)).astype(bf16)

    block = pl.BlockSpec((rows, units), lambda g: (g, 0))
    return call(
        kernel,
        "gated_backward",
        (4,),
        [pl.BlockSpec((rows, features), lambda g: (g, 0))]
        + [fixed(w.shape) for w in down_pieces]
        + [block] * 2,
        pl.BlockSpec((rows, 2 * units), lambda g: (g, 0)),
        jax.ShapeDtypeStruct((total, 2 * units), bf16),
    )(left, *down_pieces, act, slope)


def normalize(values, gain):
    total, features = values.shape

    def kernel(value_ref, gain_ref, out_ref):
        def step(c, carry):
            at = pl.ds(pl.multiple_of(c * 16, 16), 16)
            value = value_ref[at, :].astype(f32)
            scale = lax.rsqrt(jnp.mean(value * value, axis=1, keepdims=True) + epsilon)
            out_ref[at, :] = (value * scale * gain_ref[...]).astype(bf16)
            return carry

        lax.fori_loop(0, value_ref.shape[0] // 16, step, 0)

    block = pl.BlockSpec((total // 4, features), lambda g: (g, 0))
    return call(
        kernel,
        "normalize",
        (4,),
        [block, fixed((1, features))],
        block,
        jax.ShapeDtypeStruct((total, features), bf16),
    )(values, gain.reshape(1, features))


def move_columns(blocks, order, size):
    rows, features = blocks[0].shape
    groups = features // size

    def kernel(order_ref, *refs):
        out = refs[-1]
        for r in range(groups):
            start = pl.multiple_of(order_ref[r] * size, size)
            for j, ref in enumerate(refs[:-1]):
                out[j * rows : (j + 1) * rows, r * size : (r + 1) * size] = ref[
                    :, pl.ds(start, size)
                ]

    return pl.pallas_call(
        kernel,
        grid_spec=pltpu.PrefetchScalarGridSpec(
            num_scalar_prefetch=1,
            grid=(1,),
            in_specs=[fixed((rows, features))] * len(blocks),
            out_specs=fixed((rows * len(blocks), features)),
        ),
        out_shape=jax.ShapeDtypeStruct((rows * len(blocks), features), blocks[0].dtype),
        compiler_params=pltpu.CompilerParams(vmem_limit_bytes=vmem_bytes),
        cost_estimate=light,
        name="move_columns",
    )(order, *blocks)


class Ring:
    def __init__(self, count):
        self.count = count
        order = list(range(0, count, 2)) + list(range(1, count, 2))[::-1]
        self.order = order
        self.place_of = [order.index(index) for index in range(count)]
        ahead = [(order[(i + 1) % count], order[i]) for i in range(count)]
        behind = [(order[i], order[(i + 1) % count]) for i in range(count)]
        self.pairs = (ahead, behind)
        index = lax.axis_index("dp")
        half = (count + 1) // 2
        self.place = jnp.where(
            lax.rem(index, 2) == 0, lax.div(index, 2), count - 1 - lax.div(index, 2)
        ).astype(jnp.int32)
        spots = lax.rem(jnp.arange(count, dtype=jnp.int32) + self.place, count)
        self.block_of = jnp.where(spots < half, 2 * spots, 2 * (count - 1 - spots) + 1)
        self.step_of = self.steps_to(jnp.arange(count, dtype=jnp.int32))

    def steps_to(self, index):
        places = jnp.where(index % 2 == 0, index // 2, self.count - 1 - index // 2)
        return (places - self.place + self.count) % self.count

    def direct(self, blocks):
        total = blocks[0]
        for r in range(1, self.count):
            pairs = [
                (self.order[i], self.order[(i + r) % self.count]) for i in range(self.count)
            ]
            total = total + lax.ppermute(blocks[r], "dp", pairs)
        return total

    def columns_in(self, blocks, size):
        if size % 128 == 0:
            return move_columns(blocks, self.block_of, size)
        whole = jnp.concatenate(blocks, axis=0)
        ordered = [whole[:, i * size : (i + 1) * size] for i in self.order]
        return lax.dynamic_slice_in_dim(
            jnp.concatenate(ordered + ordered, axis=1),
            self.place * size,
            self.count * size,
            axis=1,
        )

    def columns_out(self, whole, size):
        if size % 128 == 0:
            return move_columns([whole], self.step_of, size)
        start = lax.rem(self.count - self.place, self.count) * size
        ordered = lax.dynamic_slice_in_dim(
            jnp.concatenate([whole, whole], axis=1), start, self.count * size, axis=1
        )
        return jnp.concatenate(
            [ordered[:, i * size : (i + 1) * size] for i in self.place_of], axis=1
        )


class Gather:
    work = 0.0

    def __init__(self, ring, own, far, axis):
        count = ring.count
        reach = count // 2 if far else (count - 1) // 2
        self.total = count
        self.hops = (reach, count - 1 - reach)
        self.left = count - 1
        self.blocks = [own] + [None] * (count - 1)
        self.axis = axis

    def receive(self, way, hop, value):
        self.blocks[hop + 1 if way == 0 else self.total - 1 - hop] = value
        self.left -= 1

    def operand(self, way, hop, gate):
        return self.blocks[hop if way == 0 else (self.total - hop) % self.total]

    def pieces(self):
        if self.blocks[0].shape[self.axis] % 128 == 0:
            return self.blocks
        return [jnp.concatenate(self.blocks, axis=self.axis)]


class Scatter:
    work = 2.0

    def __init__(self, ring, part, far):
        count = ring.count
        reach = count // 2 if far else (count - 1) // 2
        self.total = count
        self.hops = (count - 1 - reach, reach)
        self.left = count - 1
        self.part = part
        self.got = [None, None]

    def receive(self, way, hop, value):
        self.got[way] = value
        self.left -= 1

    def operand(self, way, hop, gate):
        distance = self.hops[way] - hop
        value = self.part(distance if way == 1 else self.total - distance)
        if hop:
            (got,) = gate(self.got[way])
            value = value + got.astype(f32)
        return value.astype(bf16)

    def result(self, gate):
        got = gate(*self.got)
        return self.part(0) + got[0].astype(f32) + got[1].astype(f32)


class Lanes:
    def __init__(self, ring, depth):
        self.ring = ring
        self.depth = depth
        self.queue = ([], [])
        self.flying = ([], [])
        self.link = [0.0, 0.0]
        self.now = 0.0
        self.marks = []

    def gate(self, *values):
        if not self.marks:
            return values
        return lax.optimization_barrier(tuple(values) + tuple(self.marks))[: len(values)]

    def mark(self, *values):
        self.marks = list(values)

    def add(self, *chains):
        for chain in chains:
            for way in range(2):
                if chain.hops[way]:
                    self.queue[way].append(chain)
        self.fill()

    def start(self, way, chain, hop):
        (operand,) = self.gate(chain.operand(way, hop, self.gate))
        self.mark(operand)
        self.now += chain.work + 1.5
        value = lax.ppermute(operand, "dp", self.ring.pairs[way])
        begin = max(self.now, self.link[way])
        self.link[way] = begin + operand.size / 22000.0
        self.flying[way].append((self.link[way] + 3.0, chain, hop, value))

    def fill(self):
        for way in range(2):
            while self.queue[way] and len(self.flying[way]) < self.depth:
                self.start(way, self.queue[way].pop(0), 0)

    def step(self, limit):
        heads = [(self.flying[way][0][0], way) for way in range(2) if self.flying[way]]
        if not heads or min(heads)[0] > limit:
            return False
        finish, way = min(heads)
        _, chain, hop, value = self.flying[way].pop(0)
        self.now = max(self.now, finish)
        chain.receive(way, hop, value)
        if hop + 1 < chain.hops[way]:
            self.start(way, chain, hop + 1)
        else:
            self.mark(value, *self.marks)
        self.fill()
        return True

    def catch_up(self, time=None):
        time = self.now if time is None else time
        while self.step(time):
            time = max(time, self.now)
        self.now = max(self.now, time)

    def until(self, *chains):
        while any(chain.left for chain in chains):
            assert self.step(float("inf"))

    def did(self, time, *values):
        self.mark(*values)
        self.now += time
        self.catch_up()


core_pairs = [(0, 1), (1, 0), (2, 3), (3, 2)]
chip_pairs = [(0, 2), (1, 3), (2, 0), (3, 1)]


def tensor_gather(own):
    across = lax.ppermute(own, "tensor", chip_pairs)
    sibling = lax.ppermute(own, "tensor", core_pairs)
    far = lax.ppermute(across, "tensor", core_pairs)
    return [own, sibling, across, far]


def tensor_scatter(blocks):
    own, sibling, across, far = blocks
    far = lax.ppermute(far, "tensor", core_pairs)
    sibling = lax.ppermute(sibling, "tensor", core_pairs)
    across = (across.astype(f32) + far.astype(f32)).astype(bf16)
    return own, sibling, across, lax.ppermute(across, "tensor", chip_pairs)


def summed(parts):
    own, sibling, _, across = parts
    return own.astype(f32) + sibling.astype(f32) + across.astype(f32)


def tensor_sum(value):
    value = value + lax.ppermute(value, "tensor", core_pairs)
    return value + lax.ppermute(value, "tensor", chip_pairs)


def row_scale(values):
    return lax.rsqrt(jnp.mean(values * values, axis=-1, keepdims=True) + epsilon)


def norm_backward(values, scale, gain, grad):
    weighted = grad * gain
    inner = jnp.mean(weighted * values, axis=-1, keepdims=True)
    row_grad = scale * weighted - values * (scale * scale * scale * inner)
    return row_grad, jnp.sum(grad * values * scale, axis=0)


def body(
    inputs,
    segment_ids,
    gain_mixer,
    branch_weight,
    input_weight,
    conv_weight,
    conv_bias,
    rate_weight,
    rate_bias,
    entry_weight,
    entry_bias,
    decay_param,
    output_weight,
    gain_mlp,
    gate_weight,
    up_weight,
    down_weight,
    cotangent,
    *,
    dp,
    tensor,
):
    ring = Ring(dp)
    lanes = Lanes(ring, 2)
    shard, width = branch_weight.shape
    features = inputs.shape[1]
    length = segment_ids.shape[0]
    gate_blocks, piece, block_width = rate_weight.shape
    taps = conv_weight.shape[0]
    units = gate_weight.shape[1]
    place = lax.axis_index("tensor").astype(jnp.int32).reshape(1)

    columns = jnp.stack(
        [conv_weight[k] for k in range(taps)] + [conv_bias, rate_bias, entry_bias, decay_param],
        axis=-1,
    )
    table = jnp.concatenate([rate_weight, entry_weight, columns], axis=-1)
    table = table.reshape(gate_blocks * piece, table.shape[-1])
    table_rows, table_columns = table.shape
    wide = -(-table_columns // 128) * 128
    high = -(-(table_rows + 2) // 16) * 16
    gains = jnp.pad(jnp.stack([gain_mixer, gain_mlp]), ((0, 0), (0, wide - shard)))
    table = jnp.concatenate(
        [jnp.pad(table, ((0, 0), (0, wide - table_columns))), gains], axis=0
    )
    table = jnp.pad(table, ((0, high - table_rows - 2), (0, 0)))

    masks = []
    for offset in range(1, taps):
        earlier = jnp.concatenate(
            [jnp.full((offset,), -1, segment_ids.dtype), segment_ids[: length - offset]]
        )
        masks.append((earlier == segment_ids).astype(f32))
    masks = jnp.stack([masks[0]] + masks, axis=1)
    masks = jnp.pad(masks, ((0, 0), (0, 128 - taps)))

    half = units // 2
    halves = (slice(0, half), slice(half, units))
    small_chain = Gather(ring, table, True, 0)
    pair_chain = Gather(ring, jnp.concatenate([branch_weight, input_weight], axis=1), False, 0)
    output_chain = Gather(ring, output_weight, True, 1)
    gated_chains = [
        Gather(
            ring,
            jnp.concatenate([gate_weight[:, at], up_weight[:, at]], axis=1),
            at.start == 0,
            0,
        )
        for at in halves
    ]
    down_chains = [Gather(ring, down_weight[at], at.start == 0, 1) for at in halves]
    input_blocks = tensor_gather(inputs)
    lanes.add(pair_chain, small_chain, output_chain, *gated_chains, *down_chains)
    lanes.catch_up(12.0)
    cotangent_blocks = tensor_gather(cotangent)

    lanes.until(small_chain)
    tables = jnp.concatenate(small_chain.blocks, axis=0)
    (tables,) = lanes.gate(tables)
    by_block = tables.reshape(dp, high, wide)
    gain_one = by_block[:, table_rows, :shard].reshape(features).astype(f32)
    gain_two = by_block[:, table_rows + 1, :shard].reshape(features).astype(f32)
    channel = jnp.arange(width)
    owner = (channel % block_width) // piece
    source = ring.steps_to(owner) * high + (channel // block_width) * piece + channel % piece
    mover = (source[:, None] == jnp.arange(dp * high)[None, :]).astype(bf16)
    whole_table = dot(mover, tables).astype(bf16)
    gate_column = jnp.arange(2 * width)
    picked = (gate_column // width) * block_width + gate_column % block_width
    spreader = (jnp.arange(wide)[:, None] == picked[None, :]).astype(bf16)
    same_block = (channel // block_width)[:, None] == (
        (gate_column % width) // block_width
    )[None, :]
    gates = jnp.where(same_block, dot(whole_table, spreader), 0.0).astype(bf16)
    picker = (jnp.arange(wide)[None, :] == (2 * block_width + jnp.arange(8))[:, None]).astype(bf16)
    small = dot_back(picker, whole_table)
    decay_full = small[7:8]
    small = jnp.concatenate([small[:7], -lru_scale * jax.nn.softplus(-decay_full)], axis=0)

    token_rows = ring.columns_in(input_blocks, shard)
    mixer_rows = normalize(token_rows, gain_one)
    rows = inputs.shape[0]
    lanes.did(25.0, mixer_rows, gates, small)
    lanes.until(pair_chain)
    (mixer_rows,) = lanes.gate(mixer_rows)
    pre = collect(mixer_rows, [pair_chain.pieces()], False, "mixer_in")
    lanes.did(11.0, pre)
    (pre,) = lanes.gate(pre)
    mixer_low, mixed, rate, entry, state = core_forward(place, pre, masks, gates, small, tensor)
    lanes.did(21.0, mixer_low)
    lanes.until(output_chain)
    output_pieces = output_chain.pieces()
    (mixer_low,) = lanes.gate(mixer_low)
    blocks = spread([(mixer_low, 0)], [output_pieces], 3, 4, False, "mixer_out")[::-1]
    parts = tensor_scatter(blocks)
    lanes.did(11.0, parts[2])
    arrival = lanes.now + 26.0
    (moved,) = lanes.gate(cotangent_blocks[0])
    cotangent_rows = ring.columns_in([moved] + cotangent_blocks[1:], shard)
    lanes.did(5.0, cotangent_rows)
    lanes.catch_up(arrival)
    parts = lanes.gate(*parts)
    tokens = token_rows[:rows].astype(f32)
    middle = tokens + summed(parts)
    scale_two = row_scale(middle)
    mlp_blocks = tensor_gather((middle * scale_two * gain_two).astype(bf16))
    lanes.did(5.0, mlp_blocks[0])
    lanes.catch_up(lanes.now + 28.0)
    mlp_blocks = lanes.gate(*mlp_blocks)
    mlp_rows = jnp.concatenate(mlp_blocks, axis=0)
    lanes.did(5.0, mlp_rows)

    def columns_of(array, r):
        return lax.slice_in_dim(array, r * shard, (r + 1) * shard, axis=1)

    hidden, acts, slopes, down_scatters = [], [], [], []
    for h in range(2):
        lanes.until(gated_chains[h])
        (gated,) = lanes.gate(mlp_rows)
        one, two, three = gated_forward(gated, gated_chains[h].pieces())
        hidden.append(one)
        acts.append(two)
        slopes.append(three)
        down_scatters.append(
            Scatter(
                ring,
                lambda r, one=one: dot_rows(one, columns_of(cotangent_rows, r)),
                h == 1,
            )
        )
        lanes.did(12.0, one)
    lanes.add(*down_scatters)
    gated_lows, gated_scatters = [], []
    for h in range(2):
        lanes.until(down_chains[h])
        (gated,) = lanes.gate(cotangent_rows)
        low = gated_backward(gated, down_chains[h].pieces(), acts[h], slopes[h])
        gated_lows.append(low)
        gated_scatters.append(
            Scatter(
                ring,
                lambda r, low=low: dot_rows(columns_of(mlp_rows, r), low),
                h == 0,
            )
        )
        lanes.did(8.5, low)
    lanes.add(*gated_scatters)
    weights = [chain.pieces() for chain in gated_chains]

    def lefts():
        return [(low, 0) for low in lanes.gate(*gated_lows)]

    far, across = spread(lefts(), weights, 3, 2, True, "mlp_in_grad")
    lanes.did(14.0, far)
    sibling, own = spread(lefts(), weights, 1, 2, True, "mlp_in_grad")
    parts = tensor_scatter([own, sibling, across, far])
    lanes.did(14.0, own)
    lanes.catch_up(lanes.now + 28.0)
    parts = lanes.gate(*parts)
    middle_norm_grad, gain_two_part = norm_backward(middle, scale_two, gain_two, summed(parts))
    middle_grad = (
        lax.slice_in_dim(cotangent_rows, 0, rows, axis=0).astype(f32) + middle_norm_grad
    )
    residual_blocks = tensor_gather(middle_grad.astype(bf16))
    lanes.did(5.0, residual_blocks[0])
    lanes.catch_up(lanes.now + 26.0)
    residual_blocks = lanes.gate(*residual_blocks)
    residual_rows = jnp.concatenate(residual_blocks, axis=0)
    lanes.did(5.0, residual_rows)

    (residual_rows,) = lanes.gate(residual_rows)
    mixer_grad = collect(residual_rows, [output_pieces], True, "mixer_grad")
    lanes.did(8.0, mixer_grad)
    (mixer_grad,) = lanes.gate(mixer_grad)
    pair_low, gate_grads, small_grads = core_backward(
        place, mixer_grad, pre, mixed, rate, entry, state, masks, gates, small, tensor
    )
    lanes.did(28.0, pair_low)
    output_scatter = Scatter(
        ring, lambda r: dot_rows(mixer_low, columns_of(residual_rows, r)), True
    )
    whole_low = pair_low
    pair_scatter = Scatter(ring, lambda r: dot_rows(columns_of(mixer_rows, r), whole_low), False)
    lanes.add(output_scatter, pair_scatter)
    (pair_low,) = lanes.gate(pair_low)
    blocks = spread([(pair_low, 0)], [pair_chain.pieces()], 3, 4, True, "mixer_in_grad")[::-1]
    parts = tensor_scatter(blocks)
    lanes.did(14.0, parts[2])
    arrival = lanes.now + 26.0

    (gate_grads,) = lanes.gate(gate_grads)
    decay_grad = lru_scale * small_grads[7:8] * jax.nn.sigmoid(-decay_full)
    small_grads = jnp.concatenate([small_grads[:7], decay_grad], axis=0).astype(bf16)
    grad_table = dot_back(
        jnp.where(same_block, gate_grads, 0.0).astype(bf16), spreader
    ) + dot_rows(small_grads, picker)
    grad_tables = dot_rows(mover, grad_table.astype(bf16)).astype(bf16)
    table_scatter = Scatter(
        ring,
        lambda r: lax.slice_in_dim(grad_tables, r * high, (r + 1) * high, axis=0).astype(f32),
        True,
    )
    lanes.did(12.0, grad_tables)
    lanes.add(table_scatter)
    lanes.catch_up(arrival)
    parts = lanes.gate(*parts)
    tokens_norm_grad, gain_one_part = norm_backward(tokens, row_scale(tokens), gain_one, summed(parts))
    inputs_grad = ring.columns_out((middle_grad + tokens_norm_grad).astype(bf16), shard)
    gain_parts = tensor_sum(jnp.stack([gain_one_part, gain_two_part]))
    gain_sums = ring.direct([columns_of(gain_parts, r) for r in range(dp)])
    lanes.did(8.0, inputs_grad)

    late = lanes.gate(*hidden)
    blocks = spread(
        [(low, 0) for low in late],
        [chain.pieces() for chain in down_chains],
        3,
        4,
        False,
        "mlp_out",
    )[::-1]
    parts = tensor_scatter(blocks)
    lanes.did(14.0, parts[2])
    lanes.catch_up(lanes.now + 26.0)
    parts = lanes.gate(*parts)
    layer_out = ring.columns_out((middle + summed(parts)).astype(bf16), shard)
    lanes.did(5.0, layer_out)
    lanes.until(
        *down_scatters, *gated_scatters, output_scatter, pair_scatter, table_scatter
    )

    free = lambda *values: values
    table_grad = table_scatter.result(free)[:table_rows].reshape(gate_blocks, piece, wide)
    rate_wgrad = table_grad[:, :, :block_width]
    entry_wgrad = table_grad[:, :, block_width : 2 * block_width]
    singles = [table_grad[:, :, 2 * block_width + k] for k in range(taps + 4)]
    pair_wgrad = pair_scatter.result(free)
    gated_wgrads = [scatter.result(free) for scatter in gated_scatters]
    return (
        layer_out,
        inputs_grad,
        gain_sums[0],
        pair_wgrad[:, :width],
        pair_wgrad[:, width:],
        jnp.stack(singles[:taps]),
        singles[taps],
        rate_wgrad,
        singles[taps + 1],
        entry_wgrad,
        singles[taps + 2],
        singles[taps + 3],
        output_scatter.result(free),
        gain_sums[1],
        jnp.concatenate([wgrad[:, :half] for wgrad in gated_wgrads], axis=1),
        jnp.concatenate([wgrad[:, half:] for wgrad in gated_wgrads], axis=1),
        jnp.concatenate([scatter.result(free) for scatter in down_scatters], axis=0),
    )


def solution(mesh):
    return jax.shard_map(
        functools.partial(body, dp=mesh.shape["dp"], tensor=mesh.shape["tensor"]),
        mesh=mesh,
        in_specs=(
            P(("dp", "tensor"), None),
            P("dp"),
            P("dp"),
            P("dp", "tensor"),
            P("dp", "tensor"),
            P(None, "tensor", "dp"),
            P("tensor", "dp"),
            P("tensor", "dp", None),
            P("tensor", "dp"),
            P("tensor", "dp", None),
            P("tensor", "dp"),
            P("tensor", "dp"),
            P("tensor", "dp"),
            P("dp"),
            P("dp", "tensor"),
            P("dp", "tensor"),
            P("tensor", "dp"),
            P(("dp", "tensor"), None),
        ),
        out_specs=(
            P(("dp", "tensor"), None),
            P(("dp", "tensor"), None),
            P("dp"),
            P("dp", "tensor"),
            P("dp", "tensor"),
            P(None, "tensor", "dp"),
            P("tensor", "dp"),
            P("tensor", "dp", None),
            P("tensor", "dp"),
            P("tensor", "dp", None),
            P("tensor", "dp"),
            P("tensor", "dp"),
            P("tensor", "dp"),
            P("dp"),
            P("dp", "tensor"),
            P("dp", "tensor"),
            P("tensor", "dp"),
        ),
        check_vma=False,
    )
```

```python
import functools

import jax
import jax.numpy as jnp
from jax import lax
from jax.experimental import pallas as pl
from jax.experimental.pallas import tpu as pltpu
from jax.sharding import PartitionSpec as P

epsilon = 1e-06
lru_scale = 8.0
root = 0.7978845608028654
cubic = 0.044715
f32 = jnp.float32
bf16 = jnp.bfloat16
vmem_bytes = 56 * 1024 * 1024
light = pl.CostEstimate(flops=6_000_000_000, bytes_accessed=30_000_000, transcendentals=0)


def gelu_both(value):
    square = value * value
    th = jnp.tanh(root * value * (1.0 + cubic * square))
    half = 0.5 * (1.0 + th)
    slope = half + 0.5 * value * (1.0 - th * th) * (root * (1.0 + 3.0 * cubic * square))
    return value * half, slope


def gelu(value):
    return value * (0.5 * (1.0 + jnp.tanh(root * value * (1.0 + cubic * value * value))))


def one_minus_exp(x, exp_x):
    series = 1.0 + x * (1.0 / 7.0)
    for order in (6.0, 5.0, 4.0, 3.0, 2.0):
        series = 1.0 + x * (1.0 / order) * series
    return jnp.where(x > -0.5, -x * series, 1.0 - exp_x)


def decay_terms(rate, slope, keep):
    log_decay = slope * rate
    expo = jnp.exp(log_decay)
    square = expo * expo
    factor = jnp.where(keep > 0.0, jnp.sqrt(one_minus_exp(2.0 * log_decay, square)), 1.0)
    return expo * keep, square, factor


def row_index(width):
    return lax.broadcasted_iota(jnp.int32, (8, width), 0)


def down_by(current, before, offset, rows):
    if offset == 0:
        return current
    return jnp.where(
        rows < offset, pltpu.roll(before, offset, 0), pltpu.roll(current, offset, 0)
    )


def up_by(current, after, offset, rows):
    if offset == 0:
        return current
    return jnp.where(
        rows < 8 - offset,
        pltpu.roll(current, 8 - offset, 0),
        pltpu.roll(after, 8 - offset, 0),
    )


def core_forward_kernel(
    place, branch, entry_pre, masks, gates, small, out, mixed_out, rate_out, entry_out, state_out,
    mixed_low, pre, last_entry, last_state,
):
    length, width = entry_pre.shape
    rows = row_index(width)

    @pl.when(pl.program_id(0) == 0)
    def _():
        last_entry[...] = jnp.zeros_like(last_entry)
        last_state[...] = jnp.zeros_like(last_state)

    taps = [small[k : k + 1, :] for k in range(4)]
    conv_bias = small[4:5, :]

    def convolve(step, before):
        parts = []
        for half in range(2):
            at = pl.ds(pl.multiple_of(step * 16 + half * 8, 8), 8)
            here = entry_pre[at, :]
            mask = masks[at, :]
            mixed = here * taps[0] + conv_bias
            for k in range(1, 4):
                mixed += down_by(here, before, k, rows) * mask[:, k : k + 1] * taps[k]
            mixed_out[at, :] = mixed
            parts.append(mixed)
            before = here
        mixed_low[pl.ds(pl.multiple_of(step * 16, 16), 16), :] = jnp.concatenate(
            parts, axis=0
        ).astype(bf16)
        return before

    last_entry[...] = lax.fori_loop(0, length // 16, convolve, last_entry[...])
    pre[...] = jnp.dot(mixed_low[...], gates[...], preferred_element_type=f32)
    rate_bias = small[5:6, :]
    entry_bias = small[6:7, :]
    slope = small[7:8, :]

    def scan(step, carry):
        parts = []
        for half in range(2):
            at = pl.ds(pl.multiple_of(step * 16 + half * 8, 8), 8)
            keep = masks[at, :][:, 0:1]
            rate = jax.nn.sigmoid(pre[at, :width] + rate_bias)
            entry = jax.nn.sigmoid(pre[at, width:] + entry_bias)
            decay, _, factor = decay_terms(rate, slope, keep)
            drive = factor * entry * mixed_out[at, :]
            for shift in (1, 2, 4):
                inside = rows >= shift
                drive += decay * jnp.where(inside, pltpu.roll(drive, shift, 0), 0.0)
                decay = decay * jnp.where(inside, pltpu.roll(decay, shift, 0), 1.0)
            state = drive + decay * carry
            carry = jnp.broadcast_to(state[7:8, :], state.shape)
            rate_out[at, :] = rate
            entry_out[at, :] = entry
            state_out[at, :] = state
            parts.append(gelu(branch[at, :]) * state)
        out[pl.ds(pl.multiple_of(step * 16, 16), 16), :] = jnp.concatenate(parts, axis=0).astype(
            bf16
        )
        return carry

    last_state[...] = lax.fori_loop(0, length // 16, scan, last_state[...])


def core_backward_kernel(
    place, grad, branch, entry_pre, mixed_in, rate_in, entry_in, state_in, state_tail, entry_tail,
    masks, gates, small, low, gate_grads, small_grads,
    state_long, entry_long, gate_low, mixed_grad, sums, next_decay, next_carried, next_mixed,
):
    length, width = entry_pre.shape
    rows = row_index(width)

    @pl.when(pl.program_id(0) == 0)
    def _():
        next_decay[...] = jnp.zeros_like(next_decay)
        next_carried[...] = jnp.zeros_like(next_carried)
        next_mixed[...] = jnp.zeros_like(next_mixed)
        sums[...] = jnp.zeros_like(sums)
        gate_grads[...] = jnp.zeros_like(gate_grads)

    state_long[0:8, :] = state_tail[...]
    state_long[8:, :] = state_in[...]
    entry_long[0:8, :] = entry_tail[...]
    entry_long[8:, :] = entry_pre[...]
    slope = small[7:8, :]

    def reverse(step, carry):
        after_decay, carried_after = carry
        step = length // 16 - 1 - step
        branch_parts, rate_parts, entry_parts = [], [], []
        for half in (1, 0):
            start = pl.multiple_of(step * 16 + half * 8, 8)
            at = pl.ds(start, 8)
            keep = masks[at, :][:, 0:1]
            rate = rate_in[at, :]
            entry = entry_in[at, :]
            mixed = mixed_in[at, :]
            decay, square, factor = decay_terms(rate, slope, keep)
            up = grad[at, :]
            act, act_slope = gelu_both(branch[at, :])
            state = state_in[at, :]
            branch_parts.append(up * state * act_slope)
            value = up * act
            ahead = up_by(decay, after_decay, 1, rows)
            after_decay = decay
            for shift in (1, 2, 4):
                inside = rows < 8 - shift
                value += ahead * jnp.where(inside, pltpu.roll(value, 8 - shift, 0), 0.0)
                ahead = ahead * jnp.where(inside, pltpu.roll(ahead, 8 - shift, 0), 1.0)
            carried = value + ahead * carried_after
            carried_after = jnp.broadcast_to(carried[0:1, :], carried.shape)
            earlier = down_by(state, state_long[at, :], 1, rows)
            driven = carried * entry
            log_grad = keep * (carried * earlier * decay - driven * mixed * square / factor)
            scaled = log_grad * rate
            rate_pre_grad = slope * scaled * (1.0 - rate)
            entry_pre_grad = driven * factor * mixed * (1.0 - entry)
            mixed_grad[at, :] = driven * factor
            sums[40:48, :] += rate_pre_grad
            sums[48:56, :] += entry_pre_grad
            sums[56:64, :] += scaled
            rate_parts.append(rate_pre_grad)
            entry_parts.append(entry_pre_grad)
        both = pl.ds(pl.multiple_of(step * 16, 16), 16)
        low[both, :width] = jnp.concatenate(branch_parts[::-1], axis=0).astype(bf16)
        gate_low[both, :width] = jnp.concatenate(rate_parts[::-1], axis=0).astype(bf16)
        gate_low[both, width:] = jnp.concatenate(entry_parts[::-1], axis=0).astype(bf16)
        return after_decay, carried_after

    after_decay, carried_after = lax.fori_loop(
        0, length // 16, reverse, (next_decay[...], next_carried[...])
    )
    next_decay[...] = after_decay
    next_carried[...] = carried_after
    mixed_grad[...] += lax.dot_general(
        gate_low[...], gates[...], (((1,), (1,)), ((), ())), preferred_element_type=f32
    )
    gate_grads[...] += lax.dot_general(
        mixed_in[...].astype(bf16),
        gate_low[...],
        (((0,), (0,)), ((), ())),
        preferred_element_type=f32,
    )
    taps = [small[k : k + 1, :] for k in range(4)]

    def convolve(step, after):
        step = length // 16 - 1 - step
        parts = []
        for half in (1, 0):
            start = pl.multiple_of(step * 16 + half * 8, 8)
            at = pl.ds(start, 8)
            mask = masks[at, :]
            here = mixed_grad[at, :]
            value = entry_pre[at, :]
            before = entry_long[at, :]
            sums[32:40, :] += here
            sums[0:8, :] += here * value
            total = here * taps[0]
            masked = [here * mask[:, k : k + 1] for k in range(1, 4)]
            for k in range(1, 4):
                sums[8 * k : 8 * k + 8, :] += masked[k - 1] * down_by(value, before, k, rows)
                total += up_by(masked[k - 1], after[k - 1], k, rows) * taps[k]
            after = masked
            parts.append(total)
        low[pl.ds(pl.multiple_of(step * 16, 16), 16), width:] = jnp.concatenate(
            parts[::-1], axis=0
        ).astype(bf16)
        return after

    after = lax.fori_loop(
        0,
        length // 16,
        convolve,
        [next_mixed[8 * k : 8 * k + 8, :] for k in range(3)],
    )
    for k in range(3):
        next_mixed[8 * k : 8 * k + 8, :] = after[k]

    @pl.when(pl.program_id(0) == pl.num_programs(0) - 1)
    def _():
        for k in range(8):
            small_grads[k : k + 1, :] = jnp.sum(sums[8 * k : 8 * k + 8, :], axis=0, keepdims=True)


def core_forward(place, pre, masks, gates, small, blocks):
    total, width = pre.shape[0], pre.shape[1] // 2
    length = total // blocks
    wide = lambda column: pl.BlockSpec((length, width), lambda b, t: (b ^ t[0], column))
    whole = lambda shape: pl.BlockSpec(shape, lambda b, t: (0, 0))
    kept = jax.ShapeDtypeStruct((total, width), f32)
    return pl.pallas_call(
        core_forward_kernel,
        grid_spec=pltpu.PrefetchScalarGridSpec(
            num_scalar_prefetch=1,
            grid=(blocks,),
            in_specs=[
                wide(0),
                wide(1),
                pl.BlockSpec((length, 128), lambda b, t: (b, 0)),
                whole(gates.shape),
                whole(small.shape),
            ],
            out_specs=[wide(0)] * 5,
            scratch_shapes=[
                pltpu.VMEM((length, width), bf16),
                pltpu.VMEM((length, 2 * width), f32),
                pltpu.VMEM((8, width), f32),
                pltpu.VMEM((8, width), f32),
            ],
        ),
        out_shape=[jax.ShapeDtypeStruct((total, width), bf16)] + [kept] * 4,
        compiler_params=pltpu.CompilerParams(vmem_limit_bytes=vmem_bytes),
        cost_estimate=light,
        name="core_forward",
    )(place, pre, pre, masks, gates, small)


def core_backward(place, grad, pre, mixed, rate, entry, state, masks, gates, small, blocks):
    total, width = grad.shape
    length = total // blocks
    back = lambda g: blocks - 1 - g
    wide = lambda column: pl.BlockSpec((length, width), lambda g, t: (back(g) ^ t[0], column))
    whole = lambda shape: pl.BlockSpec(shape, lambda g, t: (0, 0))

    def tail(column):
        def at(g, t):
            block = jnp.maximum(back(g) - 1, 0) ^ t[0]
            return (block * (length // 8) + length // 8 - 1, column)

        return pl.BlockSpec((8, width), at)

    return pl.pallas_call(
        core_backward_kernel,
        grid_spec=pltpu.PrefetchScalarGridSpec(
            num_scalar_prefetch=1,
            grid=(blocks,),
            in_specs=[
                wide(0),
                wide(0),
                wide(1),
                wide(0),
                wide(0),
                wide(0),
                wide(0),
                tail(0),
                tail(1),
                pl.BlockSpec((length, 128), lambda g, t: (back(g), 0)),
                whole(gates.shape),
                whole(small.shape),
            ],
            out_specs=[
                pl.BlockSpec((length, 2 * width), lambda g, t: (back(g) ^ t[0], 0)),
                whole(gates.shape),
                whole((8, width)),
            ],
            scratch_shapes=[
                pltpu.VMEM((length + 8, width), f32),
                pltpu.VMEM((length + 8, width), f32),
                pltpu.VMEM((length, 2 * width), bf16),
                pltpu.VMEM((length, width), f32),
                pltpu.VMEM((64, width), f32),
                pltpu.VMEM((8, width), f32),
                pltpu.VMEM((8, width), f32),
                pltpu.VMEM((24, width), f32),
            ],
        ),
        out_shape=[
            jax.ShapeDtypeStruct((total, 2 * width), bf16),
            jax.ShapeDtypeStruct(gates.shape, f32),
            jax.ShapeDtypeStruct((8, width), f32),
        ],
        compiler_params=pltpu.CompilerParams(vmem_limit_bytes=vmem_bytes),
        cost_estimate=light,
        name="core_backward",
    )(place, grad, pre, pre, mixed, rate, entry, state, state, pre, masks, gates, small)


def dot(left, right):
    return jnp.dot(left, right, preferred_element_type=f32)


def dot_rows(left, right):
    return lax.dot_general(left, right, (((0,), (0,)), ((), ())), preferred_element_type=f32)


def dot_back(left, right):
    return lax.dot_general(left, right, (((1,), (1,)), ((), ())), preferred_element_type=f32)


def fixed(shape):
    zeros = (0,) * len(shape)
    return pl.BlockSpec(shape, lambda *_: zeros)


def call(kernel, name, grid, in_specs, out_specs, out_shape, scratch=()):
    return pl.pallas_call(
        kernel,
        grid=grid,
        in_specs=in_specs,
        out_specs=out_specs,
        out_shape=out_shape,
        scratch_shapes=list(scratch),
        compiler_params=pltpu.CompilerParams(vmem_limit_bytes=vmem_bytes),
        cost_estimate=light,
        name=name,
    )


def spread(lefts, weights, place, blocks, transposed, name):
    total = lefts[0][0].shape[0]
    rows = total // 4
    pieces = len(weights[0])
    product = dot_back if transposed else dot
    sizes = [w.shape[0 if transposed else 1] for w in weights[0]]
    widths = [width for _, _, width in lefts]
    features = sum(sizes)
    terms = len(lefts)
    count = len(blocks) if blocks else 4

    def kernel(place_ref, *refs):
        left = [ref[...] for ref in refs[:terms]]
        flat = refs[terms : terms + terms * pieces]
        outs = refs[terms + terms * pieces :]
        result = outs[-1]
        at = 0
        for r in range(pieces):
            value = None
            for i in range(terms):
                weight = flat[i * pieces + r]
                if transposed:
                    weight = weight[:, : widths[i]]
                else:
                    weight = weight[...]
                term = product(left[i], weight)
                value = term if value is None else value + term
            result[:, at : at + sizes[r]] = value.astype(bf16)
            at += sizes[r]
        if blocks:
            for g in range(count):

                @pl.when(pl.program_id(0) == g)
                def _():
                    outs[g][...] = result[...]

    def left_spec(column, width):
        if blocks:
            first = blocks[0]
            return pl.BlockSpec((rows, width), lambda g, t: ((first - g) ^ t[0], column))
        return pl.BlockSpec((rows, width), lambda g, t: (g, column))

    if blocks:
        out_specs = [fixed((rows, features))] * count
        out_shape = [jax.ShapeDtypeStruct((rows, features), bf16)] * count
        scratch = [pltpu.VMEM((rows, features), bf16)]
    else:
        out_specs = pl.BlockSpec((rows, features), lambda g, t: (g, 0))
        out_shape = jax.ShapeDtypeStruct((total, features), bf16)
        scratch = []
    return pl.pallas_call(
        kernel,
        grid_spec=pltpu.PrefetchScalarGridSpec(
            num_scalar_prefetch=1,
            grid=(count,),
            in_specs=[left_spec(column, width) for _, column, width in lefts]
            + [fixed(w.shape) for group in weights for w in group],
            out_specs=out_specs,
            scratch_shapes=scratch,
        ),
        out_shape=out_shape,
        compiler_params=pltpu.CompilerParams(vmem_limit_bytes=vmem_bytes),
        cost_estimate=light,
        name=name,
    )(place, *[left for left, _, _ in lefts], *[w for group in weights for w in group])


def collect(left, weights, width, transposed, name):
    total, features = left.shape
    rows = total // 4
    count = len(weights)
    pieces = len(weights[0])
    product = dot_back if transposed else dot
    sizes = [w.shape[1 if transposed else 0] for w in weights[0]]

    def kernel(*refs):
        out = refs[-1]
        for i in range(count):
            at = 0
            value = None
            for r in range(pieces):
                ref = refs[1 + i * pieces + r]
                weight = ref[...] if transposed else ref[:, :width]
                term = product(refs[0][:, at : at + sizes[r]], weight)
                value = term if value is None else value + term
                at += sizes[r]
            out[:, i * width : (i + 1) * width] = value

    return call(
        kernel,
        name,
        (4,),
        [pl.BlockSpec((rows, features), lambda g: (g, 0))]
        + [fixed(w.shape) for group in weights for w in group],
        pl.BlockSpec((rows, count * width), lambda g: (g, 0)),
        jax.ShapeDtypeStruct((total, count * width), f32),
    )(left, *[w for group in weights for w in group])


def gated_forward(left, weights):
    total, features = left.shape
    rows = total // 4
    pieces = len(weights)
    size = features // pieces
    units = weights[0].shape[1] // 2
    step = units // 3

    def kernel(*refs):
        left_ref = refs[0]
        hidden, act_out, slope_out = refs[1 + pieces :]
        for c in range(3):
            at = slice(c * step, (c + 1) * step)
            after = slice(units + c * step, units + (c + 1) * step)
            gate = up = None
            for r in range(pieces):
                part = left_ref[:, r * size : (r + 1) * size]
                one = dot(part, refs[1 + r][:, at])
                two = dot(part, refs[1 + r][:, after])
                gate = one if gate is None else gate + one
                up = two if up is None else up + two
            act, slope = gelu_both(gate)
            hidden[:, at] = (act * up).astype(bf16)
            act_out[:, at] = act.astype(bf16)
            slope_out[:, at] = (up * slope).astype(bf16)

    block = pl.BlockSpec((rows, units), lambda g: (g, 0))
    return call(
        kernel,
        "gated_forward",
        (4,),
        [pl.BlockSpec((rows, features), lambda g: (g, 0))] + [fixed(w.shape) for w in weights],
        [block] * 3,
        [jax.ShapeDtypeStruct((total, units), bf16)] * 3,
    )(left, *weights)


def gated_backward(left, down_pieces, act, slope):
    total, features = left.shape
    rows = total // 4
    pieces = len(down_pieces)
    size = features // pieces
    units = down_pieces[0].shape[0]

    def kernel(*refs):
        left_ref = refs[0]
        act_ref, slope_ref, out = refs[1 + pieces :]
        grad = None
        for r in range(pieces):
            term = dot_back(left_ref[:, r * size : (r + 1) * size], refs[1 + r][...])
            grad = term if grad is None else grad + term
        out[:, :units] = (grad * slope_ref[...].astype(f32)).astype(bf16)
        out[:, units:] = (grad * act_ref[...].astype(f32)).astype(bf16)

    block = pl.BlockSpec((rows, units), lambda g: (g, 0))
    return call(
        kernel,
        "gated_backward",
        (4,),
        [pl.BlockSpec((rows, features), lambda g: (g, 0))]
        + [fixed(w.shape) for w in down_pieces]
        + [block] * 2,
        pl.BlockSpec((rows, 2 * units), lambda g: (g, 0)),
        jax.ShapeDtypeStruct((total, 2 * units), bf16),
    )(left, *down_pieces, act, slope)


def weight_grads(lefts, right, pieces, by_left, name, extras=()):
    total = right.shape[0]
    terms = len(lefts)
    operands = list(lefts) + [right]
    if (lefts[0] if by_left else right).shape[1] // pieces % 128:
        return weight_grads_plain(lefts, right, pieces, by_left, extras)
    if by_left:
        (left,) = lefts
        size = left.shape[1] // pieces
        parts = len(extras) or 1
        width = right.shape[1] // parts
        more = extras[0].shape[1] if extras else 0
        shapes = [(size, width + more)] * parts
        in_specs = [pl.BlockSpec((total, size), lambda g: (0, g)), fixed(right.shape)]
        operands += extras
        in_specs += [pl.BlockSpec((size, more), lambda g: (g, 0)) for _ in extras]
    else:
        size = right.shape[1] // pieces
        parts = terms
        shapes = [(left.shape[1], size) for left in lefts]
        in_specs = [fixed(left.shape) for left in lefts] + [
            pl.BlockSpec((total, size), lambda g: (0, g))
        ]

    def kernel(*refs):
        outs = refs[len(operands) : len(operands) + parts * pieces]
        results = refs[len(operands) + parts * pieces :]
        for i in range(parts):
            if by_left:
                value = dot_rows(refs[0][...], refs[1][:, i * width : (i + 1) * width])
                results[i][:, :width] = value.astype(bf16)
                if extras:
                    results[i][:, width:] = refs[2 + i][...]
            else:
                results[i][...] = dot_rows(refs[i][...], refs[terms][...]).astype(bf16)
        for r in range(pieces):

            @pl.when(pl.program_id(0) == r)
            def _():
                for i in range(parts):
                    outs[i * pieces + r][...] = results[i][...]

    out = call(
        kernel,
        name,
        (pieces,),
        in_specs,
        [fixed(shape) for shape in shapes for _ in range(pieces)],
        [jax.ShapeDtypeStruct(shape, bf16) for shape in shapes for _ in range(pieces)],
        [pltpu.VMEM(shape, bf16) for shape in shapes],
    )(*operands)
    return [out[i * pieces : (i + 1) * pieces] for i in range(parts)]


def weight_grads_plain(lefts, right, pieces, by_left, extras):
    if not by_left:
        wholes = [dot_rows(left, right).astype(bf16) for left in lefts]
        return [jnp.split(whole, pieces, axis=1) for whole in wholes]
    wholes = jnp.split(dot_rows(lefts[0], right).astype(bf16), len(extras) or 1, axis=1)
    if extras:
        wholes = [jnp.concatenate(pair, axis=1) for pair in zip(wholes, extras)]
    return [jnp.split(whole, pieces, axis=0) for whole in wholes]


def one_hot(rows, columns, hit):
    row = lax.broadcasted_iota(jnp.int32, (rows, columns), 0)
    column = lax.broadcasted_iota(jnp.int32, (rows, columns), 1)
    return jnp.where(hit(row, column), 1.0, 0.0).astype(bf16)


def table_movers(width, shard, piece, block_width):
    table_rows = width // block_width * piece
    return [
        one_hot(
            width,
            shard,
            lambda c, row, k=k: row == k * table_rows + c // block_width * piece + c % piece,
        )
        for k in range(3)
    ]


def unpack_tables(blocks, order, width, piece, block_width):
    count = len(blocks)
    shard = blocks[0].shape[0]
    table_rows = width // block_width * piece

    def kernel(order_ref, *refs):
        flat = refs[:count]
        gates, small, gains, kept = refs[count:]
        owner = lax.broadcasted_iota(jnp.int32, (width, 256), 0) % block_width // piece
        movers = table_movers(width, shard, piece, block_width)
        picks = one_hot(8, shard, lambda row, column: column == 3 * table_rows + row)
        for r in range(count):
            table = flat[r][...]
            mine = owner == order_ref[r]
            for k in range(3):
                value = dot(movers[k], table)
                if r == 0:
                    kept[k] = jnp.where(mine, value, 0.0)
                else:
                    kept[k] = jnp.where(mine, value, kept[k])
            rows = dot(picks, table)
            gains[:, r * shard : (r + 1) * shard] = rows[:, :shard]
        spreader = one_hot(256, width, lambda row, column: row == column % block_width)
        same = lax.broadcasted_iota(jnp.int32, (width, width), 0) // block_width == (
            lax.broadcasted_iota(jnp.int32, (width, width), 1) // block_width
        )
        for k in range(2):
            value = dot(kept[k].astype(bf16), spreader)
            gates[:, k * width : (k + 1) * width] = jnp.where(same, value, 0.0).astype(bf16)
        picker = one_hot(8, 256, lambda row, column: row == column)
        small[...] = dot_back(picker, kept[2].astype(bf16))

    return pl.pallas_call(
        kernel,
        grid_spec=pltpu.PrefetchScalarGridSpec(
            num_scalar_prefetch=1,
            grid=(1,),
            in_specs=[fixed((shard, 256))] * count,
            out_specs=[
                fixed((width, 2 * width)),
                fixed((8, width)),
                fixed((8, count * shard)),
            ],
            scratch_shapes=[pltpu.VMEM((3, width, 256), f32)],
        ),
        out_shape=[
            jax.ShapeDtypeStruct((width, 2 * width), bf16),
            jax.ShapeDtypeStruct((8, width), f32),
            jax.ShapeDtypeStruct((8, count * shard), f32),
        ],
        compiler_params=pltpu.CompilerParams(vmem_limit_bytes=vmem_bytes),
        cost_estimate=light,
        name="unpack_tables",
    )(order, *blocks)


def pack_tables(gate_grads, small_grads, order, count, shard, piece, block_width):
    width = gate_grads.shape[0]

    def kernel(order_ref, gate_ref, small_ref, left, right):
        spreader = one_hot(256, width, lambda row, column: row == column % block_width)
        same = lax.broadcasted_iota(jnp.int32, (width, width), 0) // block_width == (
            lax.broadcasted_iota(jnp.int32, (width, width), 1) // block_width
        )
        folded = [
            dot_back(
                jnp.where(same, gate_ref[:, k * width : (k + 1) * width], 0.0).astype(bf16),
                spreader,
            )
            for k in range(2)
        ]
        picker = one_hot(8, 256, lambda row, column: row == column)
        folded.append(dot_rows(small_ref[...].astype(bf16), picker))
        owner = lax.broadcasted_iota(jnp.int32, (width, 256), 0) % block_width // piece
        movers = table_movers(width, shard, piece, block_width)
        for r in range(count):
            total = None
            for k in range(3):
                mine = jnp.where(owner == order_ref[r], folded[k], 0.0).astype(bf16)
                term = dot_rows(movers[k], mine)
                total = term if total is None else total + term
            at = slice(r * shard, (r + 1) * shard)
            left[at, :] = total[:, :128].astype(bf16)
            right[at, :] = total[:, 128:].astype(bf16)

    shape = (count * shard, 128)
    return pl.pallas_call(
        kernel,
        grid_spec=pltpu.PrefetchScalarGridSpec(
            num_scalar_prefetch=1,
            grid=(1,),
            in_specs=[fixed(gate_grads.shape), fixed(small_grads.shape)],
            out_specs=[fixed(shape)] * 2,
        ),
        out_shape=[jax.ShapeDtypeStruct(shape, bf16)] * 2,
        compiler_params=pltpu.CompilerParams(vmem_limit_bytes=vmem_bytes),
        cost_estimate=light,
        name="pack_tables",
    )(order, gate_grads, small_grads)


def prepare(whole, order, place, size, gain):
    total, features = whole.shape
    rows = total // 4
    groups = features // size

    def kernel(order_ref, place_ref, value_ref, gain_ref, out, own):
        j = pl.program_id(0)

        def step(c, carry):
            at = pl.ds(pl.multiple_of(c * 16, 16), 16)
            value = value_ref[at, :].astype(f32)
            scale = lax.rsqrt(jnp.mean(value * value, axis=1, keepdims=True) + epsilon)
            for r in range(groups):
                to = slice(r * size, (r + 1) * size)
                start = pl.multiple_of(order_ref[r] * size, size)
                part = value_ref[at, pl.ds(start, size)].astype(f32)
                out[at, to] = (part * scale * gain_ref[:, to]).astype(bf16)
            return carry

        lax.fori_loop(0, rows // 16, step, 0, unroll=2)

        @pl.when(j == place_ref[0])
        def _():
            for r in range(groups):
                start = pl.multiple_of(order_ref[r] * size, size)
                own[:, r * size : (r + 1) * size] = value_ref[:, pl.ds(start, size)]

    block = pl.BlockSpec((rows, features), lambda g, *_: (g, 0))
    return pl.pallas_call(
        kernel,
        grid_spec=pltpu.PrefetchScalarGridSpec(
            num_scalar_prefetch=2,
            grid=(4,),
            in_specs=[block, fixed((1, features))],
            out_specs=[block, fixed((rows, features))],
        ),
        out_shape=[
            jax.ShapeDtypeStruct((total, features), bf16),
            jax.ShapeDtypeStruct((rows, features), bf16),
        ],
        compiler_params=pltpu.CompilerParams(vmem_limit_bytes=vmem_bytes),
        cost_estimate=light,
        name="prepare",
    )(order, place, whole, gain.reshape(1, features))


def move_columns(blocks, order, size):
    rows, features = blocks[0].shape
    groups = features // size

    def kernel(order_ref, *refs):
        out = refs[-1]
        for r in range(groups):
            start = pl.multiple_of(order_ref[r] * size, size)
            for j, ref in enumerate(refs[:-1]):
                out[j * rows : (j + 1) * rows, r * size : (r + 1) * size] = ref[
                    :, pl.ds(start, size)
                ]

    return pl.pallas_call(
        kernel,
        grid_spec=pltpu.PrefetchScalarGridSpec(
            num_scalar_prefetch=1,
            grid=(1,),
            in_specs=[fixed((rows, features))] * len(blocks),
            out_specs=fixed((rows * len(blocks), features)),
        ),
        out_shape=jax.ShapeDtypeStruct((rows * len(blocks), features), blocks[0].dtype),
        compiler_params=pltpu.CompilerParams(vmem_limit_bytes=vmem_bytes),
        cost_estimate=light,
        name="move_columns",
    )(order, *blocks)


class Ring:
    def __init__(self, count):
        self.count = count
        order = list(range(0, count, 2)) + list(range(1, count, 2))[::-1]
        self.order = order
        self.place_of = [order.index(index) for index in range(count)]
        ahead = [(order[(i + 1) % count], order[i]) for i in range(count)]
        behind = [(order[i], order[(i + 1) % count]) for i in range(count)]
        self.pairs = (ahead, behind)
        index = lax.axis_index("dp")
        half = (count + 1) // 2
        self.place = jnp.where(
            lax.rem(index, 2) == 0, lax.div(index, 2), count - 1 - lax.div(index, 2)
        ).astype(jnp.int32)
        spots = lax.rem(jnp.arange(count, dtype=jnp.int32) + self.place, count)
        self.block_of = jnp.where(spots < half, 2 * spots, 2 * (count - 1 - spots) + 1)
        self.step_of = self.steps_to(jnp.arange(count, dtype=jnp.int32))

    def steps_to(self, index):
        places = jnp.where(index % 2 == 0, index // 2, self.count - 1 - index // 2)
        return (places - self.place + self.count) % self.count

    def normal_in(self, rows, place, size, gain):
        if size % 128 == 0:
            return prepare(rows, self.block_of, place, size, gain)
        whole = self.columns_in([rows], size)
        value = whole.astype(f32)
        scale = lax.rsqrt(jnp.mean(value * value, axis=1, keepdims=True) + epsilon)
        own = whole.shape[0] // 4
        return (value * scale * gain).astype(bf16), lax.dynamic_slice_in_dim(
            whole, place[0] * own, own, axis=0
        )

    def columns_in(self, blocks, size):
        if size % 128 == 0:
            return move_columns(blocks, self.block_of, size)
        whole = jnp.concatenate(blocks, axis=0)
        ordered = [whole[:, i * size : (i + 1) * size] for i in self.order]
        return lax.dynamic_slice_in_dim(
            jnp.concatenate(ordered + ordered, axis=1),
            self.place * size,
            self.count * size,
            axis=1,
        )

    def columns_out(self, whole, size):
        if size % 128 == 0:
            return move_columns([whole], self.step_of, size)
        start = lax.rem(self.count - self.place, self.count) * size
        ordered = lax.dynamic_slice_in_dim(
            jnp.concatenate([whole, whole], axis=1), start, self.count * size, axis=1
        )
        return jnp.concatenate(
            [ordered[:, i * size : (i + 1) * size] for i in self.place_of], axis=1
        )


class Gather:
    work = 0.0

    def __init__(self, ring, own, far, axis):
        count = ring.count
        reach = count // 2 if far else (count - 1) // 2
        self.total = count
        self.hops = (reach, count - 1 - reach)
        self.left = count - 1
        self.blocks = [own] + [None] * (count - 1)
        self.axis = axis

    def receive(self, way, hop, value):
        self.blocks[hop + 1 if way == 0 else self.total - 1 - hop] = value
        self.left -= 1

    def operand(self, way, hop, gate):
        return self.blocks[hop if way == 0 else (self.total - hop) % self.total]

    def pieces(self):
        if self.blocks[0].shape[self.axis] % 128 == 0:
            return self.blocks
        return [jnp.concatenate(self.blocks, axis=self.axis)]


class Scatter:
    work = 2.0

    def __init__(self, ring, part, far):
        count = ring.count
        reach = count // 2 if far else (count - 1) // 2
        self.total = count
        self.hops = (count - 1 - reach, reach)
        self.left = count - 1
        self.part = part
        self.got = [None, None]

    def receive(self, way, hop, value):
        self.got[way] = value
        self.left -= 1

    def operand(self, way, hop, gate):
        distance = self.hops[way] - hop
        value = self.part[distance if way == 1 else self.total - distance]
        if hop:
            (got,) = gate(self.got[way])
            value = (value.astype(f32) + got.astype(f32)).astype(bf16)
        return value

    def result(self, gate):
        got = gate(*self.got)
        return self.part[0].astype(f32) + got[0].astype(f32) + got[1].astype(f32)


class Lanes:
    def __init__(self, ring, depth):
        self.ring = ring
        self.depth = depth
        self.queue = ([], [])
        self.flying = ([], [])
        self.link = [0.0, 0.0]
        self.now = 0.0
        self.marks = []

    def gate(self, *values):
        if not self.marks:
            return values
        return lax.optimization_barrier(tuple(values) + tuple(self.marks))[: len(values)]

    def mark(self, *values):
        self.marks = list(values)

    def add(self, *chains):
        for chain in chains:
            for way in range(2):
                if chain.hops[way]:
                    self.queue[way].append(chain)
        self.fill()

    def start(self, way, chain, hop):
        (operand,) = self.gate(chain.operand(way, hop, self.gate))
        self.mark(operand)
        self.now += chain.work + 2.0
        value = lax.ppermute(operand, "dp", self.ring.pairs[way])
        begin = max(self.now, self.link[way])
        self.link[way] = begin + operand.size / 22000.0
        self.flying[way].append((self.link[way] + 3.0, chain, hop, value))

    def fill(self):
        for way in range(2):
            while self.queue[way] and len(self.flying[way]) < self.depth:
                self.start(way, self.queue[way].pop(0), 0)

    def step(self, limit):
        heads = [(self.flying[way][0][0], way) for way in range(2) if self.flying[way]]
        if not heads or min(heads)[0] > limit:
            return False
        finish, way = min(heads)
        _, chain, hop, value = self.flying[way].pop(0)
        self.now = max(self.now, finish)
        chain.receive(way, hop, value)
        if hop + 1 < chain.hops[way]:
            self.start(way, chain, hop + 1)
        else:
            self.mark(value, *self.marks)
        self.fill()
        return True

    def catch_up(self, time=None):
        time = self.now if time is None else time
        while self.step(time):
            time = max(time, self.now)
        self.now = max(self.now, time)

    def serve(self, times):
        for _ in range(2 * times):
            self.step(float("inf"))

    def until(self, *chains):
        while any(chain.left for chain in chains):
            assert self.step(float("inf"))

    def did(self, time, *values):
        self.mark(*values)
        self.now += time
        self.catch_up()


core_pairs = [(0, 1), (1, 0), (2, 3), (3, 2)]
chip_pairs = [(0, 2), (1, 3), (2, 0), (3, 1)]


def tensor_gather(own):
    return lax.all_gather(own, "tensor", axis=0, tiled=True)


def tensor_reduce(whole):
    return lax.psum_scatter(whole, "tensor", scatter_dimension=0, tiled=True)


def tensor_scatter(blocks):
    own, sibling, across, far = blocks
    far = lax.ppermute(far, "tensor", core_pairs)
    sibling, far = lax.optimization_barrier((sibling, far))
    sibling = lax.ppermute(sibling, "tensor", core_pairs)
    across = (across.astype(f32) + far.astype(f32)).astype(bf16)
    across, sibling = lax.optimization_barrier((across, sibling))
    return own, sibling, across, lax.ppermute(across, "tensor", chip_pairs)


def summed(parts):
    own, sibling, _, across = parts
    return own.astype(f32) + sibling.astype(f32) + across.astype(f32)


def tensor_sum(value):
    value = value + lax.ppermute(value, "tensor", core_pairs)
    return value + lax.ppermute(value, "tensor", chip_pairs)


def row_scale(values):
    return lax.rsqrt(jnp.mean(values * values, axis=-1, keepdims=True) + epsilon)


def norm_backward(values, scale, gain, grad):
    weighted = grad * gain
    inner = jnp.mean(weighted * values, axis=-1, keepdims=True)
    return scale * weighted - values * (scale * scale * scale * inner)


def body(
    inputs,
    segment_ids,
    gain_mixer,
    branch_weight,
    input_weight,
    conv_weight,
    conv_bias,
    rate_weight,
    rate_bias,
    entry_weight,
    entry_bias,
    decay_param,
    output_weight,
    gain_mlp,
    gate_weight,
    up_weight,
    down_weight,
    cotangent,
    *,
    dp,
    tensor,
):
    ring = Ring(dp)
    lanes = Lanes(ring, 2)
    shard, width = branch_weight.shape
    features = inputs.shape[1]
    length = segment_ids.shape[0]
    gate_blocks, piece, block_width = rate_weight.shape
    taps = conv_weight.shape[0]
    units = gate_weight.shape[1]
    place = lax.axis_index("tensor").astype(jnp.int32).reshape(1)

    table_rows = gate_blocks * piece
    wide = 256
    columns = jnp.stack(
        [conv_weight[k] for k in range(taps)] + [conv_bias, rate_bias, entry_bias, decay_param],
        axis=-1,
    )

    def padded(rows):
        return jnp.pad(rows, ((0, 0), (0, wide - rows.shape[1])))

    table = jnp.concatenate(
        [
            padded(rate_weight.reshape(table_rows, block_width)),
            padded(entry_weight.reshape(table_rows, block_width)),
            padded(columns.reshape(table_rows, taps + 4)),
            padded(jnp.stack([gain_mixer, gain_mlp])),
        ],
        axis=0,
    )
    table = jnp.pad(table, ((0, shard - 3 * table_rows - 2), (0, 0)))

    masks = []
    for offset in range(1, taps):
        earlier = jnp.concatenate(
            [jnp.full((offset,), -1, segment_ids.dtype), segment_ids[: length - offset]]
        )
        masks.append((earlier == segment_ids).astype(f32))
    masks = jnp.stack([masks[0]] + masks, axis=1)
    masks = jnp.pad(masks, ((0, 0), (0, 128 - taps)))

    half = units // 2
    halves = (slice(0, half), slice(half, units))
    table_chain = Gather(ring, table, False, 0)
    pair_chains = [Gather(ring, branch_weight, True, 0), Gather(ring, input_weight, False, 0)]
    output_chain = Gather(ring, output_weight, True, 1)
    gated_chains = [
        Gather(
            ring,
            jnp.concatenate([gate_weight[:, at], up_weight[:, at]], axis=1),
            at.start == 0,
            0,
        )
        for at in halves
    ]
    down_chains = [Gather(ring, down_weight[at], at.start == 0, 1) for at in halves]
    lanes.now = 10.0
    input_rows = tensor_gather(inputs)
    lanes.add(pair_chains[0], table_chain, pair_chains[1], output_chain, *gated_chains, *down_chains)
    cotangent_rows = tensor_gather(cotangent)

    lanes.until(table_chain)
    gates, small, gains = unpack_tables(
        lanes.gate(*table_chain.blocks),
        ring.block_of,
        width,
        piece,
        block_width,
    )
    gain_one, gain_two = gains[0], gains[1]
    decay_full = small[7:8]
    small = jnp.concatenate([small[:7], -lru_scale * jax.nn.softplus(-decay_full)], axis=0)
    mixer_rows, tokens_low = ring.normal_in(input_rows, place, shard, gain_one)
    lanes.did(18.0, mixer_rows)
    lanes.until(*pair_chains)
    (mixer_rows,) = lanes.gate(mixer_rows)

    rows = inputs.shape[0]
    start = jnp.zeros((1,), jnp.int32)
    pair_weights = [chain.pieces() for chain in pair_chains]
    pre = collect(mixer_rows, pair_weights, width, False, "mixer_in")
    lanes.did(12.0, pre)
    (pre,) = lanes.gate(pre)
    mixer_low, mixed, rate, entry, state = core_forward(start, pre, masks, gates, small, tensor)
    lanes.did(21.0, mixer_low)
    lanes.until(output_chain)
    output_pieces = output_chain.pieces()
    (mixer_low,) = lanes.gate(mixer_low)
    mixer_out = spread([(mixer_low, 0, width)], [output_pieces], place, (), False, "mixer_out")
    lanes.did(9.0, mixer_out)
    mixer_sum = tensor_reduce(mixer_out)
    arrival = lanes.now + 46.0
    (cotangent_rows,) = lanes.gate(cotangent_rows)
    cotangent_rows = ring.columns_in([cotangent_rows], shard)
    lanes.did(5.0, cotangent_rows)
    lanes.catch_up(arrival)
    (mixer_sum,) = lanes.gate(mixer_sum)
    tokens = tokens_low.astype(f32)
    middle = tokens + mixer_sum.astype(f32)
    scale_two = row_scale(middle)
    mlp_own = (middle * scale_two * gain_two).astype(bf16)
    lanes.did(5.0, mlp_own)
    mlp_rows = tensor_gather(mlp_own)
    lanes.catch_up(lanes.now + 34.0)
    (mlp_rows,) = lanes.gate(mlp_rows)

    def columns_of(array, r):
        return lax.slice_in_dim(array, r * shard, (r + 1) * shard, axis=1)

    hidden, acts, slopes = [], [], []
    for h in range(2):
        lanes.until(gated_chains[h])
        (gated,) = lanes.gate(mlp_rows)
        one, two, three = gated_forward(gated, gated_chains[h].pieces())
        hidden.append(one)
        acts.append(two)
        slopes.append(three)
        lanes.did(13.5, one)
    lefts = lanes.gate(*hidden)
    down_scatters = [
        Scatter(ring, part, h == 1)
        for h, part in enumerate(weight_grads(lefts, cotangent_rows, dp, False, "down_grads"))
    ]
    lanes.did(13.5, down_scatters[0].part[0])
    lanes.add(*down_scatters)
    gated_lows, gated_scatters = [], []
    for h in range(2):
        lanes.until(down_chains[h])
        (gated,) = lanes.gate(cotangent_rows)
        low = gated_backward(gated, down_chains[h].pieces(), acts[h], slopes[h])
        gated_lows.append(low)
        lanes.did(8.5, low)
    (gated,) = lanes.gate(gated_lows[0])
    gated_scatters.append(
        Scatter(ring, weight_grads([mlp_rows], gated, dp, True, "gated_grads")[0], True)
    )
    lanes.did(14.0, gated_scatters[0].part[0])
    lanes.add(gated_scatters[0])
    weights = [chain.pieces() for chain in gated_chains]

    lefts = [(low, 0, 2 * half) for low in lanes.gate(*gated_lows)]
    mlp_in_grad = spread(lefts, weights, place, (), True, "mlp_in_grad")
    lanes.did(20.5, mlp_in_grad)
    mlp_in_grad = tensor_reduce(mlp_in_grad)
    arrival = lanes.now + 46.0
    (gated,) = lanes.gate(gated_lows[1])
    gated_scatters.append(
        Scatter(ring, weight_grads([mlp_rows], gated, dp, True, "gated_grads")[0], False)
    )
    lanes.did(14.0, gated_scatters[1].part[0])
    lanes.add(gated_scatters[1])
    lanes.catch_up(arrival)
    (mlp_in_grad,) = lanes.gate(mlp_in_grad)
    middle_norm_grad = norm_backward(middle, scale_two, gain_two, mlp_in_grad.astype(f32))
    middle_grad = (
        lax.dynamic_slice_in_dim(cotangent_rows, place[0] * rows, rows, axis=0).astype(f32)
        + middle_norm_grad
    )
    residual_own = middle_grad.astype(bf16)
    lanes.did(6.0, residual_own)
    residual_rows = tensor_gather(residual_own)
    arrival = lanes.now + 34.0
    late = [(low, 0, half) for low in lanes.gate(*hidden)]
    mlp_out = spread(
        late, [chain.pieces() for chain in down_chains], place, (), False, "mlp_out"
    )
    lanes.did(13.0, mlp_out)
    lanes.catch_up(arrival)
    mlp_out, residual_rows = lanes.gate(mlp_out, residual_rows)
    mlp_sum = tensor_reduce(mlp_out)

    mixer_grad = collect(residual_rows, [output_pieces], width, True, "mixer_grad")
    lanes.did(8.0, mixer_grad)
    (residual_rows,) = lanes.gate(residual_rows)
    output_scatter = Scatter(
        ring, weight_grads([mixer_low], residual_rows, dp, False, "output_grads")[0], True
    )
    lanes.did(9.0, output_scatter.part[0])
    lanes.add(output_scatter)
    (mixer_grad,) = lanes.gate(mixer_grad)
    pair_low, gate_grads, small_grads = core_backward(
        start, mixer_grad, pre, mixed, rate, entry, state, masks, gates, small, tensor
    )
    lanes.did(28.0, pair_low)
    decay_grad = lru_scale * small_grads[7:8] * jax.nn.sigmoid(-decay_full)
    small_grads = jnp.concatenate([small_grads[:7], decay_grad], axis=0)
    grad_tables = pack_tables(
        gate_grads, small_grads, ring.block_of, dp, shard, piece, block_width
    )
    lanes.did(8.0, grad_tables[0])
    (low,) = lanes.gate(pair_low)
    pair_parts = weight_grads([mixer_rows], low, dp, True, "pair_grads", grad_tables)
    pair_scatters = [Scatter(ring, part, h == 0) for h, part in enumerate(pair_parts)]
    lanes.did(13.0, pair_parts[0][0])
    lanes.add(*pair_scatters)
    (pair_low,) = lanes.gate(pair_low)
    mixer_in_grad = spread(
        [(pair_low, 0, width), (pair_low, 1, width)],
        pair_weights,
        place,
        (),
        True,
        "mixer_in_grad",
    )
    lanes.did(12.0, mixer_in_grad)
    mixer_in_grad = tensor_reduce(mixer_in_grad)
    arrival = lanes.now + 48.0
    (mlp_sum,) = lanes.gate(mlp_sum)
    layer_out = ring.columns_out((middle + mlp_sum.astype(f32)).astype(bf16), shard)
    lanes.did(6.0, layer_out)
    lanes.catch_up(arrival)
    (mixer_in_grad,) = lanes.gate(mixer_in_grad)
    tokens_norm_grad = norm_backward(
        tokens, row_scale(tokens), gain_one, mixer_in_grad.astype(f32)
    )
    inputs_grad = ring.columns_out((middle_grad + tokens_norm_grad).astype(bf16), shard)
    lanes.did(9.0, inputs_grad)
    lanes.until(*down_scatters, *gated_scatters, output_scatter, *pair_scatters)

    free = lambda *values: values
    pair_wgrads = [scatter.result(free) for scatter in pair_scatters]
    table_grad = jnp.concatenate([wgrad[:, width:] for wgrad in pair_wgrads], axis=1)
    pair_wgrads = [wgrad[:, :width] for wgrad in pair_wgrads]
    rate_wgrad, entry_wgrad, column_grads = [
        table_grad[k * table_rows : (k + 1) * table_rows].reshape(gate_blocks, piece, wide)
        for k in range(3)
    ]
    rate_wgrad = rate_wgrad[:, :, :block_width]
    entry_wgrad = entry_wgrad[:, :, :block_width]
    singles = [column_grads[:, :, k] for k in range(taps + 4)]
    gated_wgrads = [scatter.result(free) for scatter in gated_scatters]

    def gain_grad(gain, own_weights, wgrads):
        total = sum(
            jnp.sum(weight[:, : wgrad.shape[1]].astype(f32) * wgrad, axis=1)
            for weight, wgrad in zip(own_weights, wgrads)
        )
        return total / gain.astype(f32)

    gain_grads = tensor_sum(
        jnp.stack(
            [
                gain_grad(
                    gain_mixer,
                    [branch_weight, input_weight],
                    pair_wgrads,
                ),
                gain_grad(gain_mlp, [chain.blocks[0] for chain in gated_chains], gated_wgrads),
            ]
        )
    )
    return (
        layer_out,
        inputs_grad,
        gain_grads[0],
        *pair_wgrads,
        jnp.stack(singles[:taps]),
        singles[taps],
        rate_wgrad,
        singles[taps + 1],
        entry_wgrad,
        singles[taps + 2],
        singles[taps + 3],
        output_scatter.result(free),
        gain_grads[1],
        jnp.concatenate([wgrad[:, :half] for wgrad in gated_wgrads], axis=1),
        jnp.concatenate([wgrad[:, half:] for wgrad in gated_wgrads], axis=1),
        jnp.concatenate([scatter.result(free) for scatter in down_scatters], axis=0),
    )


def solution(mesh):
    return jax.shard_map(
        functools.partial(body, dp=mesh.shape["dp"], tensor=mesh.shape["tensor"]),
        mesh=mesh,
        in_specs=(
            P(("dp", "tensor"), None),
            P("dp"),
            P("dp"),
            P("dp", "tensor"),
            P("dp", "tensor"),
            P(None, "tensor", "dp"),
            P("tensor", "dp"),
            P("tensor", "dp", None),
            P("tensor", "dp"),
            P("tensor", "dp", None),
            P("tensor", "dp"),
            P("tensor", "dp"),
            P("tensor", "dp"),
            P("dp"),
            P("dp", "tensor"),
            P("dp", "tensor"),
            P("tensor", "dp"),
            P(("dp", "tensor"), None),
        ),
        out_specs=(
            P(("dp", "tensor"), None),
            P(("dp", "tensor"), None),
            P("dp"),
            P("dp", "tensor"),
            P("dp", "tensor"),
            P(None, "tensor", "dp"),
            P("tensor", "dp"),
            P("tensor", "dp", None),
            P("tensor", "dp"),
            P("tensor", "dp", None),
            P("tensor", "dp"),
            P("tensor", "dp"),
            P("tensor", "dp"),
            P("dp"),
            P("dp", "tensor"),
            P("dp", "tensor"),
            P("tensor", "dp"),
        ),
        check_vma=False,
    )
```

```python
import functools

import jax
import jax.numpy as jnp
from jax import lax
from jax.experimental import pallas as pl
from jax.experimental.pallas import tpu as pltpu
from jax.sharding import PartitionSpec as P

epsilon = 1e-06
lru_scale = 8.0
root = 0.7978845608028654
cubic = 0.044715
f32 = jnp.float32
bf16 = jnp.bfloat16
vmem_bytes = 56 * 1024 * 1024
light = pl.CostEstimate(flops=6_000_000_000, bytes_accessed=30_000_000, transcendentals=0)


def gelu_both(value):
    square = value * value
    th = jnp.tanh(root * value * (1.0 + cubic * square))
    half = 0.5 * (1.0 + th)
    slope = half + 0.5 * value * (1.0 - th * th) * (root * (1.0 + 3.0 * cubic * square))
    return value * half, slope


def gelu(value):
    return value * (0.5 * (1.0 + jnp.tanh(root * value * (1.0 + cubic * value * value))))


def one_minus_exp(x, exp_x):
    series = 1.0 + x * (1.0 / 7.0)
    for order in (6.0, 5.0, 4.0, 3.0, 2.0):
        series = 1.0 + x * (1.0 / order) * series
    return jnp.where(x > -0.5, -x * series, 1.0 - exp_x)


def decay_terms(rate, slope, keep):
    log_decay = slope * rate
    expo = jnp.exp(log_decay)
    square = expo * expo
    factor = jnp.where(keep > 0.0, jnp.sqrt(one_minus_exp(2.0 * log_decay, square)), 1.0)
    return expo * keep, square, factor


def row_index(width):
    return lax.broadcasted_iota(jnp.int32, (8, width), 0)


def down_by(current, before, offset, rows):
    if offset == 0:
        return current
    return jnp.where(
        rows < offset, pltpu.roll(before, offset, 0), pltpu.roll(current, offset, 0)
    )


def up_by(current, after, offset, rows):
    if offset == 0:
        return current
    return jnp.where(
        rows < 8 - offset,
        pltpu.roll(current, 8 - offset, 0),
        pltpu.roll(after, 8 - offset, 0),
    )


def core_forward_kernel(
    place, branch, entry_pre, masks, gates, small, out, mixed_out, rate_out, entry_out, state_out,
    mixed_low, pre, last_entry, last_state,
):
    length, width = entry_pre.shape
    rows = row_index(width)

    @pl.when(pl.program_id(0) == 0)
    def _():
        last_entry[...] = jnp.zeros_like(last_entry)
        last_state[...] = jnp.zeros_like(last_state)

    taps = [small[k : k + 1, :] for k in range(4)]
    conv_bias = small[4:5, :]

    def convolve(step, before):
        parts = []
        for half in range(2):
            at = pl.ds(pl.multiple_of(step * 16 + half * 8, 8), 8)
            here = entry_pre[at, :]
            mask = masks[at, :]
            mixed = here * taps[0] + conv_bias
            for k in range(1, 4):
                mixed += down_by(here, before, k, rows) * mask[:, k : k + 1] * taps[k]
            mixed_out[at, :] = mixed
            parts.append(mixed)
            before = here
        mixed_low[pl.ds(pl.multiple_of(step * 16, 16), 16), :] = jnp.concatenate(
            parts, axis=0
        ).astype(bf16)
        return before

    last_entry[...] = lax.fori_loop(0, length // 16, convolve, last_entry[...], unroll=4)
    pre[...] = jnp.dot(mixed_low[...], gates[...], preferred_element_type=f32)
    rate_bias = small[5:6, :]
    entry_bias = small[6:7, :]
    slope = small[7:8, :]

    def scan(step, carry):
        parts = []
        for half in range(2):
            at = pl.ds(pl.multiple_of(step * 16 + half * 8, 8), 8)
            keep = masks[at, :][:, 0:1]
            rate = jax.nn.sigmoid(pre[at, :width] + rate_bias)
            entry = jax.nn.sigmoid(pre[at, width:] + entry_bias)
            decay, _, factor = decay_terms(rate, slope, keep)
            drive = factor * entry * mixed_out[at, :]
            for shift in (1, 2, 4):
                inside = rows >= shift
                drive += decay * jnp.where(inside, pltpu.roll(drive, shift, 0), 0.0)
                decay = decay * jnp.where(inside, pltpu.roll(decay, shift, 0), 1.0)
            state = drive + decay * carry
            carry = jnp.broadcast_to(state[7:8, :], state.shape)
            rate_out[at, :] = rate
            entry_out[at, :] = entry
            state_out[at, :] = state
            parts.append(gelu(branch[at, :]) * state)
        out[pl.ds(pl.multiple_of(step * 16, 16), 16), :] = jnp.concatenate(parts, axis=0).astype(
            bf16
        )
        return carry

    last_state[...] = lax.fori_loop(0, length // 16, scan, last_state[...], unroll=4)


def core_backward_kernel(
    place, grad, entry_pre, mixed_in, rate_in, entry_in, state_in, state_tail, entry_tail,
    masks, gates, small, low, gate_grads, small_grads,
    state_long, entry_long, gate_low, mixed_grad, sums, next_decay, next_carried, next_mixed,
):
    length, width = entry_pre.shape
    rows = row_index(width)

    @pl.when(pl.program_id(0) == 0)
    def _():
        next_decay[...] = jnp.zeros_like(next_decay)
        next_carried[...] = jnp.zeros_like(next_carried)
        next_mixed[...] = jnp.zeros_like(next_mixed)
        sums[...] = jnp.zeros_like(sums)
        gate_grads[...] = jnp.zeros_like(gate_grads)

    state_long[0:8, :] = state_tail[...]
    state_long[8:, :] = state_in[...]
    entry_long[0:8, :] = entry_tail[...]
    entry_long[8:, :] = entry_pre[...]
    slope = small[7:8, :]

    def reverse(step, carry):
        after_decay, carried_after = carry
        step = length // 16 - 1 - step
        rate_parts, entry_parts = [], []
        for half in (1, 0):
            start = pl.multiple_of(step * 16 + half * 8, 8)
            at = pl.ds(start, 8)
            keep = masks[at, :][:, 0:1]
            rate = rate_in[at, :]
            entry = entry_in[at, :]
            mixed = mixed_in[at, :]
            decay, square, factor = decay_terms(rate, slope, keep)
            state = state_in[at, :]
            value = grad[at, :]
            ahead = up_by(decay, after_decay, 1, rows)
            after_decay = decay
            for shift in (1, 2, 4):
                inside = rows < 8 - shift
                value += ahead * jnp.where(inside, pltpu.roll(value, 8 - shift, 0), 0.0)
                ahead = ahead * jnp.where(inside, pltpu.roll(ahead, 8 - shift, 0), 1.0)
            carried = value + ahead * carried_after
            carried_after = jnp.broadcast_to(carried[0:1, :], carried.shape)
            earlier = down_by(state, state_long[at, :], 1, rows)
            driven = carried * entry
            log_grad = keep * (carried * earlier * decay - driven * mixed * square / factor)
            scaled = log_grad * rate
            rate_pre_grad = slope * scaled * (1.0 - rate)
            entry_pre_grad = driven * factor * mixed * (1.0 - entry)
            mixed_grad[at, :] = driven * factor
            sums[40:48, :] += rate_pre_grad
            sums[48:56, :] += entry_pre_grad
            sums[56:64, :] += scaled
            rate_parts.append(rate_pre_grad)
            entry_parts.append(entry_pre_grad)
        both = pl.ds(pl.multiple_of(step * 16, 16), 16)
        gate_low[both, :width] = jnp.concatenate(rate_parts[::-1], axis=0).astype(bf16)
        gate_low[both, width:] = jnp.concatenate(entry_parts[::-1], axis=0).astype(bf16)
        return after_decay, carried_after

    after_decay, carried_after = lax.fori_loop(
        0, length // 16, reverse, (next_decay[...], next_carried[...]), unroll=4
    )
    next_decay[...] = after_decay
    next_carried[...] = carried_after
    mixed_grad[...] += lax.dot_general(
        gate_low[...], gates[...], (((1,), (1,)), ((), ())), preferred_element_type=f32
    )
    gate_grads[...] += lax.dot_general(
        mixed_in[...].astype(bf16),
        gate_low[...],
        (((0,), (0,)), ((), ())),
        preferred_element_type=f32,
    )
    taps = [small[k : k + 1, :] for k in range(4)]

    def convolve(step, after):
        step = length // 16 - 1 - step
        parts = []
        for half in (1, 0):
            start = pl.multiple_of(step * 16 + half * 8, 8)
            at = pl.ds(start, 8)
            mask = masks[at, :]
            here = mixed_grad[at, :]
            value = entry_pre[at, :]
            before = entry_long[at, :]
            sums[32:40, :] += here
            sums[0:8, :] += here * value
            total = here * taps[0]
            masked = [here * mask[:, k : k + 1] for k in range(1, 4)]
            for k in range(1, 4):
                sums[8 * k : 8 * k + 8, :] += masked[k - 1] * down_by(value, before, k, rows)
                total += up_by(masked[k - 1], after[k - 1], k, rows) * taps[k]
            after = masked
            parts.append(total)
        low[pl.ds(pl.multiple_of(step * 16, 16), 16), :] = jnp.concatenate(
            parts[::-1], axis=0
        ).astype(bf16)
        return after

    after = lax.fori_loop(
        0,
        length // 16,
        convolve,
        [next_mixed[8 * k : 8 * k + 8, :] for k in range(3)],
        unroll=4,
    )
    for k in range(3):
        next_mixed[8 * k : 8 * k + 8, :] = after[k]

    @pl.when(pl.program_id(0) == pl.num_programs(0) - 1)
    def _():
        for k in range(8):
            small_grads[k : k + 1, :] = jnp.sum(sums[8 * k : 8 * k + 8, :], axis=0, keepdims=True)


def core_forward(place, pre, masks, gates, small, blocks):
    total, width = pre.shape[0], pre.shape[1] // 2
    length = total // blocks
    wide = lambda column: pl.BlockSpec((length, width), lambda b, t: (b ^ t[0], column))
    whole = lambda shape: pl.BlockSpec(shape, lambda b, t: (0, 0))
    kept = jax.ShapeDtypeStruct((total, width), f32)
    return pl.pallas_call(
        core_forward_kernel,
        grid_spec=pltpu.PrefetchScalarGridSpec(
            num_scalar_prefetch=1,
            grid=(blocks,),
            in_specs=[
                wide(0),
                wide(1),
                pl.BlockSpec((length, 128), lambda b, t: (b, 0)),
                whole(gates.shape),
                whole(small.shape),
            ],
            out_specs=[wide(0)] * 5,
            scratch_shapes=[
                pltpu.VMEM((length, width), bf16),
                pltpu.VMEM((length, 2 * width), f32),
                pltpu.VMEM((8, width), f32),
                pltpu.VMEM((8, width), f32),
            ],
        ),
        out_shape=[jax.ShapeDtypeStruct((total, width), bf16)] + [kept] * 4,
        compiler_params=pltpu.CompilerParams(vmem_limit_bytes=vmem_bytes),
        cost_estimate=light,
        name="core_forward",
    )(place, pre, pre, masks, gates, small)


def core_backward(place, grad, pre, mixed, rate, entry, state, masks, gates, small, blocks):
    total, width = grad.shape
    length = total // blocks
    back = lambda g: blocks - 1 - g
    wide = lambda column: pl.BlockSpec((length, width), lambda g, t: (back(g) ^ t[0], column))
    whole = lambda shape: pl.BlockSpec(shape, lambda g, t: (0, 0))

    def tail(column):
        def at(g, t):
            block = jnp.maximum(back(g) - 1, 0) ^ t[0]
            return (block * (length // 8) + length // 8 - 1, column)

        return pl.BlockSpec((8, width), at)

    return pl.pallas_call(
        core_backward_kernel,
        grid_spec=pltpu.PrefetchScalarGridSpec(
            num_scalar_prefetch=1,
            grid=(blocks,),
            in_specs=[
                wide(0),
                wide(1),
                wide(0),
                wide(0),
                wide(0),
                wide(0),
                tail(0),
                tail(1),
                pl.BlockSpec((length, 128), lambda g, t: (back(g), 0)),
                whole(gates.shape),
                whole(small.shape),
            ],
            out_specs=[
                wide(0),
                whole(gates.shape),
                whole((8, width)),
            ],
            scratch_shapes=[
                pltpu.VMEM((length + 8, width), f32),
                pltpu.VMEM((length + 8, width), f32),
                pltpu.VMEM((length, 2 * width), bf16),
                pltpu.VMEM((length, width), f32),
                pltpu.VMEM((64, width), f32),
                pltpu.VMEM((8, width), f32),
                pltpu.VMEM((8, width), f32),
                pltpu.VMEM((24, width), f32),
            ],
        ),
        out_shape=[
            jax.ShapeDtypeStruct((total, width), bf16),
            jax.ShapeDtypeStruct(gates.shape, f32),
            jax.ShapeDtypeStruct((8, width), f32),
        ],
        compiler_params=pltpu.CompilerParams(vmem_limit_bytes=vmem_bytes),
        cost_estimate=light,
        name="core_backward",
    )(place, grad, pre, mixed, rate, entry, state, state, pre, masks, gates, small)


def dot(left, right):
    return jnp.dot(left, right, preferred_element_type=f32)


def dot_rows(left, right):
    return lax.dot_general(left, right, (((0,), (0,)), ((), ())), preferred_element_type=f32)


def dot_back(left, right):
    return lax.dot_general(left, right, (((1,), (1,)), ((), ())), preferred_element_type=f32)


def fixed(shape):
    zeros = (0,) * len(shape)
    return pl.BlockSpec(shape, lambda *_: zeros)


def call(kernel, name, grid, in_specs, out_specs, out_shape, scratch=()):
    return pl.pallas_call(
        kernel,
        grid=grid,
        in_specs=in_specs,
        out_specs=out_specs,
        out_shape=out_shape,
        scratch_shapes=list(scratch),
        compiler_params=pltpu.CompilerParams(vmem_limit_bytes=vmem_bytes),
        cost_estimate=light,
        name=name,
    )


def spread(lefts, weights, place, blocks, transposed, name, base=None):
    total = lefts[0][0].shape[0]
    rows = total // 4
    pieces = len(weights[0])
    product = dot_back if transposed else dot
    sizes = [w.shape[0 if transposed else 1] for w in weights[0]]
    widths = [width for _, _, width in lefts]
    features = sum(sizes)
    terms = len(lefts)
    count = len(blocks) if blocks else 4

    def kernel(place_ref, *refs):
        left = [ref[...] for ref in refs[:terms]]
        flat = refs[terms : terms + terms * pieces]
        outs = refs[terms + terms * pieces + (base is not None) :]
        result = outs[-1]
        at = 0
        for r in range(pieces):
            value = None
            for i in range(terms):
                weight = flat[i * pieces + r]
                if transposed:
                    weight = weight[:, : widths[i]]
                else:
                    weight = weight[...]
                term = product(left[i], weight)
                value = term if value is None else value + term
            if base is not None:
                value += refs[terms + terms * pieces][:, at : at + sizes[r]].astype(f32)
            result[:, at : at + sizes[r]] = value.astype(bf16)
            at += sizes[r]
        if blocks:
            for g in range(count):

                @pl.when(pl.program_id(0) == g)
                def _():
                    outs[g][...] = result[...]

    def left_spec(column, width):
        if blocks:
            first = blocks[0]
            return pl.BlockSpec((rows, width), lambda g, t: ((first - g) ^ t[0], column))
        return pl.BlockSpec((rows, width), lambda g, t: (g, column))

    if blocks:
        out_specs = [fixed((rows, features))] * count
        out_shape = [jax.ShapeDtypeStruct((rows, features), bf16)] * count
        scratch = [pltpu.VMEM((rows, features), bf16)]
    else:
        out_specs = pl.BlockSpec((rows, features), lambda g, t: (g, 0))
        out_shape = jax.ShapeDtypeStruct((total, features), bf16)
        scratch = []
    return pl.pallas_call(
        kernel,
        grid_spec=pltpu.PrefetchScalarGridSpec(
            num_scalar_prefetch=1,
            grid=(count,),
            in_specs=[left_spec(column, width) for _, column, width in lefts]
            + [fixed(w.shape) for group in weights for w in group]
            + [pl.BlockSpec((rows, features), lambda g, t: (g, 0))] * (base is not None),
            out_specs=out_specs,
            scratch_shapes=scratch,
        ),
        out_shape=out_shape,
        compiler_params=pltpu.CompilerParams(vmem_limit_bytes=vmem_bytes),
        cost_estimate=light,
        name=name,
    )(place, *[left for left, _, _ in lefts], *[w for group in weights for w in group], *([] if base is None else [base]))


def collect(left, weights, width, transposed, name):
    total, features = left.shape
    rows = total // 4
    count = len(weights)
    pieces = len(weights[0])
    product = dot_back if transposed else dot
    sizes = [w.shape[1 if transposed else 0] for w in weights[0]]

    def kernel(*refs):
        out = refs[-1]
        for i in range(count):
            at = 0
            value = None
            for r in range(pieces):
                ref = refs[1 + i * pieces + r]
                weight = ref[...] if transposed else ref[:, :width]
                term = product(refs[0][:, at : at + sizes[r]], weight)
                value = term if value is None else value + term
                at += sizes[r]
            out[:, i * width : (i + 1) * width] = value

    return call(
        kernel,
        name,
        (4,),
        [pl.BlockSpec((rows, features), lambda g: (g, 0))]
        + [fixed(w.shape) for group in weights for w in group],
        pl.BlockSpec((rows, count * width), lambda g: (g, 0)),
        jax.ShapeDtypeStruct((total, count * width), f32),
    )(left, *[w for group in weights for w in group])


def mixer_back(left, weights, pre, state):
    total, features = left.shape
    rows = total // 4
    pieces = len(weights)
    sizes = [w.shape[1] for w in weights]
    width = state.shape[1]

    def kernel(*refs):
        branch_ref, state_ref, state_grad, branch_low = refs[1 + pieces :]
        at = 0
        value = None
        for r in range(pieces):
            term = dot_back(refs[0][:, at : at + sizes[r]], refs[1 + r][...])
            value = term if value is None else value + term
            at += sizes[r]
        act, slope = gelu_both(branch_ref[...])
        state_grad[...] = value * act
        branch_low[...] = (value * state_ref[...] * slope).astype(bf16)

    block = pl.BlockSpec((rows, width), lambda g: (g, 0))
    return call(
        kernel,
        "mixer_back",
        (4,),
        [pl.BlockSpec((rows, features), lambda g: (g, 0))]
        + [fixed(w.shape) for w in weights]
        + [block] * 2,
        [block] * 2,
        [
            jax.ShapeDtypeStruct((total, width), f32),
            jax.ShapeDtypeStruct((total, width), bf16),
        ],
    )(left, *weights, pre, state)


def gated_forward(left, weights):
    total, features = left.shape
    rows = total // 4
    pieces = len(weights)
    size = features // pieces
    units = weights[0].shape[1] // 2
    step = units // 3

    def kernel(*refs):
        left_ref = refs[0]
        hidden, act_out, slope_out = refs[1 + pieces :]
        for c in range(3):
            at = slice(c * step, (c + 1) * step)
            after = slice(units + c * step, units + (c + 1) * step)
            gate = up = None
            for r in range(pieces):
                part = left_ref[:, r * size : (r + 1) * size]
                one = dot(part, refs[1 + r][:, at])
                two = dot(part, refs[1 + r][:, after])
                gate = one if gate is None else gate + one
                up = two if up is None else up + two
            act, slope = gelu_both(gate)
            hidden[:, at] = (act * up).astype(bf16)
            act_out[:, at] = act.astype(bf16)
            slope_out[:, at] = (up * slope).astype(bf16)

    block = pl.BlockSpec((rows, units), lambda g: (g, 0))
    return call(
        kernel,
        "gated_forward",
        (4,),
        [pl.BlockSpec((rows, features), lambda g: (g, 0))] + [fixed(w.shape) for w in weights],
        [block] * 3,
        [jax.ShapeDtypeStruct((total, units), bf16)] * 3,
    )(left, *weights)


def gated_backward(left, down_pieces, act, slope):
    total, features = left.shape
    rows = total // 4
    pieces = len(down_pieces)
    size = features // pieces
    units = down_pieces[0].shape[0]

    def kernel(*refs):
        left_ref = refs[0]
        act_ref, slope_ref, out = refs[1 + pieces :]
        grad = None
        for r in range(pieces):
            term = dot_back(left_ref[:, r * size : (r + 1) * size], refs[1 + r][...])
            grad = term if grad is None else grad + term
        out[:, :units] = (grad * slope_ref[...].astype(f32)).astype(bf16)
        out[:, units:] = (grad * act_ref[...].astype(f32)).astype(bf16)

    block = pl.BlockSpec((rows, units), lambda g: (g, 0))
    return call(
        kernel,
        "gated_backward",
        (4,),
        [pl.BlockSpec((rows, features), lambda g: (g, 0))]
        + [fixed(w.shape) for w in down_pieces]
        + [block] * 2,
        pl.BlockSpec((rows, 2 * units), lambda g: (g, 0)),
        jax.ShapeDtypeStruct((total, 2 * units), bf16),
    )(left, *down_pieces, act, slope)


def weight_grads(lefts, right, pieces, by_left, name, extras=()):
    total = right.shape[0]
    terms = len(lefts)
    operands = list(lefts) + [right]
    if (lefts[0] if by_left else right).shape[1] // pieces % 128:
        return weight_grads_plain(lefts, right, pieces, by_left, extras)
    if by_left:
        (left,) = lefts
        size = left.shape[1] // pieces
        parts = len(extras) or 1
        width = right.shape[1] // parts
        more = extras[0].shape[1] if extras else 0
        shapes = [(size, width + more)] * parts
        in_specs = [pl.BlockSpec((total, size), lambda g: (0, g)), fixed(right.shape)]
        operands += extras
        in_specs += [pl.BlockSpec((size, more), lambda g: (g, 0)) for _ in extras]
    else:
        size = right.shape[1] // pieces
        parts = terms
        shapes = [(left.shape[1], size) for left in lefts]
        in_specs = [fixed(left.shape) for left in lefts] + [
            pl.BlockSpec((total, size), lambda g: (0, g))
        ]

    def kernel(*refs):
        outs = refs[len(operands) : len(operands) + parts * pieces]
        results = refs[len(operands) + parts * pieces :]
        for i in range(parts):
            if by_left:
                value = dot_rows(refs[0][...], refs[1][:, i * width : (i + 1) * width])
                results[i][:, :width] = value.astype(bf16)
                if extras:
                    results[i][:, width:] = refs[2 + i][...]
            else:
                results[i][...] = dot_rows(refs[i][...], refs[terms][...]).astype(bf16)
        for r in range(pieces):

            @pl.when(pl.program_id(0) == r)
            def _():
                for i in range(parts):
                    outs[i * pieces + r][...] = results[i][...]

    out = call(
        kernel,
        name,
        (pieces,),
        in_specs,
        [fixed(shape) for shape in shapes for _ in range(pieces)],
        [jax.ShapeDtypeStruct(shape, bf16) for shape in shapes for _ in range(pieces)],
        [pltpu.VMEM(shape, bf16) for shape in shapes],
    )(*operands)
    return [out[i * pieces : (i + 1) * pieces] for i in range(parts)]


def weight_grads_plain(lefts, right, pieces, by_left, extras):
    if not by_left:
        wholes = [dot_rows(left, right).astype(bf16) for left in lefts]
        return [jnp.split(whole, pieces, axis=1) for whole in wholes]
    wholes = jnp.split(dot_rows(lefts[0], right).astype(bf16), len(extras) or 1, axis=1)
    if extras:
        wholes = [jnp.concatenate(pair, axis=1) for pair in zip(wholes, extras)]
    return [jnp.split(whole, pieces, axis=0) for whole in wholes]


def one_hot(rows, columns, hit):
    row = lax.broadcasted_iota(jnp.int32, (rows, columns), 0)
    column = lax.broadcasted_iota(jnp.int32, (rows, columns), 1)
    return jnp.where(hit(row, column), 1.0, 0.0).astype(bf16)


def table_movers(width, shard, piece, block_width):
    table_rows = width // block_width * piece
    return [
        one_hot(
            width,
            shard,
            lambda c, row, k=k: row == k * table_rows + c // block_width * piece + c % piece,
        )
        for k in range(3)
    ]


def unpack_tables(blocks, order, width, piece, block_width):
    count = len(blocks)
    shard = blocks[0].shape[0]
    table_rows = width // block_width * piece

    def kernel(order_ref, *refs):
        flat = refs[:count]
        gates, small, gains, kept = refs[count:]
        owner = lax.broadcasted_iota(jnp.int32, (width, 256), 0) % block_width // piece
        movers = table_movers(width, shard, piece, block_width)
        picks = one_hot(8, shard, lambda row, column: column == 3 * table_rows + row)
        for r in range(count):
            table = flat[r][...]
            mine = owner == order_ref[r]
            for k in range(3):
                value = dot(movers[k], table)
                if r == 0:
                    kept[k] = jnp.where(mine, value, 0.0)
                else:
                    kept[k] = jnp.where(mine, value, kept[k])
            rows = dot(picks, table)
            gains[:, r * shard : (r + 1) * shard] = rows[:, :shard]
        spreader = one_hot(256, width, lambda row, column: row == column % block_width)
        same = lax.broadcasted_iota(jnp.int32, (width, width), 0) // block_width == (
            lax.broadcasted_iota(jnp.int32, (width, width), 1) // block_width
        )
        for k in range(2):
            value = dot(kept[k].astype(bf16), spreader)
            gates[:, k * width : (k + 1) * width] = jnp.where(same, value, 0.0).astype(bf16)
        picker = one_hot(8, 256, lambda row, column: row == column)
        small[...] = dot_back(picker, kept[2].astype(bf16))

    return pl.pallas_call(
        kernel,
        grid_spec=pltpu.PrefetchScalarGridSpec(
            num_scalar_prefetch=1,
            grid=(1,),
            in_specs=[fixed((shard, 256))] * count,
            out_specs=[
                fixed((width, 2 * width)),
                fixed((8, width)),
                fixed((8, count * shard)),
            ],
            scratch_shapes=[pltpu.VMEM((3, width, 256), f32)],
        ),
        out_shape=[
            jax.ShapeDtypeStruct((width, 2 * width), bf16),
            jax.ShapeDtypeStruct((8, width), f32),
            jax.ShapeDtypeStruct((8, count * shard), f32),
        ],
        compiler_params=pltpu.CompilerParams(vmem_limit_bytes=vmem_bytes),
        cost_estimate=light,
        name="unpack_tables",
    )(order, *blocks)


def pack_tables(gate_grads, small_grads, order, count, shard, piece, block_width):
    width = gate_grads.shape[0]

    def kernel(order_ref, gate_ref, small_ref, out):
        spreader = one_hot(256, width, lambda row, column: row == column % block_width)
        same = lax.broadcasted_iota(jnp.int32, (width, width), 0) // block_width == (
            lax.broadcasted_iota(jnp.int32, (width, width), 1) // block_width
        )
        folded = [
            dot_back(
                jnp.where(same, gate_ref[:, k * width : (k + 1) * width], 0.0).astype(bf16),
                spreader,
            )
            for k in range(2)
        ]
        picker = one_hot(8, 256, lambda row, column: row == column)
        folded.append(dot_rows(small_ref[...].astype(bf16), picker))
        owner = lax.broadcasted_iota(jnp.int32, (width, 256), 0) % block_width // piece
        movers = table_movers(width, shard, piece, block_width)
        for r in range(count):
            total = None
            for k in range(3):
                mine = jnp.where(owner == order_ref[r], folded[k], 0.0).astype(bf16)
                term = dot_rows(movers[k], mine)
                total = term if total is None else total + term
            at = slice(r * shard, (r + 1) * shard)
            out[at, :] = total.astype(bf16)

    shape = (count * shard, 256)
    return pl.pallas_call(
        kernel,
        grid_spec=pltpu.PrefetchScalarGridSpec(
            num_scalar_prefetch=1,
            grid=(1,),
            in_specs=[fixed(gate_grads.shape), fixed(small_grads.shape)],
            out_specs=fixed(shape),
        ),
        out_shape=jax.ShapeDtypeStruct(shape, bf16),
        compiler_params=pltpu.CompilerParams(vmem_limit_bytes=vmem_bytes),
        cost_estimate=light,
        name="pack_tables",
    )(order, gate_grads, small_grads)


def prepare(whole, order, place, size, gain):
    total, features = whole.shape
    rows = total // 4
    groups = features // size

    def kernel(order_ref, place_ref, value_ref, gain_ref, out, own):
        j = pl.program_id(0)

        def step(c, carry):
            at = pl.ds(pl.multiple_of(c * 16, 16), 16)
            value = value_ref[at, :].astype(f32)
            scale = lax.rsqrt(jnp.mean(value * value, axis=1, keepdims=True) + epsilon)
            for r in range(groups):
                to = slice(r * size, (r + 1) * size)
                start = pl.multiple_of(order_ref[r] * size, size)
                part = value_ref[at, pl.ds(start, size)].astype(f32)
                out[at, to] = (part * scale * gain_ref[:, to]).astype(bf16)
            return carry

        lax.fori_loop(0, rows // 16, step, 0, unroll=2)

        @pl.when(j == place_ref[0])
        def _():
            for r in range(groups):
                start = pl.multiple_of(order_ref[r] * size, size)
                own[:, r * size : (r + 1) * size] = value_ref[:, pl.ds(start, size)]

    block = pl.BlockSpec((rows, features), lambda g, *_: (g, 0))
    return pl.pallas_call(
        kernel,
        grid_spec=pltpu.PrefetchScalarGridSpec(
            num_scalar_prefetch=2,
            grid=(4,),
            in_specs=[block, fixed((1, features))],
            out_specs=[block, fixed((rows, features))],
        ),
        out_shape=[
            jax.ShapeDtypeStruct((total, features), bf16),
            jax.ShapeDtypeStruct((rows, features), bf16),
        ],
        compiler_params=pltpu.CompilerParams(vmem_limit_bytes=vmem_bytes),
        cost_estimate=light,
        name="prepare",
    )(order, place, whole, gain.reshape(1, features))


def move_columns(blocks, order, size):
    rows, features = blocks[0].shape
    groups = features // size

    def kernel(order_ref, *refs):
        out = refs[-1]
        for r in range(groups):
            start = pl.multiple_of(order_ref[r] * size, size)
            for j, ref in enumerate(refs[:-1]):
                out[j * rows : (j + 1) * rows, r * size : (r + 1) * size] = ref[
                    :, pl.ds(start, size)
                ]

    return pl.pallas_call(
        kernel,
        grid_spec=pltpu.PrefetchScalarGridSpec(
            num_scalar_prefetch=1,
            grid=(1,),
            in_specs=[fixed((rows, features))] * len(blocks),
            out_specs=fixed((rows * len(blocks), features)),
        ),
        out_shape=jax.ShapeDtypeStruct((rows * len(blocks), features), blocks[0].dtype),
        compiler_params=pltpu.CompilerParams(vmem_limit_bytes=vmem_bytes),
        cost_estimate=light,
        name="move_columns",
    )(order, *blocks)


class Ring:
    def __init__(self, count):
        self.count = count
        order = list(range(0, count, 2)) + list(range(1, count, 2))[::-1]
        self.order = order
        self.place_of = [order.index(index) for index in range(count)]
        ahead = [(order[(i + 1) % count], order[i]) for i in range(count)]
        behind = [(order[i], order[(i + 1) % count]) for i in range(count)]
        self.pairs = (ahead, behind)
        index = lax.axis_index("dp")
        half = (count + 1) // 2
        self.place = jnp.where(
            lax.rem(index, 2) == 0, lax.div(index, 2), count - 1 - lax.div(index, 2)
        ).astype(jnp.int32)
        spots = lax.rem(jnp.arange(count, dtype=jnp.int32) + self.place, count)
        self.block_of = jnp.where(spots < half, 2 * spots, 2 * (count - 1 - spots) + 1)
        self.step_of = self.steps_to(jnp.arange(count, dtype=jnp.int32))

    def steps_to(self, index):
        places = jnp.where(index % 2 == 0, index // 2, self.count - 1 - index // 2)
        return (places - self.place + self.count) % self.count

    def normal_in(self, rows, place, size, gain):
        if size % 128 == 0:
            return prepare(rows, self.block_of, place, size, gain)
        whole = self.columns_in([rows], size)
        value = whole.astype(f32)
        scale = lax.rsqrt(jnp.mean(value * value, axis=1, keepdims=True) + epsilon)
        own = whole.shape[0] // 4
        return (value * scale * gain).astype(bf16), lax.dynamic_slice_in_dim(
            whole, place[0] * own, own, axis=0
        )

    def columns_in(self, blocks, size):
        if size % 128 == 0:
            return move_columns(blocks, self.block_of, size)
        whole = jnp.concatenate(blocks, axis=0)
        ordered = [whole[:, i * size : (i + 1) * size] for i in self.order]
        return lax.dynamic_slice_in_dim(
            jnp.concatenate(ordered + ordered, axis=1),
            self.place * size,
            self.count * size,
            axis=1,
        )

    def columns_out(self, whole, size):
        if size % 128 == 0:
            return move_columns([whole], self.step_of, size)
        start = lax.rem(self.count - self.place, self.count) * size
        ordered = lax.dynamic_slice_in_dim(
            jnp.concatenate([whole, whole], axis=1), start, self.count * size, axis=1
        )
        return jnp.concatenate(
            [ordered[:, i * size : (i + 1) * size] for i in self.place_of], axis=1
        )


class Gather:
    work = 0.0

    def __init__(self, ring, own, far, axis):
        count = ring.count
        reach = count // 2 if far else (count - 1) // 2
        self.total = count
        self.hops = (reach, count - 1 - reach)
        self.left = count - 1
        self.blocks = [own] + [None] * (count - 1)
        self.axis = axis

    def receive(self, way, hop, value):
        self.blocks[hop + 1 if way == 0 else self.total - 1 - hop] = value
        self.left -= 1

    def operand(self, way, hop, gate):
        return self.blocks[hop if way == 0 else (self.total - hop) % self.total]

    def pieces(self):
        if self.blocks[0].shape[self.axis] % 128 == 0:
            return self.blocks
        return [jnp.concatenate(self.blocks, axis=self.axis)]


class Scatter:
    work = 2.0

    def __init__(self, ring, part, far):
        count = ring.count
        reach = count // 2 if far else (count - 1) // 2
        self.total = count
        self.hops = (count - 1 - reach, reach)
        self.left = count - 1
        self.part = part
        self.got = [None, None]

    def receive(self, way, hop, value):
        self.got[way] = value
        self.left -= 1

    def operand(self, way, hop, gate):
        distance = self.hops[way] - hop
        value = self.part[distance if way == 1 else self.total - distance]
        if hop:
            (got,) = gate(self.got[way])
            value = (value.astype(f32) + got.astype(f32)).astype(bf16)
        return value

    def result(self, gate):
        got = gate(*self.got)
        return self.part[0].astype(f32) + got[0].astype(f32) + got[1].astype(f32)


class Lanes:
    def __init__(self, ring, depth):
        self.ring = ring
        self.depth = depth
        self.queue = ([], [])
        self.flying = ([], [])
        self.link = [0.0, 0.0]
        self.now = 0.0
        self.marks = []

    def gate(self, *values):
        if not self.marks:
            return values
        return lax.optimization_barrier(tuple(values) + tuple(self.marks))[: len(values)]

    def mark(self, *values):
        self.marks = list(values)

    def add(self, *chains):
        for chain in chains:
            for way in range(2):
                if chain.hops[way]:
                    self.queue[way].append(chain)
        self.fill()

    def start(self, way, chain, hop):
        (operand,) = self.gate(chain.operand(way, hop, self.gate))
        self.mark(operand)
        self.now += chain.work + 2.0
        value = lax.ppermute(operand, "dp", self.ring.pairs[way])
        begin = max(self.now, self.link[way])
        self.link[way] = begin + operand.size / 22000.0
        self.flying[way].append((self.link[way] + 3.0, chain, hop, value))

    def fill(self):
        for way in range(2):
            while self.queue[way] and len(self.flying[way]) < self.depth:
                self.start(way, self.queue[way].pop(0), 0)

    def step(self, limit):
        heads = [(self.flying[way][0][0], way) for way in range(2) if self.flying[way]]
        if not heads or min(heads)[0] > limit:
            return False
        finish, way = min(heads)
        _, chain, hop, value = self.flying[way].pop(0)
        self.now = max(self.now, finish)
        chain.receive(way, hop, value)
        if hop + 1 < chain.hops[way]:
            self.start(way, chain, hop + 1)
        else:
            self.mark(value, *self.marks)
        self.fill()
        return True

    def catch_up(self, time=None):
        time = self.now if time is None else time
        while self.step(time):
            time = max(time, self.now)
        self.now = max(self.now, time)

    def serve(self, times):
        for _ in range(2 * times):
            self.step(float("inf"))

    def until(self, *chains):
        while any(chain.left for chain in chains):
            assert self.step(float("inf"))

    def did(self, time, *values):
        self.mark(*values)
        self.now += time
        self.catch_up()


core_pairs = [(0, 1), (1, 0), (2, 3), (3, 2)]
chip_pairs = [(0, 2), (1, 3), (2, 0), (3, 1)]


def tensor_gather(own):
    return lax.all_gather(own, "tensor", axis=0, tiled=True)


def tensor_reduce(whole):
    return lax.psum_scatter(whole, "tensor", scatter_dimension=0, tiled=True)


def tensor_scatter(blocks):
    own, sibling, across, far = blocks
    far = lax.ppermute(far, "tensor", core_pairs)
    sibling, far = lax.optimization_barrier((sibling, far))
    sibling = lax.ppermute(sibling, "tensor", core_pairs)
    across = (across.astype(f32) + far.astype(f32)).astype(bf16)
    across, sibling = lax.optimization_barrier((across, sibling))
    return own, sibling, across, lax.ppermute(across, "tensor", chip_pairs)


def summed(parts):
    own, sibling, _, across = parts
    return own.astype(f32) + sibling.astype(f32) + across.astype(f32)


def tensor_sum(value):
    value = value + lax.ppermute(value, "tensor", core_pairs)
    return value + lax.ppermute(value, "tensor", chip_pairs)


def row_scale(values):
    return lax.rsqrt(jnp.mean(values * values, axis=-1, keepdims=True) + epsilon)


def norm_backward(values, scale, gain, grad):
    weighted = grad * gain
    inner = jnp.mean(weighted * values, axis=-1, keepdims=True)
    return scale * weighted - values * (scale * scale * scale * inner)


def body(
    inputs,
    segment_ids,
    gain_mixer,
    branch_weight,
    input_weight,
    conv_weight,
    conv_bias,
    rate_weight,
    rate_bias,
    entry_weight,
    entry_bias,
    decay_param,
    output_weight,
    gain_mlp,
    gate_weight,
    up_weight,
    down_weight,
    cotangent,
    *,
    dp,
    tensor,
):
    ring = Ring(dp)
    lanes = Lanes(ring, 2)
    shard, width = branch_weight.shape
    features = inputs.shape[1]
    length = segment_ids.shape[0]
    gate_blocks, piece, block_width = rate_weight.shape
    taps = conv_weight.shape[0]
    units = gate_weight.shape[1]
    place = lax.axis_index("tensor").astype(jnp.int32).reshape(1)

    table_rows = gate_blocks * piece
    wide = 256
    columns = jnp.stack(
        [conv_weight[k] for k in range(taps)] + [conv_bias, rate_bias, entry_bias, decay_param],
        axis=-1,
    )

    def padded(rows):
        return jnp.pad(rows, ((0, 0), (0, wide - rows.shape[1])))

    table = jnp.concatenate(
        [
            padded(rate_weight.reshape(table_rows, block_width)),
            padded(entry_weight.reshape(table_rows, block_width)),
            padded(columns.reshape(table_rows, taps + 4)),
            padded(jnp.stack([gain_mixer, gain_mlp])),
        ],
        axis=0,
    )
    table = jnp.pad(table, ((0, shard - 3 * table_rows - 2), (0, 0)))

    masks = []
    for offset in range(1, taps):
        earlier = jnp.concatenate(
            [jnp.full((offset,), -1, segment_ids.dtype), segment_ids[: length - offset]]
        )
        masks.append((earlier == segment_ids).astype(f32))
    masks = jnp.stack([masks[0]] + masks, axis=1)
    masks = jnp.pad(masks, ((0, 0), (0, 128 - taps)))

    half = units // 2
    halves = (slice(0, half), slice(half, units))
    table_chain = Gather(ring, table, False, 0)
    pair_chains = [Gather(ring, branch_weight, True, 0), Gather(ring, input_weight, False, 0)]
    output_chain = Gather(ring, output_weight, True, 1)
    gated_chains = [
        Gather(
            ring,
            jnp.concatenate([gate_weight[:, at], up_weight[:, at]], axis=1),
            at.start == 0,
            0,
        )
        for at in halves
    ]
    down_chains = [Gather(ring, down_weight[at], at.start == 0, 1) for at in halves]
    lanes.now = 10.0
    input_rows = tensor_gather(inputs)
    lanes.add(pair_chains[0], table_chain, pair_chains[1], output_chain, *gated_chains, *down_chains)
    cotangent_rows = tensor_gather(cotangent)

    lanes.until(table_chain)
    gates, small, gains = unpack_tables(
        lanes.gate(*table_chain.blocks),
        ring.block_of,
        width,
        piece,
        block_width,
    )
    gain_one, gain_two = gains[0], gains[1]
    decay_full = small[7:8]
    small = jnp.concatenate([small[:7], -lru_scale * jax.nn.softplus(-decay_full)], axis=0)
    mixer_rows, tokens_low = ring.normal_in(input_rows, place, shard, gain_one)
    lanes.did(18.0, mixer_rows)
    lanes.until(*pair_chains)
    (mixer_rows,) = lanes.gate(mixer_rows)

    rows = inputs.shape[0]
    start = jnp.zeros((1,), jnp.int32)
    pair_weights = [chain.pieces() for chain in pair_chains]
    pre = collect(mixer_rows, pair_weights, width, False, "mixer_in")
    lanes.did(12.0, pre)
    (pre,) = lanes.gate(pre)
    mixer_low, mixed, rate, entry, state = core_forward(start, pre, masks, gates, small, tensor)
    lanes.did(21.0, mixer_low)
    lanes.until(output_chain)
    output_pieces = output_chain.pieces()
    (mixer_low,) = lanes.gate(mixer_low)
    mixer_out = spread([(mixer_low, 0, width)], [output_pieces], place, (), False, "mixer_out")
    lanes.did(9.0, mixer_out)
    mixer_sum = tensor_reduce(mixer_out)
    arrival = lanes.now + 46.0
    (cotangent_rows,) = lanes.gate(cotangent_rows)
    cotangent_rows = ring.columns_in([cotangent_rows], shard)
    lanes.did(5.0, cotangent_rows)
    lanes.catch_up(arrival)
    (mixer_sum,) = lanes.gate(mixer_sum)
    tokens = tokens_low.astype(f32)
    middle = tokens + mixer_sum.astype(f32)
    scale_two = row_scale(middle)
    mlp_own = (middle * scale_two * gain_two).astype(bf16)
    lanes.did(5.0, mlp_own)
    mlp_rows = tensor_gather(mlp_own)
    lanes.catch_up(lanes.now + 34.0)
    (mlp_rows,) = lanes.gate(mlp_rows)

    def columns_of(array, r):
        return lax.slice_in_dim(array, r * shard, (r + 1) * shard, axis=1)

    hidden, acts, slopes = [], [], []
    for h in range(2):
        lanes.until(gated_chains[h])
        (gated,) = lanes.gate(mlp_rows)
        one, two, three = gated_forward(gated, gated_chains[h].pieces())
        hidden.append(one)
        acts.append(two)
        slopes.append(three)
        lanes.did(13.5, one)
    lefts = lanes.gate(*hidden)
    down_scatters = [
        Scatter(ring, part, h == 1)
        for h, part in enumerate(weight_grads(lefts, cotangent_rows, dp, False, "down_grads"))
    ]
    lanes.did(13.5, down_scatters[0].part[0])
    lanes.add(*down_scatters)
    gated_lows, gated_scatters = [], []

    def gated_back(h):
        lanes.until(down_chains[h])
        (gated,) = lanes.gate(cotangent_rows)
        gated_lows.append(gated_backward(gated, down_chains[h].pieces(), acts[h], slopes[h]))
        lanes.did(8.5, gated_lows[h])

    def gated_grads(h):
        (gated,) = lanes.gate(gated_lows[h])
        (part,) = weight_grads([mlp_rows], gated, dp, True, "gated_grads")
        gated_scatters.append(Scatter(ring, part, h == 0))
        lanes.did(14.0, part[0])
        lanes.add(gated_scatters[h])

    gated_back(0)
    gated_back(1)
    mlp_in_grad = None
    for h in range(2):
        (gated,) = lanes.gate(gated_lows[h])
        mlp_in_grad = spread(
            [(gated, 0, 2 * half)],
            [gated_chains[h].pieces()],
            place,
            (),
            True,
            "mlp_in_grad",
            mlp_in_grad,
        )
        lanes.did(11.0, mlp_in_grad)
    mlp_in_grad = tensor_reduce(mlp_in_grad)
    arrival = lanes.now + 46.0
    gated_grads(0)
    gated_grads(1)
    lanes.catch_up(arrival)
    (mlp_in_grad,) = lanes.gate(mlp_in_grad)
    middle_norm_grad = norm_backward(middle, scale_two, gain_two, mlp_in_grad.astype(f32))
    middle_grad = (
        lax.dynamic_slice_in_dim(cotangent_rows, place[0] * rows, rows, axis=0).astype(f32)
        + middle_norm_grad
    )
    residual_own = middle_grad.astype(bf16)
    lanes.did(6.0, residual_own)
    residual_rows = tensor_gather(residual_own)
    arrival = lanes.now + 34.0
    late = [(low, 0, half) for low in lanes.gate(*hidden)]
    mlp_out = spread(
        late, [chain.pieces() for chain in down_chains], place, (), False, "mlp_out"
    )
    lanes.did(13.0, mlp_out)
    lanes.catch_up(arrival)
    mlp_out, residual_rows = lanes.gate(mlp_out, residual_rows)
    mlp_sum = tensor_reduce(mlp_out)

    state_grad, branch_low = mixer_back(residual_rows, output_pieces, pre, state)
    lanes.did(10.5, state_grad)
    (state_grad,) = lanes.gate(state_grad)
    entry_low, gate_grads, small_grads = core_backward(
        start, state_grad, pre, mixed, rate, entry, state, masks, gates, small, tensor
    )
    lanes.did(23.0, entry_low)
    (residual_rows,) = lanes.gate(residual_rows)
    (part,) = weight_grads([mixer_low], residual_rows, dp, False, "output_grads")
    output_scatter = Scatter(ring, part, True)
    lanes.did(9.5, part[0])
    lanes.add(output_scatter)
    (low,) = lanes.gate(branch_low)
    (part,) = weight_grads([mixer_rows], low, dp, True, "branch_grads")
    pair_scatters = [Scatter(ring, part, False)]
    lanes.did(8.0, part[0])
    lanes.add(pair_scatters[0])
    decay_grad = lru_scale * small_grads[7:8] * jax.nn.sigmoid(-decay_full)
    small_grads = jnp.concatenate([small_grads[:7], decay_grad], axis=0)
    (gate_grads,) = lanes.gate(gate_grads)
    grad_tables = pack_tables(
        gate_grads, small_grads, ring.block_of, dp, shard, piece, block_width
    )
    lanes.did(7.5, grad_tables)
    (low,) = lanes.gate(entry_low)
    (part,) = weight_grads([mixer_rows], low, dp, True, "input_grads", (grad_tables,))
    pair_scatters.append(Scatter(ring, part, True))
    lanes.did(9.0, part[0])
    lanes.add(pair_scatters[1])
    branch_late, entry_late = lanes.gate(branch_low, entry_low)
    mixer_in_grad = spread(
        [(branch_late, 0, width), (entry_late, 0, width)],
        pair_weights,
        place,
        (),
        True,
        "mixer_in_grad",
    )
    lanes.did(11.5, mixer_in_grad)
    mixer_in_grad = tensor_reduce(mixer_in_grad)
    arrival = lanes.now + 30.0

    (mlp_sum,) = lanes.gate(mlp_sum)
    layer_out = ring.columns_out((middle + mlp_sum.astype(f32)).astype(bf16), shard)
    lanes.did(6.0, layer_out)
    lanes.catch_up(arrival)
    (mixer_in_grad,) = lanes.gate(mixer_in_grad)
    tokens_norm_grad = norm_backward(
        tokens, row_scale(tokens), gain_one, mixer_in_grad.astype(f32)
    )
    inputs_grad = ring.columns_out((middle_grad + tokens_norm_grad).astype(bf16), shard)
    lanes.did(9.0, inputs_grad)
    lanes.until(*down_scatters, *gated_scatters, output_scatter, *pair_scatters)

    free = lambda *values: values
    pair_wgrads = [scatter.result(free) for scatter in pair_scatters]
    table_grad = pair_wgrads[1][:, width:]
    pair_wgrads = [wgrad[:, :width] for wgrad in pair_wgrads]
    rate_wgrad, entry_wgrad, column_grads = [
        table_grad[k * table_rows : (k + 1) * table_rows].reshape(gate_blocks, piece, wide)
        for k in range(3)
    ]
    rate_wgrad = rate_wgrad[:, :, :block_width]
    entry_wgrad = entry_wgrad[:, :, :block_width]
    singles = [column_grads[:, :, k] for k in range(taps + 4)]
    gated_wgrads = [scatter.result(free) for scatter in gated_scatters]

    def gain_grad(gain, own_weights, wgrads):
        total = sum(
            jnp.sum(weight[:, : wgrad.shape[1]].astype(f32) * wgrad, axis=1)
            for weight, wgrad in zip(own_weights, wgrads)
        )
        return total / gain.astype(f32)

    gain_grads = tensor_sum(
        jnp.stack(
            [
                gain_grad(
                    gain_mixer,
                    [branch_weight, input_weight],
                    pair_wgrads,
                ),
                gain_grad(gain_mlp, [chain.blocks[0] for chain in gated_chains], gated_wgrads),
            ]
        )
    )
    return (
        layer_out,
        inputs_grad,
        gain_grads[0],
        *pair_wgrads,
        jnp.stack(singles[:taps]),
        singles[taps],
        rate_wgrad,
        singles[taps + 1],
        entry_wgrad,
        singles[taps + 2],
        singles[taps + 3],
        output_scatter.result(free),
        gain_grads[1],
        jnp.concatenate([wgrad[:, :half] for wgrad in gated_wgrads], axis=1),
        jnp.concatenate([wgrad[:, half:] for wgrad in gated_wgrads], axis=1),
        jnp.concatenate([scatter.result(free) for scatter in down_scatters], axis=0),
    )


def solution(mesh):
    return jax.shard_map(
        functools.partial(body, dp=mesh.shape["dp"], tensor=mesh.shape["tensor"]),
        mesh=mesh,
        in_specs=(
            P(("dp", "tensor"), None),
            P("dp"),
            P("dp"),
            P("dp", "tensor"),
            P("dp", "tensor"),
            P(None, "tensor", "dp"),
            P("tensor", "dp"),
            P("tensor", "dp", None),
            P("tensor", "dp"),
            P("tensor", "dp", None),
            P("tensor", "dp"),
            P("tensor", "dp"),
            P("tensor", "dp"),
            P("dp"),
            P("dp", "tensor"),
            P("dp", "tensor"),
            P("tensor", "dp"),
            P(("dp", "tensor"), None),
        ),
        out_specs=(
            P(("dp", "tensor"), None),
            P(("dp", "tensor"), None),
            P("dp"),
            P("dp", "tensor"),
            P("dp", "tensor"),
            P(None, "tensor", "dp"),
            P("tensor", "dp"),
            P("tensor", "dp", None),
            P("tensor", "dp"),
            P("tensor", "dp", None),
            P("tensor", "dp"),
            P("tensor", "dp"),
            P("tensor", "dp"),
            P("dp"),
            P("dp", "tensor"),
            P("dp", "tensor"),
            P("tensor", "dp"),
        ),
        check_vma=False,
    )
```

```python
import functools

import jax
import jax.numpy as jnp
from jax import lax
from jax.experimental import pallas as pl
from jax.experimental.pallas import tpu as pltpu
from jax.sharding import PartitionSpec as P

epsilon = 1e-06
lru_scale = 8.0
root = 0.7978845608028654
cubic = 0.044715
f32 = jnp.float32
bf16 = jnp.bfloat16
vmem_bytes = 56 * 1024 * 1024
light = pl.CostEstimate(flops=6_000_000_000, bytes_accessed=30_000_000, transcendentals=0)


def gelu_both(value):
    square = value * value
    th = jnp.tanh(root * value * (1.0 + cubic * square))
    half = 0.5 * (1.0 + th)
    slope = half + 0.5 * value * (1.0 - th * th) * (root * (1.0 + 3.0 * cubic * square))
    return value * half, slope


def gelu(value):
    return value * (0.5 * (1.0 + jnp.tanh(root * value * (1.0 + cubic * value * value))))


def one_minus_exp(x, exp_x):
    series = 1.0 + x * (1.0 / 7.0)
    for order in (6.0, 5.0, 4.0, 3.0, 2.0):
        series = 1.0 + x * (1.0 / order) * series
    return jnp.where(x > -0.5, -x * series, 1.0 - exp_x)


def decay_terms(rate, slope, keep):
    log_decay = slope * rate
    expo = jnp.exp(log_decay)
    square = expo * expo
    factor = jnp.where(keep > 0.0, jnp.sqrt(one_minus_exp(2.0 * log_decay, square)), 1.0)
    return expo * keep, square, factor


def row_index(width):
    return lax.broadcasted_iota(jnp.int32, (8, width), 0)


def down_by(current, before, offset, rows):
    if offset == 0:
        return current
    return jnp.where(
        rows < offset, pltpu.roll(before, offset, 0), pltpu.roll(current, offset, 0)
    )


def up_by(current, after, offset, rows):
    if offset == 0:
        return current
    return jnp.where(
        rows < 8 - offset,
        pltpu.roll(current, 8 - offset, 0),
        pltpu.roll(after, 8 - offset, 0),
    )


def core_forward_kernel(
    place, branch, entry_pre, masks, gates, small, out, mixed_out, rate_out, entry_out, state_out,
    mixed_low, pre, last_entry, last_state,
):
    length, width = entry_pre.shape
    rows = row_index(width)

    @pl.when(pl.program_id(0) == 0)
    def _():
        last_entry[...] = jnp.zeros_like(last_entry)
        last_state[...] = jnp.zeros_like(last_state)

    taps = [small[k : k + 1, :] for k in range(4)]
    conv_bias = small[4:5, :]

    def convolve(step, before):
        parts = []
        for half in range(2):
            at = pl.ds(pl.multiple_of(step * 16 + half * 8, 8), 8)
            here = entry_pre[at, :]
            mask = masks[at, :]
            mixed = here * taps[0] + conv_bias
            for k in range(1, 4):
                mixed += down_by(here, before, k, rows) * mask[:, k : k + 1] * taps[k]
            mixed_out[at, :] = mixed
            parts.append(mixed)
            before = here
        mixed_low[pl.ds(pl.multiple_of(step * 16, 16), 16), :] = jnp.concatenate(
            parts, axis=0
        ).astype(bf16)
        return before

    last_entry[...] = lax.fori_loop(0, length // 16, convolve, last_entry[...], unroll=8)
    pre[...] = jnp.dot(mixed_low[...], gates[...], preferred_element_type=f32)
    rate_bias = small[5:6, :]
    entry_bias = small[6:7, :]
    slope = small[7:8, :]

    def scan(step, carry):
        parts = []
        for half in range(2):
            at = pl.ds(pl.multiple_of(step * 16 + half * 8, 8), 8)
            keep = masks[at, :][:, 0:1]
            rate = jax.nn.sigmoid(pre[at, :width] + rate_bias)
            entry = jax.nn.sigmoid(pre[at, width:] + entry_bias)
            decay, _, factor = decay_terms(rate, slope, keep)
            drive = factor * entry * mixed_out[at, :]
            for shift in (1, 2, 4):
                inside = rows >= shift
                drive += decay * jnp.where(inside, pltpu.roll(drive, shift, 0), 0.0)
                decay = decay * jnp.where(inside, pltpu.roll(decay, shift, 0), 1.0)
            state = drive + decay * carry
            carry = jnp.broadcast_to(state[7:8, :], state.shape)
            rate_out[at, :] = rate
            entry_out[at, :] = entry
            state_out[at, :] = state
            parts.append(gelu(branch[at, :]) * state)
        out[pl.ds(pl.multiple_of(step * 16, 16), 16), :] = jnp.concatenate(parts, axis=0).astype(
            bf16
        )
        return carry

    last_state[...] = lax.fori_loop(0, length // 16, scan, last_state[...], unroll=8)


def core_backward_kernel(
    place, grad, entry_pre, mixed_in, rate_in, entry_in, state_in, state_tail, entry_tail,
    masks, gates, small, low, gate_grads, small_grads,
    state_long, entry_long, gate_low, mixed_grad, sums, next_decay, next_carried, next_mixed,
):
    length, width = entry_pre.shape
    rows = row_index(width)

    @pl.when(pl.program_id(0) == 0)
    def _():
        next_decay[...] = jnp.zeros_like(next_decay)
        next_carried[...] = jnp.zeros_like(next_carried)
        next_mixed[...] = jnp.zeros_like(next_mixed)
        sums[...] = jnp.zeros_like(sums)
        gate_grads[...] = jnp.zeros_like(gate_grads)

    state_long[0:8, :] = state_tail[...]
    state_long[8:, :] = state_in[...]
    entry_long[0:8, :] = entry_tail[...]
    entry_long[8:, :] = entry_pre[...]
    slope = small[7:8, :]

    def reverse(step, carry):
        after_decay, carried_after = carry
        step = length // 16 - 1 - step
        rate_parts, entry_parts = [], []
        for half in (1, 0):
            start = pl.multiple_of(step * 16 + half * 8, 8)
            at = pl.ds(start, 8)
            keep = masks[at, :][:, 0:1]
            rate = rate_in[at, :]
            entry = entry_in[at, :]
            mixed = mixed_in[at, :]
            decay, square, factor = decay_terms(rate, slope, keep)
            state = state_in[at, :]
            value = grad[at, :]
            ahead = up_by(decay, after_decay, 1, rows)
            after_decay = decay
            for shift in (1, 2, 4):
                inside = rows < 8 - shift
                value += ahead * jnp.where(inside, pltpu.roll(value, 8 - shift, 0), 0.0)
                ahead = ahead * jnp.where(inside, pltpu.roll(ahead, 8 - shift, 0), 1.0)
            carried = value + ahead * carried_after
            carried_after = jnp.broadcast_to(carried[0:1, :], carried.shape)
            earlier = down_by(state, state_long[at, :], 1, rows)
            driven = carried * entry
            log_grad = keep * (carried * earlier * decay - driven * mixed * square / factor)
            scaled = log_grad * rate
            rate_pre_grad = slope * scaled * (1.0 - rate)
            entry_pre_grad = driven * factor * mixed * (1.0 - entry)
            mixed_grad[at, :] = driven * factor
            sums[40:48, :] += rate_pre_grad
            sums[48:56, :] += entry_pre_grad
            sums[56:64, :] += scaled
            rate_parts.append(rate_pre_grad)
            entry_parts.append(entry_pre_grad)
        both = pl.ds(pl.multiple_of(step * 16, 16), 16)
        gate_low[both, :width] = jnp.concatenate(rate_parts[::-1], axis=0).astype(bf16)
        gate_low[both, width:] = jnp.concatenate(entry_parts[::-1], axis=0).astype(bf16)
        return after_decay, carried_after

    after_decay, carried_after = lax.fori_loop(
        0, length // 16, reverse, (next_decay[...], next_carried[...]), unroll=8
    )
    next_decay[...] = after_decay
    next_carried[...] = carried_after
    mixed_grad[...] += lax.dot_general(
        gate_low[...], gates[...], (((1,), (1,)), ((), ())), preferred_element_type=f32
    )
    gate_grads[...] += lax.dot_general(
        mixed_in[...].astype(bf16),
        gate_low[...],
        (((0,), (0,)), ((), ())),
        preferred_element_type=f32,
    )
    taps = [small[k : k + 1, :] for k in range(4)]

    def convolve(step, after):
        step = length // 16 - 1 - step
        parts = []
        for half in (1, 0):
            start = pl.multiple_of(step * 16 + half * 8, 8)
            at = pl.ds(start, 8)
            mask = masks[at, :]
            here = mixed_grad[at, :]
            value = entry_pre[at, :]
            before = entry_long[at, :]
            sums[32:40, :] += here
            sums[0:8, :] += here * value
            total = here * taps[0]
            masked = [here * mask[:, k : k + 1] for k in range(1, 4)]
            for k in range(1, 4):
                sums[8 * k : 8 * k + 8, :] += masked[k - 1] * down_by(value, before, k, rows)
                total += up_by(masked[k - 1], after[k - 1], k, rows) * taps[k]
            after = masked
            parts.append(total)
        low[pl.ds(pl.multiple_of(step * 16, 16), 16), :] = jnp.concatenate(
            parts[::-1], axis=0
        ).astype(bf16)
        return after

    after = lax.fori_loop(
        0,
        length // 16,
        convolve,
        [next_mixed[8 * k : 8 * k + 8, :] for k in range(3)],
        unroll=8,
    )
    for k in range(3):
        next_mixed[8 * k : 8 * k + 8, :] = after[k]

    @pl.when(pl.program_id(0) == pl.num_programs(0) - 1)
    def _():
        for k in range(8):
            small_grads[k : k + 1, :] = jnp.sum(sums[8 * k : 8 * k + 8, :], axis=0, keepdims=True)


def core_forward(place, pre, masks, gates, small, blocks):
    total, width = pre.shape[0], pre.shape[1] // 2
    length = total // blocks
    wide = lambda column: pl.BlockSpec((length, width), lambda b, t: (b ^ t[0], column))
    whole = lambda shape: pl.BlockSpec(shape, lambda b, t: (0, 0))
    kept = jax.ShapeDtypeStruct((total, width), f32)
    return pl.pallas_call(
        core_forward_kernel,
        grid_spec=pltpu.PrefetchScalarGridSpec(
            num_scalar_prefetch=1,
            grid=(blocks,),
            in_specs=[
                wide(0),
                wide(1),
                pl.BlockSpec((length, 128), lambda b, t: (b, 0)),
                whole(gates.shape),
                whole(small.shape),
            ],
            out_specs=[wide(0)] * 5,
            scratch_shapes=[
                pltpu.VMEM((length, width), bf16),
                pltpu.VMEM((length, 2 * width), f32),
                pltpu.VMEM((8, width), f32),
                pltpu.VMEM((8, width), f32),
            ],
        ),
        out_shape=[jax.ShapeDtypeStruct((total, width), bf16)] + [kept] * 4,
        compiler_params=pltpu.CompilerParams(vmem_limit_bytes=vmem_bytes),
        cost_estimate=light,
        name="core_forward",
    )(place, pre, pre, masks, gates, small)


def core_backward(place, grad, pre, mixed, rate, entry, state, masks, gates, small, blocks):
    total, width = grad.shape
    length = total // blocks
    back = lambda g: blocks - 1 - g
    wide = lambda column: pl.BlockSpec((length, width), lambda g, t: (back(g) ^ t[0], column))
    whole = lambda shape: pl.BlockSpec(shape, lambda g, t: (0, 0))

    def tail(column):
        def at(g, t):
            block = jnp.maximum(back(g) - 1, 0) ^ t[0]
            return (block * (length // 8) + length // 8 - 1, column)

        return pl.BlockSpec((8, width), at)

    return pl.pallas_call(
        core_backward_kernel,
        grid_spec=pltpu.PrefetchScalarGridSpec(
            num_scalar_prefetch=1,
            grid=(blocks,),
            in_specs=[
                wide(0),
                wide(1),
                wide(0),
                wide(0),
                wide(0),
                wide(0),
                tail(0),
                tail(1),
                pl.BlockSpec((length, 128), lambda g, t: (back(g), 0)),
                whole(gates.shape),
                whole(small.shape),
            ],
            out_specs=[
                wide(0),
                whole(gates.shape),
                whole((8, width)),
            ],
            scratch_shapes=[
                pltpu.VMEM((length + 8, width), f32),
                pltpu.VMEM((length + 8, width), f32),
                pltpu.VMEM((length, 2 * width), bf16),
                pltpu.VMEM((length, width), f32),
                pltpu.VMEM((64, width), f32),
                pltpu.VMEM((8, width), f32),
                pltpu.VMEM((8, width), f32),
                pltpu.VMEM((24, width), f32),
            ],
        ),
        out_shape=[
            jax.ShapeDtypeStruct((total, width), bf16),
            jax.ShapeDtypeStruct(gates.shape, f32),
            jax.ShapeDtypeStruct((8, width), f32),
        ],
        compiler_params=pltpu.CompilerParams(vmem_limit_bytes=vmem_bytes),
        cost_estimate=light,
        name="core_backward",
    )(place, grad, pre, mixed, rate, entry, state, state, pre, masks, gates, small)


def dot(left, right):
    return jnp.dot(left, right, preferred_element_type=f32)


def dot_rows(left, right):
    return lax.dot_general(left, right, (((0,), (0,)), ((), ())), preferred_element_type=f32)


def dot_back(left, right):
    return lax.dot_general(left, right, (((1,), (1,)), ((), ())), preferred_element_type=f32)


def fixed(shape):
    zeros = (0,) * len(shape)
    return pl.BlockSpec(shape, lambda *_: zeros)


def call(kernel, name, grid, in_specs, out_specs, out_shape, scratch=()):
    return pl.pallas_call(
        kernel,
        grid=grid,
        in_specs=in_specs,
        out_specs=out_specs,
        out_shape=out_shape,
        scratch_shapes=list(scratch),
        compiler_params=pltpu.CompilerParams(vmem_limit_bytes=vmem_bytes),
        cost_estimate=light,
        name=name,
    )


def spread(lefts, weights, place, blocks, transposed, name, base=None):
    total = lefts[0][0].shape[0]
    rows = total // 4
    pieces = len(weights[0])
    product = dot_back if transposed else dot
    sizes = [w.shape[0 if transposed else 1] for w in weights[0]]
    widths = [width for _, _, width in lefts]
    features = sum(sizes)
    terms = len(lefts)
    count = len(blocks) if blocks else 4

    def kernel(place_ref, *refs):
        left = [ref[...] for ref in refs[:terms]]
        flat = refs[terms : terms + terms * pieces]
        outs = refs[terms + terms * pieces + (base is not None) :]
        result = outs[-1]
        at = 0
        for r in range(pieces):
            value = None
            for i in range(terms):
                weight = flat[i * pieces + r]
                if transposed:
                    weight = weight[:, : widths[i]]
                else:
                    weight = weight[...]
                term = product(left[i], weight)
                value = term if value is None else value + term
            if base is not None:
                value += refs[terms + terms * pieces][:, at : at + sizes[r]].astype(f32)
            result[:, at : at + sizes[r]] = value.astype(bf16)
            at += sizes[r]
        if blocks:
            for g in range(count):

                @pl.when(pl.program_id(0) == g)
                def _():
                    outs[g][...] = result[...]

    def left_spec(column, width):
        if blocks:
            first = blocks[0]
            return pl.BlockSpec((rows, width), lambda g, t: ((first - g) ^ t[0], column))
        return pl.BlockSpec((rows, width), lambda g, t: (g, column))

    if blocks:
        out_specs = [fixed((rows, features))] * count
        out_shape = [jax.ShapeDtypeStruct((rows, features), bf16)] * count
        scratch = [pltpu.VMEM((rows, features), bf16)]
    else:
        out_specs = pl.BlockSpec((rows, features), lambda g, t: (g, 0))
        out_shape = jax.ShapeDtypeStruct((total, features), bf16)
        scratch = []
    return pl.pallas_call(
        kernel,
        grid_spec=pltpu.PrefetchScalarGridSpec(
            num_scalar_prefetch=1,
            grid=(count,),
            in_specs=[left_spec(column, width) for _, column, width in lefts]
            + [fixed(w.shape) for group in weights for w in group]
            + [pl.BlockSpec((rows, features), lambda g, t: (g, 0))] * (base is not None),
            out_specs=out_specs,
            scratch_shapes=scratch,
        ),
        out_shape=out_shape,
        compiler_params=pltpu.CompilerParams(vmem_limit_bytes=vmem_bytes),
        cost_estimate=light,
        name=name,
    )(place, *[left for left, _, _ in lefts], *[w for group in weights for w in group], *([] if base is None else [base]))


def collect(left, weights, width, transposed, name):
    total, features = left.shape
    rows = total // 4
    count = len(weights)
    pieces = len(weights[0])
    product = dot_back if transposed else dot
    sizes = [w.shape[1 if transposed else 0] for w in weights[0]]

    def kernel(*refs):
        out = refs[-1]
        for i in range(count):
            at = 0
            value = None
            for r in range(pieces):
                ref = refs[1 + i * pieces + r]
                weight = ref[...] if transposed else ref[:, :width]
                term = product(refs[0][:, at : at + sizes[r]], weight)
                value = term if value is None else value + term
                at += sizes[r]
            out[:, i * width : (i + 1) * width] = value

    return call(
        kernel,
        name,
        (4,),
        [pl.BlockSpec((rows, features), lambda g: (g, 0))]
        + [fixed(w.shape) for group in weights for w in group],
        pl.BlockSpec((rows, count * width), lambda g: (g, 0)),
        jax.ShapeDtypeStruct((total, count * width), f32),
    )(left, *[w for group in weights for w in group])


def mixer_back(left, weights, pre, state):
    total, features = left.shape
    rows = total // 4
    pieces = len(weights)
    sizes = [w.shape[1] for w in weights]
    width = state.shape[1]

    def kernel(*refs):
        branch_ref, state_ref, state_grad, branch_low = refs[1 + pieces :]
        at = 0
        value = None
        for r in range(pieces):
            term = dot_back(refs[0][:, at : at + sizes[r]], refs[1 + r][...])
            value = term if value is None else value + term
            at += sizes[r]
        act, slope = gelu_both(branch_ref[...])
        state_grad[...] = value * act
        branch_low[...] = (value * state_ref[...] * slope).astype(bf16)

    block = pl.BlockSpec((rows, width), lambda g: (g, 0))
    return call(
        kernel,
        "mixer_back",
        (4,),
        [pl.BlockSpec((rows, features), lambda g: (g, 0))]
        + [fixed(w.shape) for w in weights]
        + [block] * 2,
        [block] * 2,
        [
            jax.ShapeDtypeStruct((total, width), f32),
            jax.ShapeDtypeStruct((total, width), bf16),
        ],
    )(left, *weights, pre, state)


def gated_forward(left, weights):
    total, features = left.shape
    rows = total // 4
    pieces = len(weights)
    size = features // pieces
    units = weights[0].shape[1] // 2
    step = units // 3

    def kernel(*refs):
        left_ref = refs[0]
        hidden, act_out, slope_out = refs[1 + pieces :]
        for c in range(3):
            at = slice(c * step, (c + 1) * step)
            after = slice(units + c * step, units + (c + 1) * step)
            gate = up = None
            for r in range(pieces):
                part = left_ref[:, r * size : (r + 1) * size]
                one = dot(part, refs[1 + r][:, at])
                two = dot(part, refs[1 + r][:, after])
                gate = one if gate is None else gate + one
                up = two if up is None else up + two
            act, slope = gelu_both(gate)
            hidden[:, at] = (act * up).astype(bf16)
            act_out[:, at] = act.astype(bf16)
            slope_out[:, at] = (up * slope).astype(bf16)

    block = pl.BlockSpec((rows, units), lambda g: (g, 0))
    return call(
        kernel,
        "gated_forward",
        (4,),
        [pl.BlockSpec((rows, features), lambda g: (g, 0))] + [fixed(w.shape) for w in weights],
        [block] * 3,
        [jax.ShapeDtypeStruct((total, units), bf16)] * 3,
    )(left, *weights)


def gated_backward(left, down_pieces, act, slope):
    total, features = left.shape
    rows = total // 4
    pieces = len(down_pieces)
    size = features // pieces
    units = down_pieces[0].shape[0]

    def kernel(*refs):
        left_ref = refs[0]
        act_ref, slope_ref, out = refs[1 + pieces :]
        grad = None
        for r in range(pieces):
            term = dot_back(left_ref[:, r * size : (r + 1) * size], refs[1 + r][...])
            grad = term if grad is None else grad + term
        out[:, :units] = (grad * slope_ref[...].astype(f32)).astype(bf16)
        out[:, units:] = (grad * act_ref[...].astype(f32)).astype(bf16)

    block = pl.BlockSpec((rows, units), lambda g: (g, 0))
    return call(
        kernel,
        "gated_backward",
        (4,),
        [pl.BlockSpec((rows, features), lambda g: (g, 0))]
        + [fixed(w.shape) for w in down_pieces]
        + [block] * 2,
        pl.BlockSpec((rows, 2 * units), lambda g: (g, 0)),
        jax.ShapeDtypeStruct((total, 2 * units), bf16),
    )(left, *down_pieces, act, slope)


def weight_grads(lefts, right, pieces, by_left, name, extras=()):
    total = right.shape[0]
    terms = len(lefts)
    operands = list(lefts) + [right]
    if (lefts[0] if by_left else right).shape[1] // pieces % 128:
        return weight_grads_plain(lefts, right, pieces, by_left, extras)
    if by_left:
        (left,) = lefts
        size = left.shape[1] // pieces
        parts = len(extras) or 1
        width = right.shape[1] // parts
        more = extras[0].shape[1] if extras else 0
        shapes = [(size, width + more)] * parts
        in_specs = [pl.BlockSpec((total, size), lambda g: (0, g)), fixed(right.shape)]
        operands += extras
        in_specs += [pl.BlockSpec((size, more), lambda g: (g, 0)) for _ in extras]
    else:
        size = right.shape[1] // pieces
        parts = terms
        shapes = [(left.shape[1], size) for left in lefts]
        in_specs = [fixed(left.shape) for left in lefts] + [
            pl.BlockSpec((total, size), lambda g: (0, g))
        ]

    def kernel(*refs):
        outs = refs[len(operands) : len(operands) + parts * pieces]
        results = refs[len(operands) + parts * pieces :]
        for i in range(parts):
            if by_left:
                value = dot_rows(refs[0][...], refs[1][:, i * width : (i + 1) * width])
                results[i][:, :width] = value.astype(bf16)
                if extras:
                    results[i][:, width:] = refs[2 + i][...]
            else:
                results[i][...] = dot_rows(refs[i][...], refs[terms][...]).astype(bf16)
        for r in range(pieces):

            @pl.when(pl.program_id(0) == r)
            def _():
                for i in range(parts):
                    outs[i * pieces + r][...] = results[i][...]

    out = call(
        kernel,
        name,
        (pieces,),
        in_specs,
        [fixed(shape) for shape in shapes for _ in range(pieces)],
        [jax.ShapeDtypeStruct(shape, bf16) for shape in shapes for _ in range(pieces)],
        [pltpu.VMEM(shape, bf16) for shape in shapes],
    )(*operands)
    return [out[i * pieces : (i + 1) * pieces] for i in range(parts)]


def weight_grads_plain(lefts, right, pieces, by_left, extras):
    if not by_left:
        wholes = [dot_rows(left, right).astype(bf16) for left in lefts]
        return [jnp.split(whole, pieces, axis=1) for whole in wholes]
    wholes = jnp.split(dot_rows(lefts[0], right).astype(bf16), len(extras) or 1, axis=1)
    if extras:
        wholes = [jnp.concatenate(pair, axis=1) for pair in zip(wholes, extras)]
    return [jnp.split(whole, pieces, axis=0) for whole in wholes]


def one_hot(rows, columns, hit):
    row = lax.broadcasted_iota(jnp.int32, (rows, columns), 0)
    column = lax.broadcasted_iota(jnp.int32, (rows, columns), 1)
    return jnp.where(hit(row, column), 1.0, 0.0).astype(bf16)


def table_movers(width, shard, piece, block_width):
    table_rows = width // block_width * piece
    return [
        one_hot(
            width,
            shard,
            lambda c, row, k=k: row == k * table_rows + c // block_width * piece + c % piece,
        )
        for k in range(3)
    ]


def unpack_tables(blocks, order, width, piece, block_width):
    count = len(blocks)
    shard = blocks[0].shape[0]
    table_rows = width // block_width * piece

    def kernel(order_ref, *refs):
        flat = refs[:count]
        gates, small, gains, kept = refs[count:]
        owner = lax.broadcasted_iota(jnp.int32, (width, 256), 0) % block_width // piece
        movers = table_movers(width, shard, piece, block_width)
        picks = one_hot(8, shard, lambda row, column: column == 3 * table_rows + row)
        for r in range(count):
            table = flat[r][...]
            mine = owner == order_ref[r]
            for k in range(3):
                value = dot(movers[k], table)
                if r == 0:
                    kept[k] = jnp.where(mine, value, 0.0)
                else:
                    kept[k] = jnp.where(mine, value, kept[k])
            rows = dot(picks, table)
            gains[:, r * shard : (r + 1) * shard] = rows[:, :shard]
        spreader = one_hot(256, width, lambda row, column: row == column % block_width)
        same = lax.broadcasted_iota(jnp.int32, (width, width), 0) // block_width == (
            lax.broadcasted_iota(jnp.int32, (width, width), 1) // block_width
        )
        for k in range(2):
            value = dot(kept[k].astype(bf16), spreader)
            gates[:, k * width : (k + 1) * width] = jnp.where(same, value, 0.0).astype(bf16)
        picker = one_hot(8, 256, lambda row, column: row == column)
        small[...] = dot_back(picker, kept[2].astype(bf16))

    return pl.pallas_call(
        kernel,
        grid_spec=pltpu.PrefetchScalarGridSpec(
            num_scalar_prefetch=1,
            grid=(1,),
            in_specs=[fixed((shard, 256))] * count,
            out_specs=[
                fixed((width, 2 * width)),
                fixed((8, width)),
                fixed((8, count * shard)),
            ],
            scratch_shapes=[pltpu.VMEM((3, width, 256), f32)],
        ),
        out_shape=[
            jax.ShapeDtypeStruct((width, 2 * width), bf16),
            jax.ShapeDtypeStruct((8, width), f32),
            jax.ShapeDtypeStruct((8, count * shard), f32),
        ],
        compiler_params=pltpu.CompilerParams(vmem_limit_bytes=vmem_bytes),
        cost_estimate=light,
        name="unpack_tables",
    )(order, *blocks)


def pack_tables(gate_grads, small_grads, order, count, shard, piece, block_width):
    width = gate_grads.shape[0]

    def kernel(order_ref, gate_ref, small_ref, out):
        spreader = one_hot(256, width, lambda row, column: row == column % block_width)
        same = lax.broadcasted_iota(jnp.int32, (width, width), 0) // block_width == (
            lax.broadcasted_iota(jnp.int32, (width, width), 1) // block_width
        )
        folded = [
            dot_back(
                jnp.where(same, gate_ref[:, k * width : (k + 1) * width], 0.0).astype(bf16),
                spreader,
            )
            for k in range(2)
        ]
        picker = one_hot(8, 256, lambda row, column: row == column)
        folded.append(dot_rows(small_ref[...].astype(bf16), picker))
        owner = lax.broadcasted_iota(jnp.int32, (width, 256), 0) % block_width // piece
        movers = table_movers(width, shard, piece, block_width)
        for r in range(count):
            total = None
            for k in range(3):
                mine = jnp.where(owner == order_ref[r], folded[k], 0.0).astype(bf16)
                term = dot_rows(movers[k], mine)
                total = term if total is None else total + term
            at = slice(r * shard, (r + 1) * shard)
            out[at, :] = total.astype(bf16)

    shape = (count * shard, 256)
    return pl.pallas_call(
        kernel,
        grid_spec=pltpu.PrefetchScalarGridSpec(
            num_scalar_prefetch=1,
            grid=(1,),
            in_specs=[fixed(gate_grads.shape), fixed(small_grads.shape)],
            out_specs=fixed(shape),
        ),
        out_shape=jax.ShapeDtypeStruct(shape, bf16),
        compiler_params=pltpu.CompilerParams(vmem_limit_bytes=vmem_bytes),
        cost_estimate=light,
        name="pack_tables",
    )(order, gate_grads, small_grads)


def prepare(whole, order, place, size, gain):
    total, features = whole.shape
    rows = total // 4
    groups = features // size

    def kernel(order_ref, place_ref, value_ref, gain_ref, out, own):
        j = pl.program_id(0)

        def step(c, carry):
            at = pl.ds(pl.multiple_of(c * 16, 16), 16)
            value = value_ref[at, :].astype(f32)
            scale = lax.rsqrt(jnp.mean(value * value, axis=1, keepdims=True) + epsilon)
            for r in range(groups):
                to = slice(r * size, (r + 1) * size)
                start = pl.multiple_of(order_ref[r] * size, size)
                part = value_ref[at, pl.ds(start, size)].astype(f32)
                out[at, to] = (part * scale * gain_ref[:, to]).astype(bf16)
            return carry

        lax.fori_loop(0, rows // 16, step, 0, unroll=4)

        @pl.when(j == place_ref[0])
        def _():
            for r in range(groups):
                start = pl.multiple_of(order_ref[r] * size, size)
                own[:, r * size : (r + 1) * size] = value_ref[:, pl.ds(start, size)]

    block = pl.BlockSpec((rows, features), lambda g, *_: (g, 0))
    return pl.pallas_call(
        kernel,
        grid_spec=pltpu.PrefetchScalarGridSpec(
            num_scalar_prefetch=2,
            grid=(4,),
            in_specs=[block, fixed((1, features))],
            out_specs=[block, fixed((rows, features))],
        ),
        out_shape=[
            jax.ShapeDtypeStruct((total, features), bf16),
            jax.ShapeDtypeStruct((rows, features), bf16),
        ],
        compiler_params=pltpu.CompilerParams(vmem_limit_bytes=vmem_bytes),
        cost_estimate=light,
        name="prepare",
    )(order, place, whole, gain.reshape(1, features))


def move_columns(blocks, order, size):
    rows, features = blocks[0].shape
    groups = features // size

    def kernel(order_ref, *refs):
        out = refs[-1]
        for r in range(groups):
            start = pl.multiple_of(order_ref[r] * size, size)
            for j, ref in enumerate(refs[:-1]):
                out[j * rows : (j + 1) * rows, r * size : (r + 1) * size] = ref[
                    :, pl.ds(start, size)
                ]

    return pl.pallas_call(
        kernel,
        grid_spec=pltpu.PrefetchScalarGridSpec(
            num_scalar_prefetch=1,
            grid=(1,),
            in_specs=[fixed((rows, features))] * len(blocks),
            out_specs=fixed((rows * len(blocks), features)),
        ),
        out_shape=jax.ShapeDtypeStruct((rows * len(blocks), features), blocks[0].dtype),
        compiler_params=pltpu.CompilerParams(vmem_limit_bytes=vmem_bytes),
        cost_estimate=light,
        name="move_columns",
    )(order, *blocks)


class Ring:
    def __init__(self, count):
        self.count = count
        order = list(range(0, count, 2)) + list(range(1, count, 2))[::-1]
        self.order = order
        self.place_of = [order.index(index) for index in range(count)]
        ahead = [(order[(i + 1) % count], order[i]) for i in range(count)]
        behind = [(order[i], order[(i + 1) % count]) for i in range(count)]
        self.pairs = (ahead, behind)
        index = lax.axis_index("dp")
        half = (count + 1) // 2
        self.place = jnp.where(
            lax.rem(index, 2) == 0, lax.div(index, 2), count - 1 - lax.div(index, 2)
        ).astype(jnp.int32)
        spots = lax.rem(jnp.arange(count, dtype=jnp.int32) + self.place, count)
        self.block_of = jnp.where(spots < half, 2 * spots, 2 * (count - 1 - spots) + 1)
        self.step_of = self.steps_to(jnp.arange(count, dtype=jnp.int32))

    def steps_to(self, index):
        places = jnp.where(index % 2 == 0, index // 2, self.count - 1 - index // 2)
        return (places - self.place + self.count) % self.count

    def normal_in(self, rows, place, size, gain):
        if size % 128 == 0:
            return prepare(rows, self.block_of, place, size, gain)
        whole = self.columns_in([rows], size)
        value = whole.astype(f32)
        scale = lax.rsqrt(jnp.mean(value * value, axis=1, keepdims=True) + epsilon)
        own = whole.shape[0] // 4
        return (value * scale * gain).astype(bf16), lax.dynamic_slice_in_dim(
            whole, place[0] * own, own, axis=0
        )

    def columns_in(self, blocks, size):
        if size % 128 == 0:
            return move_columns(blocks, self.block_of, size)
        whole = jnp.concatenate(blocks, axis=0)
        ordered = [whole[:, i * size : (i + 1) * size] for i in self.order]
        return lax.dynamic_slice_in_dim(
            jnp.concatenate(ordered + ordered, axis=1),
            self.place * size,
            self.count * size,
            axis=1,
        )

    def columns_out(self, whole, size):
        if size % 128 == 0:
            return move_columns([whole], self.step_of, size)
        start = lax.rem(self.count - self.place, self.count) * size
        ordered = lax.dynamic_slice_in_dim(
            jnp.concatenate([whole, whole], axis=1), start, self.count * size, axis=1
        )
        return jnp.concatenate(
            [ordered[:, i * size : (i + 1) * size] for i in self.place_of], axis=1
        )


class Gather:
    work = 0.0

    def __init__(self, ring, own, far, axis):
        count = ring.count
        reach = count // 2 if far else (count - 1) // 2
        self.total = count
        self.hops = (reach, count - 1 - reach)
        self.left = count - 1
        self.blocks = [own] + [None] * (count - 1)
        self.axis = axis

    def receive(self, way, hop, value):
        self.blocks[hop + 1 if way == 0 else self.total - 1 - hop] = value
        self.left -= 1

    def operand(self, way, hop, gate):
        return self.blocks[hop if way == 0 else (self.total - hop) % self.total]

    def pieces(self):
        if self.blocks[0].shape[self.axis] % 128 == 0:
            return self.blocks
        return [jnp.concatenate(self.blocks, axis=self.axis)]


class Scatter:
    work = 2.0

    def __init__(self, ring, part, far):
        count = ring.count
        reach = count // 2 if far else (count - 1) // 2
        self.total = count
        self.hops = (count - 1 - reach, reach)
        self.left = count - 1
        self.part = part
        self.got = [None, None]

    def receive(self, way, hop, value):
        self.got[way] = value
        self.left -= 1

    def operand(self, way, hop, gate):
        distance = self.hops[way] - hop
        value = self.part[distance if way == 1 else self.total - distance]
        if hop:
            (got,) = gate(self.got[way])
            value = (value.astype(f32) + got.astype(f32)).astype(bf16)
        return value

    def result(self, gate):
        got = gate(*self.got)
        return self.part[0].astype(f32) + got[0].astype(f32) + got[1].astype(f32)


class Lanes:
    def __init__(self, ring, depth):
        self.ring = ring
        self.depth = depth
        self.queue = ([], [])
        self.flying = ([], [])
        self.link = [0.0, 0.0]
        self.now = 0.0
        self.marks = []

    def gate(self, *values):
        if not self.marks:
            return values
        return lax.optimization_barrier(tuple(values) + tuple(self.marks))[: len(values)]

    def mark(self, *values):
        self.marks = list(values)

    def add(self, *chains):
        for chain in chains:
            for way in range(2):
                if chain.hops[way]:
                    self.queue[way].append(chain)
        self.fill()

    def start(self, way, chain, hop):
        (operand,) = self.gate(chain.operand(way, hop, self.gate))
        self.mark(operand)
        self.now += chain.work + 2.0
        value = lax.ppermute(operand, "dp", self.ring.pairs[way])
        begin = max(self.now, self.link[way])
        self.link[way] = begin + operand.size / 22000.0
        self.flying[way].append((self.link[way] + 3.0, chain, hop, value))

    def fill(self):
        for way in range(2):
            while self.queue[way] and len(self.flying[way]) < self.depth:
                self.start(way, self.queue[way].pop(0), 0)

    def step(self, limit):
        heads = [(self.flying[way][0][0], way) for way in range(2) if self.flying[way]]
        if not heads or min(heads)[0] > limit:
            return False
        finish, way = min(heads)
        _, chain, hop, value = self.flying[way].pop(0)
        self.now = max(self.now, finish)
        chain.receive(way, hop, value)
        if hop + 1 < chain.hops[way]:
            self.start(way, chain, hop + 1)
        else:
            self.mark(value, *self.marks)
        self.fill()
        return True

    def catch_up(self, time=None):
        time = self.now if time is None else time
        while self.step(time):
            time = max(time, self.now)
        self.now = max(self.now, time)

    def serve(self, times):
        for _ in range(2 * times):
            self.step(float("inf"))

    def until(self, *chains):
        while any(chain.left for chain in chains):
            assert self.step(float("inf"))

    def did(self, time, *values):
        self.mark(*values)
        self.now += time
        self.catch_up()


core_pairs = [(0, 1), (1, 0), (2, 3), (3, 2)]
chip_pairs = [(0, 2), (1, 3), (2, 0), (3, 1)]


def tensor_gather(own):
    return lax.all_gather(own, "tensor", axis=0, tiled=True)


def tensor_reduce(whole):
    return lax.psum_scatter(whole, "tensor", scatter_dimension=0, tiled=True)


def tensor_scatter(blocks):
    own, sibling, across, far = blocks
    far = lax.ppermute(far, "tensor", core_pairs)
    sibling, far = lax.optimization_barrier((sibling, far))
    sibling = lax.ppermute(sibling, "tensor", core_pairs)
    across = (across.astype(f32) + far.astype(f32)).astype(bf16)
    across, sibling = lax.optimization_barrier((across, sibling))
    return own, sibling, across, lax.ppermute(across, "tensor", chip_pairs)


def summed(parts):
    own, sibling, _, across = parts
    return own.astype(f32) + sibling.astype(f32) + across.astype(f32)


def tensor_sum(value):
    value = value + lax.ppermute(value, "tensor", core_pairs)
    return value + lax.ppermute(value, "tensor", chip_pairs)


def row_scale(values):
    return lax.rsqrt(jnp.mean(values * values, axis=-1, keepdims=True) + epsilon)


def norm_backward(values, scale, gain, grad):
    weighted = grad * gain
    inner = jnp.mean(weighted * values, axis=-1, keepdims=True)
    return scale * weighted - values * (scale * scale * scale * inner)


def body(
    inputs,
    segment_ids,
    gain_mixer,
    branch_weight,
    input_weight,
    conv_weight,
    conv_bias,
    rate_weight,
    rate_bias,
    entry_weight,
    entry_bias,
    decay_param,
    output_weight,
    gain_mlp,
    gate_weight,
    up_weight,
    down_weight,
    cotangent,
    *,
    dp,
    tensor,
):
    ring = Ring(dp)
    lanes = Lanes(ring, 2)
    shard, width = branch_weight.shape
    features = inputs.shape[1]
    length = segment_ids.shape[0]
    gate_blocks, piece, block_width = rate_weight.shape
    taps = conv_weight.shape[0]
    units = gate_weight.shape[1]
    place = lax.axis_index("tensor").astype(jnp.int32).reshape(1)

    table_rows = gate_blocks * piece
    wide = 256
    columns = jnp.stack(
        [conv_weight[k] for k in range(taps)] + [conv_bias, rate_bias, entry_bias, decay_param],
        axis=-1,
    )

    def padded(rows):
        return jnp.pad(rows, ((0, 0), (0, wide - rows.shape[1])))

    table = jnp.concatenate(
        [
            padded(rate_weight.reshape(table_rows, block_width)),
            padded(entry_weight.reshape(table_rows, block_width)),
            padded(columns.reshape(table_rows, taps + 4)),
            padded(jnp.stack([gain_mixer, gain_mlp])),
        ],
        axis=0,
    )
    table = jnp.pad(table, ((0, shard - 3 * table_rows - 2), (0, 0)))

    masks = []
    for offset in range(1, taps):
        earlier = jnp.concatenate(
            [jnp.full((offset,), -1, segment_ids.dtype), segment_ids[: length - offset]]
        )
        masks.append((earlier == segment_ids).astype(f32))
    masks = jnp.stack([masks[0]] + masks, axis=1)
    masks = jnp.pad(masks, ((0, 0), (0, 128 - taps)))

    half = units // 2
    halves = (slice(0, half), slice(half, units))
    table_chain = Gather(ring, table, False, 0)
    pair_chains = [Gather(ring, branch_weight, True, 0), Gather(ring, input_weight, False, 0)]
    output_chain = Gather(ring, output_weight, True, 1)
    gated_chains = [
        Gather(
            ring,
            jnp.concatenate([gate_weight[:, at], up_weight[:, at]], axis=1),
            at.start == 0,
            0,
        )
        for at in halves
    ]
    down_chains = [Gather(ring, down_weight[at], at.start == 0, 1) for at in halves]
    lanes.now = 10.0
    input_rows = tensor_gather(inputs)
    lanes.add(pair_chains[0], table_chain, pair_chains[1], output_chain, *gated_chains, *down_chains)
    cotangent_rows = tensor_gather(cotangent)

    lanes.until(table_chain)
    gates, small, gains = unpack_tables(
        lanes.gate(*table_chain.blocks),
        ring.block_of,
        width,
        piece,
        block_width,
    )
    gain_one, gain_two = gains[0], gains[1]
    decay_full = small[7:8]
    small = jnp.concatenate([small[:7], -lru_scale * jax.nn.softplus(-decay_full)], axis=0)
    mixer_rows, tokens_low = ring.normal_in(input_rows, place, shard, gain_one)
    lanes.did(18.0, mixer_rows)
    lanes.until(*pair_chains)
    (mixer_rows,) = lanes.gate(mixer_rows)

    rows = inputs.shape[0]
    start = jnp.zeros((1,), jnp.int32)
    pair_weights = [chain.pieces() for chain in pair_chains]
    pre = collect(mixer_rows, pair_weights, width, False, "mixer_in")
    lanes.did(12.0, pre)
    (pre,) = lanes.gate(pre)
    mixer_low, mixed, rate, entry, state = core_forward(start, pre, masks, gates, small, tensor)
    lanes.did(21.0, mixer_low)
    lanes.until(output_chain)
    output_pieces = output_chain.pieces()
    (mixer_low,) = lanes.gate(mixer_low)
    mixer_out = spread([(mixer_low, 0, width)], [output_pieces], place, (), False, "mixer_out")
    lanes.did(9.0, mixer_out)
    mixer_sum = tensor_reduce(mixer_out)
    arrival = lanes.now + 46.0
    (cotangent_rows,) = lanes.gate(cotangent_rows)
    cotangent_rows = ring.columns_in([cotangent_rows], shard)
    lanes.did(5.0, cotangent_rows)
    lanes.catch_up(arrival)
    (mixer_sum,) = lanes.gate(mixer_sum)
    tokens = tokens_low.astype(f32)
    middle = tokens + mixer_sum.astype(f32)
    scale_two = row_scale(middle)
    mlp_own = (middle * scale_two * gain_two).astype(bf16)
    lanes.did(5.0, mlp_own)
    mlp_rows = tensor_gather(mlp_own)
    lanes.catch_up(lanes.now + 34.0)
    (mlp_rows,) = lanes.gate(mlp_rows)

    def columns_of(array, r):
        return lax.slice_in_dim(array, r * shard, (r + 1) * shard, axis=1)

    hidden, acts, slopes = [], [], []
    for h in range(2):
        lanes.until(gated_chains[h])
        (gated,) = lanes.gate(mlp_rows)
        one, two, three = gated_forward(gated, gated_chains[h].pieces())
        hidden.append(one)
        acts.append(two)
        slopes.append(three)
        lanes.did(13.5, one)
    lefts = lanes.gate(*hidden)
    down_scatters = [
        Scatter(ring, part, h == 1)
        for h, part in enumerate(weight_grads(lefts, cotangent_rows, dp, False, "down_grads"))
    ]
    lanes.did(13.5, down_scatters[0].part[0])
    lanes.add(*down_scatters)
    gated_lows, gated_scatters = [], []

    def gated_back(h):
        lanes.until(down_chains[h])
        (gated,) = lanes.gate(cotangent_rows)
        gated_lows.append(gated_backward(gated, down_chains[h].pieces(), acts[h], slopes[h]))
        lanes.did(8.5, gated_lows[h])

    def gated_grads(h):
        (gated,) = lanes.gate(gated_lows[h])
        (part,) = weight_grads([mlp_rows], gated, dp, True, "gated_grads")
        gated_scatters.append(Scatter(ring, part, h == 0))
        lanes.did(14.0, part[0])
        lanes.add(gated_scatters[h])

    gated_back(0)
    gated_back(1)
    mlp_in_grad = None
    for h in range(2):
        (gated,) = lanes.gate(gated_lows[h])
        mlp_in_grad = spread(
            [(gated, 0, 2 * half)],
            [gated_chains[h].pieces()],
            place,
            (),
            True,
            "mlp_in_grad",
            mlp_in_grad,
        )
        lanes.did(11.0, mlp_in_grad)
    mlp_in_grad = tensor_reduce(mlp_in_grad)
    arrival = lanes.now + 46.0
    gated_grads(0)
    gated_grads(1)
    lanes.catch_up(arrival)
    (mlp_in_grad,) = lanes.gate(mlp_in_grad)
    middle_norm_grad = norm_backward(middle, scale_two, gain_two, mlp_in_grad.astype(f32))
    middle_grad = (
        lax.dynamic_slice_in_dim(cotangent_rows, place[0] * rows, rows, axis=0).astype(f32)
        + middle_norm_grad
    )
    residual_own = middle_grad.astype(bf16)
    lanes.did(6.0, residual_own)
    residual_rows = tensor_gather(residual_own)
    arrival = lanes.now + 34.0
    late = [(low, 0, half) for low in lanes.gate(*hidden)]
    mlp_out = spread(
        late, [chain.pieces() for chain in down_chains], place, (), False, "mlp_out"
    )
    lanes.did(13.0, mlp_out)
    lanes.catch_up(arrival)
    mlp_out, residual_rows = lanes.gate(mlp_out, residual_rows)
    mlp_sum = tensor_reduce(mlp_out)

    state_grad, branch_low = mixer_back(residual_rows, output_pieces, pre, state)
    lanes.did(10.5, state_grad)
    (state_grad,) = lanes.gate(state_grad)
    entry_low, gate_grads, small_grads = core_backward(
        start, state_grad, pre, mixed, rate, entry, state, masks, gates, small, tensor
    )
    lanes.did(23.0, entry_low)
    (residual_rows,) = lanes.gate(residual_rows)
    (part,) = weight_grads([mixer_low], residual_rows, dp, False, "output_grads")
    output_scatter = Scatter(ring, part, True)
    lanes.did(9.5, part[0])
    lanes.add(output_scatter)
    (low,) = lanes.gate(branch_low)
    (part,) = weight_grads([mixer_rows], low, dp, True, "branch_grads")
    pair_scatters = [Scatter(ring, part, False)]
    lanes.did(8.0, part[0])
    lanes.add(pair_scatters[0])
    (late,) = lanes.gate(branch_low)
    mixer_in_grad = spread(
        [(late, 0, width)], pair_weights[:1], place, (), True, "mixer_in_grad"
    )
    lanes.did(6.5, mixer_in_grad)
    decay_grad = lru_scale * small_grads[7:8] * jax.nn.sigmoid(-decay_full)
    small_grads = jnp.concatenate([small_grads[:7], decay_grad], axis=0)
    (gate_grads,) = lanes.gate(gate_grads)
    grad_tables = pack_tables(
        gate_grads, small_grads, ring.block_of, dp, shard, piece, block_width
    )
    lanes.did(7.5, grad_tables)
    (low,) = lanes.gate(entry_low)
    (part,) = weight_grads([mixer_rows], low, dp, True, "input_grads", (grad_tables,))
    pair_scatters.append(Scatter(ring, part, True))
    lanes.did(9.0, part[0])
    lanes.add(pair_scatters[1])
    (late,) = lanes.gate(entry_low)
    mixer_in_grad = spread(
        [(late, 0, width)], pair_weights[1:], place, (), True, "mixer_in_grad", mixer_in_grad
    )
    lanes.did(7.5, mixer_in_grad)
    mixer_in_grad = tensor_reduce(mixer_in_grad)
    arrival = lanes.now + 30.0

    (mlp_sum,) = lanes.gate(mlp_sum)
    layer_out = ring.columns_out((middle + mlp_sum.astype(f32)).astype(bf16), shard)
    lanes.did(6.0, layer_out)
    lanes.until(*gated_scatters)
    gated_wgrads = [scatter.result(lanes.gate) for scatter in gated_scatters]
    lanes.catch_up(arrival)
    (mixer_in_grad,) = lanes.gate(mixer_in_grad)
    tokens_norm_grad = norm_backward(
        tokens, row_scale(tokens), gain_one, mixer_in_grad.astype(f32)
    )
    inputs_grad = ring.columns_out((middle_grad + tokens_norm_grad).astype(bf16), shard)
    lanes.did(9.0, inputs_grad)
    lanes.until(*down_scatters, *gated_scatters, output_scatter, *pair_scatters)

    free = lambda *values: values
    pair_wgrads = [scatter.result(free) for scatter in pair_scatters]
    table_grad = pair_wgrads[1][:, width:]
    pair_wgrads = [wgrad[:, :width] for wgrad in pair_wgrads]
    rate_wgrad, entry_wgrad, column_grads = [
        table_grad[k * table_rows : (k + 1) * table_rows].reshape(gate_blocks, piece, wide)
        for k in range(3)
    ]
    rate_wgrad = rate_wgrad[:, :, :block_width]
    entry_wgrad = entry_wgrad[:, :, :block_width]
    singles = [column_grads[:, :, k] for k in range(taps + 4)]

    def gain_grad(gain, own_weights, wgrads):
        total = sum(
            jnp.sum(weight[:, : wgrad.shape[1]].astype(f32) * wgrad, axis=1)
            for weight, wgrad in zip(own_weights, wgrads)
        )
        return total / gain.astype(f32)

    gain_grads = tensor_sum(
        jnp.stack(
            [
                gain_grad(
                    gain_mixer,
                    [branch_weight, input_weight],
                    pair_wgrads,
                ),
                gain_grad(gain_mlp, [chain.blocks[0] for chain in gated_chains], gated_wgrads),
            ]
        )
    )
    return (
        layer_out,
        inputs_grad,
        gain_grads[0],
        *pair_wgrads,
        jnp.stack(singles[:taps]),
        singles[taps],
        rate_wgrad,
        singles[taps + 1],
        entry_wgrad,
        singles[taps + 2],
        singles[taps + 3],
        output_scatter.result(free),
        gain_grads[1],
        jnp.concatenate([wgrad[:, :half] for wgrad in gated_wgrads], axis=1),
        jnp.concatenate([wgrad[:, half:] for wgrad in gated_wgrads], axis=1),
        jnp.concatenate([scatter.result(free) for scatter in down_scatters], axis=0),
    )


def solution(mesh):
    return jax.shard_map(
        functools.partial(body, dp=mesh.shape["dp"], tensor=mesh.shape["tensor"]),
        mesh=mesh,
        in_specs=(
            P(("dp", "tensor"), None),
            P("dp"),
            P("dp"),
            P("dp", "tensor"),
            P("dp", "tensor"),
            P(None, "tensor", "dp"),
            P("tensor", "dp"),
            P("tensor", "dp", None),
            P("tensor", "dp"),
            P("tensor", "dp", None),
            P("tensor", "dp"),
            P("tensor", "dp"),
            P("tensor", "dp"),
            P("dp"),
            P("dp", "tensor"),
            P("dp", "tensor"),
            P("tensor", "dp"),
            P(("dp", "tensor"), None),
        ),
        out_specs=(
            P(("dp", "tensor"), None),
            P(("dp", "tensor"), None),
            P("dp"),
            P("dp", "tensor"),
            P("dp", "tensor"),
            P(None, "tensor", "dp"),
            P("tensor", "dp"),
            P("tensor", "dp", None),
            P("tensor", "dp"),
            P("tensor", "dp", None),
            P("tensor", "dp"),
            P("tensor", "dp"),
            P("tensor", "dp"),
            P("dp"),
            P("dp", "tensor"),
            P("dp", "tensor"),
            P("tensor", "dp"),
        ),
        check_vma=False,
    )
```

```python
import functools

import jax
import jax.numpy as jnp
from jax import lax
from jax.experimental import pallas as pl
from jax.experimental.pallas import tpu as pltpu
from jax.sharding import PartitionSpec as P

epsilon = 1e-06
lru_scale = 8.0
root = 0.7978845608028654
cubic = 0.044715
f32 = jnp.float32
bf16 = jnp.bfloat16
vmem_bytes = 56 * 1024 * 1024
light = pl.CostEstimate(flops=6_000_000_000, bytes_accessed=30_000_000, transcendentals=0)


def gelu_both(value):
    square = value * value
    th = jnp.tanh(root * value * (1.0 + cubic * square))
    half = 0.5 * (1.0 + th)
    slope = half + 0.5 * value * (1.0 - th * th) * (root * (1.0 + 3.0 * cubic * square))
    return value * half, slope


def gelu(value):
    return value * (0.5 * (1.0 + jnp.tanh(root * value * (1.0 + cubic * value * value))))


def one_minus_exp(x, exp_x):
    series = 1.0 + x * (1.0 / 7.0)
    for order in (6.0, 5.0, 4.0, 3.0, 2.0):
        series = 1.0 + x * (1.0 / order) * series
    return jnp.where(x > -0.5, -x * series, 1.0 - exp_x)


def decay_terms(rate, slope, keep):
    log_decay = slope * rate
    expo = jnp.exp(log_decay)
    square = expo * expo
    factor = jnp.where(keep > 0.0, jnp.sqrt(one_minus_exp(2.0 * log_decay, square)), 1.0)
    return expo * keep, square, factor


def row_index(width):
    return lax.broadcasted_iota(jnp.int32, (8, width), 0)


def down_by(current, before, offset, rows):
    if offset == 0:
        return current
    return jnp.where(
        rows < offset, pltpu.roll(before, offset, 0), pltpu.roll(current, offset, 0)
    )


def up_by(current, after, offset, rows):
    if offset == 0:
        return current
    return jnp.where(
        rows < 8 - offset,
        pltpu.roll(current, 8 - offset, 0),
        pltpu.roll(after, 8 - offset, 0),
    )


def core_forward_kernel(
    place, branch, entry_pre, masks, gates, small, out, mixed_out, rate_out, entry_out, state_out,
    mixed_low, pre, last_entry, last_state,
):
    length, width = entry_pre.shape
    rows = row_index(width)

    @pl.when(pl.program_id(0) == 0)
    def _():
        last_entry[...] = jnp.zeros_like(last_entry)
        last_state[...] = jnp.zeros_like(last_state)

    taps = [small[k : k + 1, :] for k in range(4)]
    conv_bias = small[4:5, :]

    def convolve(step, before):
        parts = []
        for half in range(2):
            at = pl.ds(pl.multiple_of(step * 16 + half * 8, 8), 8)
            here = entry_pre[at, :]
            mask = masks[at, :]
            mixed = here * taps[0] + conv_bias
            for k in range(1, 4):
                mixed += down_by(here, before, k, rows) * mask[:, k : k + 1] * taps[k]
            mixed_out[at, :] = mixed
            parts.append(mixed)
            before = here
        mixed_low[pl.ds(pl.multiple_of(step * 16, 16), 16), :] = jnp.concatenate(
            parts, axis=0
        ).astype(bf16)
        return before

    last_entry[...] = lax.fori_loop(0, length // 16, convolve, last_entry[...], unroll=8)
    pre[...] = jnp.dot(mixed_low[...], gates[...], preferred_element_type=f32)
    rate_bias = small[5:6, :]
    entry_bias = small[6:7, :]
    slope = small[7:8, :]

    def scan(step, carry):
        parts = []
        for half in range(2):
            at = pl.ds(pl.multiple_of(step * 16 + half * 8, 8), 8)
            keep = masks[at, :][:, 0:1]
            rate = jax.nn.sigmoid(pre[at, :width] + rate_bias)
            entry = jax.nn.sigmoid(pre[at, width:] + entry_bias)
            decay, _, factor = decay_terms(rate, slope, keep)
            drive = factor * entry * mixed_out[at, :]
            for shift in (1, 2, 4):
                inside = rows >= shift
                drive += decay * jnp.where(inside, pltpu.roll(drive, shift, 0), 0.0)
                decay = decay * jnp.where(inside, pltpu.roll(decay, shift, 0), 1.0)
            state = drive + decay * carry
            carry = jnp.broadcast_to(state[7:8, :], state.shape)
            rate_out[at, :] = rate
            entry_out[at, :] = entry
            state_out[at, :] = state
            parts.append(gelu(branch[at, :]) * state)
        out[pl.ds(pl.multiple_of(step * 16, 16), 16), :] = jnp.concatenate(parts, axis=0).astype(
            bf16
        )
        return carry

    last_state[...] = lax.fori_loop(0, length // 16, scan, last_state[...], unroll=8)


def core_backward_kernel(
    place, grad, entry_pre, mixed_in, rate_in, entry_in, state_in, state_tail, entry_tail,
    masks, gates, small, low, gate_grads, small_grads,
    state_long, entry_long, gate_low, mixed_grad, sums, next_decay, next_carried, next_mixed,
):
    length, width = entry_pre.shape
    rows = row_index(width)

    @pl.when(pl.program_id(0) == 0)
    def _():
        next_decay[...] = jnp.zeros_like(next_decay)
        next_carried[...] = jnp.zeros_like(next_carried)
        next_mixed[...] = jnp.zeros_like(next_mixed)
        sums[...] = jnp.zeros_like(sums)
        gate_grads[...] = jnp.zeros_like(gate_grads)

    state_long[0:8, :] = state_tail[...]
    state_long[8:, :] = state_in[...]
    entry_long[0:8, :] = entry_tail[...]
    entry_long[8:, :] = entry_pre[...]
    slope = small[7:8, :]

    def reverse(step, carry):
        after_decay, carried_after = carry
        step = length // 16 - 1 - step
        rate_parts, entry_parts = [], []
        for half in (1, 0):
            start = pl.multiple_of(step * 16 + half * 8, 8)
            at = pl.ds(start, 8)
            keep = masks[at, :][:, 0:1]
            rate = rate_in[at, :]
            entry = entry_in[at, :]
            mixed = mixed_in[at, :]
            decay, square, factor = decay_terms(rate, slope, keep)
            state = state_in[at, :]
            value = grad[at, :]
            ahead = up_by(decay, after_decay, 1, rows)
            after_decay = decay
            for shift in (1, 2, 4):
                inside = rows < 8 - shift
                value += ahead * jnp.where(inside, pltpu.roll(value, 8 - shift, 0), 0.0)
                ahead = ahead * jnp.where(inside, pltpu.roll(ahead, 8 - shift, 0), 1.0)
            carried = value + ahead * carried_after
            carried_after = jnp.broadcast_to(carried[0:1, :], carried.shape)
            earlier = down_by(state, state_long[at, :], 1, rows)
            driven = carried * entry
            log_grad = keep * (carried * earlier * decay - driven * mixed * square / factor)
            scaled = log_grad * rate
            rate_pre_grad = slope * scaled * (1.0 - rate)
            entry_pre_grad = driven * factor * mixed * (1.0 - entry)
            mixed_grad[at, :] = driven * factor
            sums[40:48, :] += rate_pre_grad
            sums[48:56, :] += entry_pre_grad
            sums[56:64, :] += scaled
            rate_parts.append(rate_pre_grad)
            entry_parts.append(entry_pre_grad)
        both = pl.ds(pl.multiple_of(step * 16, 16), 16)
        gate_low[both, :width] = jnp.concatenate(rate_parts[::-1], axis=0).astype(bf16)
        gate_low[both, width:] = jnp.concatenate(entry_parts[::-1], axis=0).astype(bf16)
        return after_decay, carried_after

    after_decay, carried_after = lax.fori_loop(
        0, length // 16, reverse, (next_decay[...], next_carried[...]), unroll=8
    )
    next_decay[...] = after_decay
    next_carried[...] = carried_after
    mixed_grad[...] += lax.dot_general(
        gate_low[...], gates[...], (((1,), (1,)), ((), ())), preferred_element_type=f32
    )
    gate_grads[...] += lax.dot_general(
        mixed_in[...].astype(bf16),
        gate_low[...],
        (((0,), (0,)), ((), ())),
        preferred_element_type=f32,
    )
    taps = [small[k : k + 1, :] for k in range(4)]

    def convolve(step, after):
        step = length // 16 - 1 - step
        parts = []
        for half in (1, 0):
            start = pl.multiple_of(step * 16 + half * 8, 8)
            at = pl.ds(start, 8)
            mask = masks[at, :]
            here = mixed_grad[at, :]
            value = entry_pre[at, :]
            before = entry_long[at, :]
            sums[32:40, :] += here
            sums[0:8, :] += here * value
            total = here * taps[0]
            masked = [here * mask[:, k : k + 1] for k in range(1, 4)]
            for k in range(1, 4):
                sums[8 * k : 8 * k + 8, :] += masked[k - 1] * down_by(value, before, k, rows)
                total += up_by(masked[k - 1], after[k - 1], k, rows) * taps[k]
            after = masked
            parts.append(total)
        low[pl.ds(pl.multiple_of(step * 16, 16), 16), :] = jnp.concatenate(
            parts[::-1], axis=0
        ).astype(bf16)
        return after

    after = lax.fori_loop(
        0,
        length // 16,
        convolve,
        [next_mixed[8 * k : 8 * k + 8, :] for k in range(3)],
        unroll=8,
    )
    for k in range(3):
        next_mixed[8 * k : 8 * k + 8, :] = after[k]

    @pl.when(pl.program_id(0) == pl.num_programs(0) - 1)
    def _():
        for k in range(8):
            small_grads[k : k + 1, :] = jnp.sum(sums[8 * k : 8 * k + 8, :], axis=0, keepdims=True)


def core_forward(place, pre, masks, gates, small, blocks):
    total, width = pre.shape[0], pre.shape[1] // 2
    length = total // blocks
    wide = lambda column: pl.BlockSpec((length, width), lambda b, t: (b ^ t[0], column))
    whole = lambda shape: pl.BlockSpec(shape, lambda b, t: (0, 0))
    kept = jax.ShapeDtypeStruct((total, width), f32)
    return pl.pallas_call(
        core_forward_kernel,
        grid_spec=pltpu.PrefetchScalarGridSpec(
            num_scalar_prefetch=1,
            grid=(blocks,),
            in_specs=[
                wide(0),
                wide(1),
                pl.BlockSpec((length, 128), lambda b, t: (b, 0)),
                whole(gates.shape),
                whole(small.shape),
            ],
            out_specs=[wide(0)] * 5,
            scratch_shapes=[
                pltpu.VMEM((length, width), bf16),
                pltpu.VMEM((length, 2 * width), f32),
                pltpu.VMEM((8, width), f32),
                pltpu.VMEM((8, width), f32),
            ],
        ),
        out_shape=[jax.ShapeDtypeStruct((total, width), bf16)] + [kept] * 4,
        compiler_params=pltpu.CompilerParams(vmem_limit_bytes=vmem_bytes),
        cost_estimate=light,
        name="core_forward",
    )(place, pre, pre, masks, gates, small)


def core_backward(place, grad, pre, mixed, rate, entry, state, masks, gates, small, blocks):
    total, width = grad.shape
    length = total // blocks
    back = lambda g: blocks - 1 - g
    wide = lambda column: pl.BlockSpec((length, width), lambda g, t: (back(g) ^ t[0], column))
    whole = lambda shape: pl.BlockSpec(shape, lambda g, t: (0, 0))

    def tail(column):
        def at(g, t):
            block = jnp.maximum(back(g) - 1, 0) ^ t[0]
            return (block * (length // 8) + length // 8 - 1, column)

        return pl.BlockSpec((8, width), at)

    return pl.pallas_call(
        core_backward_kernel,
        grid_spec=pltpu.PrefetchScalarGridSpec(
            num_scalar_prefetch=1,
            grid=(blocks,),
            in_specs=[
                wide(0),
                wide(1),
                wide(0),
                wide(0),
                wide(0),
                wide(0),
                tail(0),
                tail(1),
                pl.BlockSpec((length, 128), lambda g, t: (back(g), 0)),
                whole(gates.shape),
                whole(small.shape),
            ],
            out_specs=[
                wide(0),
                whole(gates.shape),
                whole((8, width)),
            ],
            scratch_shapes=[
                pltpu.VMEM((length + 8, width), f32),
                pltpu.VMEM((length + 8, width), f32),
                pltpu.VMEM((length, 2 * width), bf16),
                pltpu.VMEM((length, width), f32),
                pltpu.VMEM((64, width), f32),
                pltpu.VMEM((8, width), f32),
                pltpu.VMEM((8, width), f32),
                pltpu.VMEM((24, width), f32),
            ],
        ),
        out_shape=[
            jax.ShapeDtypeStruct((total, width), bf16),
            jax.ShapeDtypeStruct(gates.shape, f32),
            jax.ShapeDtypeStruct((8, width), f32),
        ],
        compiler_params=pltpu.CompilerParams(vmem_limit_bytes=vmem_bytes),
        cost_estimate=light,
        name="core_backward",
    )(place, grad, pre, mixed, rate, entry, state, state, pre, masks, gates, small)


def dot(left, right):
    return jnp.dot(left, right, preferred_element_type=f32)


def dot_rows(left, right):
    return lax.dot_general(left, right, (((0,), (0,)), ((), ())), preferred_element_type=f32)


def dot_back(left, right):
    return lax.dot_general(left, right, (((1,), (1,)), ((), ())), preferred_element_type=f32)


def fixed(shape):
    zeros = (0,) * len(shape)
    return pl.BlockSpec(shape, lambda *_: zeros)


def call(kernel, name, grid, in_specs, out_specs, out_shape, scratch=()):
    return pl.pallas_call(
        kernel,
        grid=grid,
        in_specs=in_specs,
        out_specs=out_specs,
        out_shape=out_shape,
        scratch_shapes=list(scratch),
        compiler_params=pltpu.CompilerParams(vmem_limit_bytes=vmem_bytes),
        cost_estimate=light,
        name=name,
    )


def spread(lefts, weights, place, blocks, transposed, name, base=None):
    total = lefts[0][0].shape[0]
    rows = total // 4
    pieces = len(weights[0])
    product = dot_back if transposed else dot
    sizes = [w.shape[0 if transposed else 1] for w in weights[0]]
    widths = [width for _, _, width in lefts]
    features = sum(sizes)
    terms = len(lefts)
    count = len(blocks) if blocks else 4

    def kernel(place_ref, *refs):
        left = [ref[...] for ref in refs[:terms]]
        flat = refs[terms : terms + terms * pieces]
        outs = refs[terms + terms * pieces + (base is not None) :]
        result = outs[-1]
        at = 0
        for r in range(pieces):
            value = None
            for i in range(terms):
                weight = flat[i * pieces + r]
                if transposed:
                    weight = weight[:, : widths[i]]
                else:
                    weight = weight[...]
                term = product(left[i], weight)
                value = term if value is None else value + term
            if base is not None:
                value += refs[terms + terms * pieces][:, at : at + sizes[r]].astype(f32)
            result[:, at : at + sizes[r]] = value.astype(bf16)
            at += sizes[r]
        if blocks:
            for g in range(count):

                @pl.when(pl.program_id(0) == g)
                def _():
                    outs[g][...] = result[...]

    def left_spec(column, width):
        if blocks:
            first = blocks[0]
            return pl.BlockSpec((rows, width), lambda g, t: ((first - g) ^ t[0], column))
        return pl.BlockSpec((rows, width), lambda g, t: (g, column))

    if blocks:
        out_specs = [fixed((rows, features))] * count
        out_shape = [jax.ShapeDtypeStruct((rows, features), bf16)] * count
        scratch = [pltpu.VMEM((rows, features), bf16)]
    else:
        out_specs = pl.BlockSpec((rows, features), lambda g, t: (g, 0))
        out_shape = jax.ShapeDtypeStruct((total, features), bf16)
        scratch = []
    return pl.pallas_call(
        kernel,
        grid_spec=pltpu.PrefetchScalarGridSpec(
            num_scalar_prefetch=1,
            grid=(count,),
            in_specs=[left_spec(column, width) for _, column, width in lefts]
            + [fixed(w.shape) for group in weights for w in group]
            + [pl.BlockSpec((rows, features), lambda g, t: (g, 0))] * (base is not None),
            out_specs=out_specs,
            scratch_shapes=scratch,
        ),
        out_shape=out_shape,
        compiler_params=pltpu.CompilerParams(vmem_limit_bytes=vmem_bytes),
        cost_estimate=light,
        name=name,
    )(place, *[left for left, _, _ in lefts], *[w for group in weights for w in group], *([] if base is None else [base]))


def collect(left, weights, width, transposed, name):
    total, features = left.shape
    rows = total // 4
    count = len(weights)
    pieces = len(weights[0])
    product = dot_back if transposed else dot
    sizes = [w.shape[1 if transposed else 0] for w in weights[0]]

    def kernel(*refs):
        out = refs[-1]
        for i in range(count):
            at = 0
            value = None
            for r in range(pieces):
                ref = refs[1 + i * pieces + r]
                weight = ref[...] if transposed else ref[:, :width]
                term = product(refs[0][:, at : at + sizes[r]], weight)
                value = term if value is None else value + term
                at += sizes[r]
            out[:, i * width : (i + 1) * width] = value

    return call(
        kernel,
        name,
        (4,),
        [pl.BlockSpec((rows, features), lambda g: (g, 0))]
        + [fixed(w.shape) for group in weights for w in group],
        pl.BlockSpec((rows, count * width), lambda g: (g, 0)),
        jax.ShapeDtypeStruct((total, count * width), f32),
    )(left, *[w for group in weights for w in group])


def mixer_back(left, weights, pre, state):
    total, features = left.shape
    rows = total // 4
    pieces = len(weights)
    sizes = [w.shape[1] for w in weights]
    width = state.shape[1]

    def kernel(*refs):
        branch_ref, state_ref, state_grad, branch_low = refs[1 + pieces :]
        at = 0
        value = None
        for r in range(pieces):
            term = dot_back(refs[0][:, at : at + sizes[r]], refs[1 + r][...])
            value = term if value is None else value + term
            at += sizes[r]
        act, slope = gelu_both(branch_ref[...])
        state_grad[...] = value * act
        branch_low[...] = (value * state_ref[...] * slope).astype(bf16)

    block = pl.BlockSpec((rows, width), lambda g: (g, 0))
    return call(
        kernel,
        "mixer_back",
        (4,),
        [pl.BlockSpec((rows, features), lambda g: (g, 0))]
        + [fixed(w.shape) for w in weights]
        + [block] * 2,
        [block] * 2,
        [
            jax.ShapeDtypeStruct((total, width), f32),
            jax.ShapeDtypeStruct((total, width), bf16),
        ],
    )(left, *weights, pre, state)


def gated_forward(left, weights):
    total, features = left.shape
    rows = total // 4
    pieces = len(weights)
    size = features // pieces
    units = weights[0].shape[1] // 2
    step = units // 3

    def kernel(*refs):
        left_ref = refs[0]
        hidden, act_out, slope_out = refs[1 + pieces :]
        for c in range(3):
            at = slice(c * step, (c + 1) * step)
            after = slice(units + c * step, units + (c + 1) * step)
            gate = up = None
            for r in range(pieces):
                part = left_ref[:, r * size : (r + 1) * size]
                one = dot(part, refs[1 + r][:, at])
                two = dot(part, refs[1 + r][:, after])
                gate = one if gate is None else gate + one
                up = two if up is None else up + two
            act, slope = gelu_both(gate)
            hidden[:, at] = (act * up).astype(bf16)
            act_out[:, at] = act.astype(bf16)
            slope_out[:, at] = (up * slope).astype(bf16)

    block = pl.BlockSpec((rows, units), lambda g: (g, 0))
    return call(
        kernel,
        "gated_forward",
        (4,),
        [pl.BlockSpec((rows, features), lambda g: (g, 0))] + [fixed(w.shape) for w in weights],
        [block] * 3,
        [jax.ShapeDtypeStruct((total, units), bf16)] * 3,
    )(left, *weights)


def gated_backward(left, down_pieces, act, slope):
    total, features = left.shape
    rows = total // 4
    pieces = len(down_pieces)
    size = features // pieces
    units = down_pieces[0].shape[0]

    def kernel(*refs):
        left_ref = refs[0]
        act_ref, slope_ref, out = refs[1 + pieces :]
        grad = None
        for r in range(pieces):
            term = dot_back(left_ref[:, r * size : (r + 1) * size], refs[1 + r][...])
            grad = term if grad is None else grad + term
        out[:, :units] = (grad * slope_ref[...].astype(f32)).astype(bf16)
        out[:, units:] = (grad * act_ref[...].astype(f32)).astype(bf16)

    block = pl.BlockSpec((rows, units), lambda g: (g, 0))
    return call(
        kernel,
        "gated_backward",
        (4,),
        [pl.BlockSpec((rows, features), lambda g: (g, 0))]
        + [fixed(w.shape) for w in down_pieces]
        + [block] * 2,
        pl.BlockSpec((rows, 2 * units), lambda g: (g, 0)),
        jax.ShapeDtypeStruct((total, 2 * units), bf16),
    )(left, *down_pieces, act, slope)


def weight_grads(lefts, right, pieces, by_left, name, extras=()):
    total = right.shape[0]
    terms = len(lefts)
    operands = list(lefts) + [right]
    if (lefts[0] if by_left else right).shape[1] // pieces % 128:
        return weight_grads_plain(lefts, right, pieces, by_left, extras)
    if by_left:
        (left,) = lefts
        size = left.shape[1] // pieces
        parts = len(extras) or 1
        width = right.shape[1] // parts
        more = extras[0].shape[1] if extras else 0
        shapes = [(size, width + more)] * parts
        in_specs = [pl.BlockSpec((total, size), lambda g: (0, g)), fixed(right.shape)]
        operands += extras
        in_specs += [pl.BlockSpec((size, more), lambda g: (g, 0)) for _ in extras]
    else:
        size = right.shape[1] // pieces
        parts = terms
        shapes = [(left.shape[1], size) for left in lefts]
        in_specs = [fixed(left.shape) for left in lefts] + [
            pl.BlockSpec((total, size), lambda g: (0, g))
        ]

    def kernel(*refs):
        outs = refs[len(operands) : len(operands) + parts * pieces]
        results = refs[len(operands) + parts * pieces :]
        for i in range(parts):
            if by_left:
                value = dot_rows(refs[0][...], refs[1][:, i * width : (i + 1) * width])
                results[i][:, :width] = value.astype(bf16)
                if extras:
                    results[i][:, width:] = refs[2 + i][...]
            else:
                results[i][...] = dot_rows(refs[i][...], refs[terms][...]).astype(bf16)
        for r in range(pieces):

            @pl.when(pl.program_id(0) == r)
            def _():
                for i in range(parts):
                    outs[i * pieces + r][...] = results[i][...]

    out = call(
        kernel,
        name,
        (pieces,),
        in_specs,
        [fixed(shape) for shape in shapes for _ in range(pieces)],
        [jax.ShapeDtypeStruct(shape, bf16) for shape in shapes for _ in range(pieces)],
        [pltpu.VMEM(shape, bf16) for shape in shapes],
    )(*operands)
    return [out[i * pieces : (i + 1) * pieces] for i in range(parts)]


def weight_grads_plain(lefts, right, pieces, by_left, extras):
    if not by_left:
        wholes = [dot_rows(left, right).astype(bf16) for left in lefts]
        return [jnp.split(whole, pieces, axis=1) for whole in wholes]
    wholes = jnp.split(dot_rows(lefts[0], right).astype(bf16), len(extras) or 1, axis=1)
    if extras:
        wholes = [jnp.concatenate(pair, axis=1) for pair in zip(wholes, extras)]
    return [jnp.split(whole, pieces, axis=0) for whole in wholes]


def one_hot(rows, columns, hit):
    row = lax.broadcasted_iota(jnp.int32, (rows, columns), 0)
    column = lax.broadcasted_iota(jnp.int32, (rows, columns), 1)
    return jnp.where(hit(row, column), 1.0, 0.0).astype(bf16)


def table_movers(width, shard, piece, block_width):
    table_rows = width // block_width * piece
    return [
        one_hot(
            width,
            shard,
            lambda c, row, k=k: row == k * table_rows + c // block_width * piece + c % piece,
        )
        for k in range(3)
    ]


def unpack_tables(blocks, order, width, piece, block_width):
    count = len(blocks)
    shard = blocks[0].shape[0]
    table_rows = width // block_width * piece

    def kernel(order_ref, *refs):
        flat = refs[:count]
        gates, small, gains, kept = refs[count:]
        owner = lax.broadcasted_iota(jnp.int32, (width, 256), 0) % block_width // piece
        movers = table_movers(width, shard, piece, block_width)
        picks = one_hot(8, shard, lambda row, column: column == 3 * table_rows + row)
        for r in range(count):
            table = flat[r][...]
            mine = owner == order_ref[r]
            for k in range(3):
                value = dot(movers[k], table)
                if r == 0:
                    kept[k] = jnp.where(mine, value, 0.0)
                else:
                    kept[k] = jnp.where(mine, value, kept[k])
            rows = dot(picks, table)
            gains[:, r * shard : (r + 1) * shard] = rows[:, :shard]
        spreader = one_hot(256, width, lambda row, column: row == column % block_width)
        same = lax.broadcasted_iota(jnp.int32, (width, width), 0) // block_width == (
            lax.broadcasted_iota(jnp.int32, (width, width), 1) // block_width
        )
        for k in range(2):
            value = dot(kept[k].astype(bf16), spreader)
            gates[:, k * width : (k + 1) * width] = jnp.where(same, value, 0.0).astype(bf16)
        picker = one_hot(8, 256, lambda row, column: row == column)
        small[...] = dot_back(picker, kept[2].astype(bf16))

    return pl.pallas_call(
        kernel,
        grid_spec=pltpu.PrefetchScalarGridSpec(
            num_scalar_prefetch=1,
            grid=(1,),
            in_specs=[fixed((shard, 256))] * count,
            out_specs=[
                fixed((width, 2 * width)),
                fixed((8, width)),
                fixed((8, count * shard)),
            ],
            scratch_shapes=[pltpu.VMEM((3, width, 256), f32)],
        ),
        out_shape=[
            jax.ShapeDtypeStruct((width, 2 * width), bf16),
            jax.ShapeDtypeStruct((8, width), f32),
            jax.ShapeDtypeStruct((8, count * shard), f32),
        ],
        compiler_params=pltpu.CompilerParams(vmem_limit_bytes=vmem_bytes),
        cost_estimate=light,
        name="unpack_tables",
    )(order, *blocks)


def pack_tables(gate_grads, small_grads, order, count, shard, piece, block_width):
    width = gate_grads.shape[0]

    def kernel(order_ref, gate_ref, small_ref, out):
        spreader = one_hot(256, width, lambda row, column: row == column % block_width)
        same = lax.broadcasted_iota(jnp.int32, (width, width), 0) // block_width == (
            lax.broadcasted_iota(jnp.int32, (width, width), 1) // block_width
        )
        folded = [
            dot_back(
                jnp.where(same, gate_ref[:, k * width : (k + 1) * width], 0.0).astype(bf16),
                spreader,
            )
            for k in range(2)
        ]
        picker = one_hot(8, 256, lambda row, column: row == column)
        folded.append(dot_rows(small_ref[...].astype(bf16), picker))
        owner = lax.broadcasted_iota(jnp.int32, (width, 256), 0) % block_width // piece
        movers = table_movers(width, shard, piece, block_width)
        for r in range(count):
            total = None
            for k in range(3):
                mine = jnp.where(owner == order_ref[r], folded[k], 0.0).astype(bf16)
                term = dot_rows(movers[k], mine)
                total = term if total is None else total + term
            at = slice(r * shard, (r + 1) * shard)
            out[at, :] = total.astype(bf16)

    shape = (count * shard, 256)
    return pl.pallas_call(
        kernel,
        grid_spec=pltpu.PrefetchScalarGridSpec(
            num_scalar_prefetch=1,
            grid=(1,),
            in_specs=[fixed(gate_grads.shape), fixed(small_grads.shape)],
            out_specs=fixed(shape),
        ),
        out_shape=jax.ShapeDtypeStruct(shape, bf16),
        compiler_params=pltpu.CompilerParams(vmem_limit_bytes=vmem_bytes),
        cost_estimate=light,
        name="pack_tables",
    )(order, gate_grads, small_grads)


def prepare(whole, order, place, size, gain):
    total, features = whole.shape
    rows = total // 4
    groups = features // size

    def kernel(order_ref, place_ref, value_ref, gain_ref, out, own):
        j = pl.program_id(0)

        def step(c, carry):
            at = pl.ds(pl.multiple_of(c * 16, 16), 16)
            value = value_ref[at, :].astype(f32)
            scale = lax.rsqrt(jnp.mean(value * value, axis=1, keepdims=True) + epsilon)
            for r in range(groups):
                to = slice(r * size, (r + 1) * size)
                start = pl.multiple_of(order_ref[r] * size, size)
                part = value_ref[at, pl.ds(start, size)].astype(f32)
                out[at, to] = (part * scale * gain_ref[:, to]).astype(bf16)
            return carry

        lax.fori_loop(0, rows // 16, step, 0, unroll=4)

        @pl.when(j == place_ref[0])
        def _():
            for r in range(groups):
                start = pl.multiple_of(order_ref[r] * size, size)
                own[:, r * size : (r + 1) * size] = value_ref[:, pl.ds(start, size)]

    block = pl.BlockSpec((rows, features), lambda g, *_: (g, 0))
    return pl.pallas_call(
        kernel,
        grid_spec=pltpu.PrefetchScalarGridSpec(
            num_scalar_prefetch=2,
            grid=(4,),
            in_specs=[block, fixed((1, features))],
            out_specs=[block, fixed((rows, features))],
        ),
        out_shape=[
            jax.ShapeDtypeStruct((total, features), bf16),
            jax.ShapeDtypeStruct((rows, features), bf16),
        ],
        compiler_params=pltpu.CompilerParams(vmem_limit_bytes=vmem_bytes),
        cost_estimate=light,
        name="prepare",
    )(order, place, whole, gain.reshape(1, features))


def move_columns(blocks, order, size):
    rows, features = blocks[0].shape
    groups = features // size

    def kernel(order_ref, *refs):
        out = refs[-1]
        for r in range(groups):
            start = pl.multiple_of(order_ref[r] * size, size)
            for j, ref in enumerate(refs[:-1]):
                out[j * rows : (j + 1) * rows, r * size : (r + 1) * size] = ref[
                    :, pl.ds(start, size)
                ]

    return pl.pallas_call(
        kernel,
        grid_spec=pltpu.PrefetchScalarGridSpec(
            num_scalar_prefetch=1,
            grid=(1,),
            in_specs=[fixed((rows, features))] * len(blocks),
            out_specs=fixed((rows * len(blocks), features)),
        ),
        out_shape=jax.ShapeDtypeStruct((rows * len(blocks), features), blocks[0].dtype),
        compiler_params=pltpu.CompilerParams(vmem_limit_bytes=vmem_bytes),
        cost_estimate=light,
        name="move_columns",
    )(order, *blocks)


class Ring:
    def __init__(self, count):
        self.count = count
        order = list(range(0, count, 2)) + list(range(1, count, 2))[::-1]
        self.order = order
        self.place_of = [order.index(index) for index in range(count)]
        ahead = [(order[(i + 1) % count], order[i]) for i in range(count)]
        behind = [(order[i], order[(i + 1) % count]) for i in range(count)]
        self.pairs = (ahead, behind)
        index = lax.axis_index("dp")
        half = (count + 1) // 2
        self.place = jnp.where(
            lax.rem(index, 2) == 0, lax.div(index, 2), count - 1 - lax.div(index, 2)
        ).astype(jnp.int32)
        spots = lax.rem(jnp.arange(count, dtype=jnp.int32) + self.place, count)
        self.block_of = jnp.where(spots < half, 2 * spots, 2 * (count - 1 - spots) + 1)
        self.step_of = self.steps_to(jnp.arange(count, dtype=jnp.int32))

    def steps_to(self, index):
        places = jnp.where(index % 2 == 0, index // 2, self.count - 1 - index // 2)
        return (places - self.place + self.count) % self.count

    def normal_in(self, rows, place, size, gain):
        if size % 128 == 0:
            return prepare(rows, self.block_of, place, size, gain)
        whole = self.columns_in([rows], size)
        value = whole.astype(f32)
        scale = lax.rsqrt(jnp.mean(value * value, axis=1, keepdims=True) + epsilon)
        own = whole.shape[0] // 4
        return (value * scale * gain).astype(bf16), lax.dynamic_slice_in_dim(
            whole, place[0] * own, own, axis=0
        )

    def columns_in(self, blocks, size):
        if size % 128 == 0:
            return move_columns(blocks, self.block_of, size)
        whole = jnp.concatenate(blocks, axis=0)
        ordered = [whole[:, i * size : (i + 1) * size] for i in self.order]
        return lax.dynamic_slice_in_dim(
            jnp.concatenate(ordered + ordered, axis=1),
            self.place * size,
            self.count * size,
            axis=1,
        )

    def columns_out(self, whole, size):
        if size % 128 == 0:
            return move_columns([whole], self.step_of, size)
        start = lax.rem(self.count - self.place, self.count) * size
        ordered = lax.dynamic_slice_in_dim(
            jnp.concatenate([whole, whole], axis=1), start, self.count * size, axis=1
        )
        return jnp.concatenate(
            [ordered[:, i * size : (i + 1) * size] for i in self.place_of], axis=1
        )


class Gather:
    work = 0.0

    def __init__(self, ring, own, far, axis):
        count = ring.count
        reach = count // 2 if far else (count - 1) // 2
        self.total = count
        self.hops = (reach, count - 1 - reach)
        self.left = count - 1
        self.blocks = [own] + [None] * (count - 1)
        self.axis = axis

    def receive(self, way, hop, value):
        self.blocks[hop + 1 if way == 0 else self.total - 1 - hop] = value
        self.left -= 1

    def operand(self, way, hop, gate):
        return self.blocks[hop if way == 0 else (self.total - hop) % self.total]

    def pieces(self):
        if self.blocks[0].shape[self.axis] % 128 == 0:
            return self.blocks
        return [jnp.concatenate(self.blocks, axis=self.axis)]


class Scatter:
    work = 2.0

    def __init__(self, ring, part, far):
        count = ring.count
        reach = count // 2 if far else (count - 1) // 2
        self.total = count
        self.hops = (count - 1 - reach, reach)
        self.left = count - 1
        self.part = part
        self.got = [None, None]

    def receive(self, way, hop, value):
        self.got[way] = value
        self.left -= 1

    def operand(self, way, hop, gate):
        distance = self.hops[way] - hop
        value = self.part[distance if way == 1 else self.total - distance]
        if hop:
            (got,) = gate(self.got[way])
            value = (value.astype(f32) + got.astype(f32)).astype(bf16)
        return value

    def result(self, gate):
        got = gate(*self.got)
        return self.part[0].astype(f32) + got[0].astype(f32) + got[1].astype(f32)


class Lanes:
    def __init__(self, ring, depth):
        self.ring = ring
        self.depth = depth
        self.queue = ([], [])
        self.flying = ([], [])
        self.link = [0.0, 0.0]
        self.now = 0.0
        self.marks = []

    def gate(self, *values):
        if not self.marks:
            return values
        return lax.optimization_barrier(tuple(values) + tuple(self.marks))[: len(values)]

    def mark(self, *values):
        self.marks = list(values)

    def add(self, *chains):
        for chain in chains:
            for way in range(2):
                if chain.hops[way]:
                    self.queue[way].append(chain)
        self.fill()

    def start(self, way, chain, hop):
        (operand,) = self.gate(chain.operand(way, hop, self.gate))
        self.mark(operand)
        self.now += chain.work + 2.0
        value = lax.ppermute(operand, "dp", self.ring.pairs[way])
        begin = max(self.now, self.link[way])
        self.link[way] = begin + operand.size / 22000.0
        self.flying[way].append((self.link[way] + 3.0, chain, hop, value))

    def fill(self):
        for way in range(2):
            while self.queue[way] and len(self.flying[way]) < self.depth:
                self.start(way, self.queue[way].pop(0), 0)

    def step(self, limit):
        heads = [(self.flying[way][0][0], way) for way in range(2) if self.flying[way]]
        if not heads or min(heads)[0] > limit:
            return False
        finish, way = min(heads)
        _, chain, hop, value = self.flying[way].pop(0)
        self.now = max(self.now, finish)
        chain.receive(way, hop, value)
        if hop + 1 < chain.hops[way]:
            self.start(way, chain, hop + 1)
        else:
            self.mark(value, *self.marks)
        self.fill()
        return True

    def catch_up(self, time=None):
        time = self.now if time is None else time
        while self.step(time):
            time = max(time, self.now)
        self.now = max(self.now, time)

    def serve(self, times):
        for _ in range(2 * times):
            self.step(float("inf"))

    def until(self, *chains):
        while any(chain.left for chain in chains):
            assert self.step(float("inf"))

    def did(self, time, *values):
        self.mark(*values)
        self.now += time
        self.catch_up()


core_pairs = [(0, 1), (1, 0), (2, 3), (3, 2)]
chip_pairs = [(0, 2), (1, 3), (2, 0), (3, 1)]


def tensor_gather(own):
    return lax.all_gather(own, "tensor", axis=0, tiled=True)


def tensor_reduce(whole):
    return lax.psum_scatter(whole, "tensor", scatter_dimension=0, tiled=True)


def tensor_scatter(blocks):
    own, sibling, across, far = blocks
    far = lax.ppermute(far, "tensor", core_pairs)
    sibling, far = lax.optimization_barrier((sibling, far))
    sibling = lax.ppermute(sibling, "tensor", core_pairs)
    across = (across.astype(f32) + far.astype(f32)).astype(bf16)
    across, sibling = lax.optimization_barrier((across, sibling))
    return own, sibling, across, lax.ppermute(across, "tensor", chip_pairs)


def summed(parts):
    own, sibling, _, across = parts
    return own.astype(f32) + sibling.astype(f32) + across.astype(f32)


def tensor_sum(value):
    value = value + lax.ppermute(value, "tensor", core_pairs)
    return value + lax.ppermute(value, "tensor", chip_pairs)


def row_scale(values):
    return lax.rsqrt(jnp.mean(values * values, axis=-1, keepdims=True) + epsilon)


def norm_backward(values, scale, gain, grad):
    weighted = grad * gain
    inner = jnp.mean(weighted * values, axis=-1, keepdims=True)
    return scale * weighted - values * (scale * scale * scale * inner)


def body(
    inputs,
    segment_ids,
    gain_mixer,
    branch_weight,
    input_weight,
    conv_weight,
    conv_bias,
    rate_weight,
    rate_bias,
    entry_weight,
    entry_bias,
    decay_param,
    output_weight,
    gain_mlp,
    gate_weight,
    up_weight,
    down_weight,
    cotangent,
    *,
    dp,
    tensor,
):
    ring = Ring(dp)
    lanes = Lanes(ring, 2)
    shard, width = branch_weight.shape
    features = inputs.shape[1]
    length = segment_ids.shape[0]
    gate_blocks, piece, block_width = rate_weight.shape
    taps = conv_weight.shape[0]
    units = gate_weight.shape[1]
    place = lax.axis_index("tensor").astype(jnp.int32).reshape(1)

    table_rows = gate_blocks * piece
    wide = 256
    columns = jnp.stack(
        [conv_weight[k] for k in range(taps)] + [conv_bias, rate_bias, entry_bias, decay_param],
        axis=-1,
    )

    def padded(rows):
        return jnp.pad(rows, ((0, 0), (0, wide - rows.shape[1])))

    table = jnp.concatenate(
        [
            padded(rate_weight.reshape(table_rows, block_width)),
            padded(entry_weight.reshape(table_rows, block_width)),
            padded(columns.reshape(table_rows, taps + 4)),
            padded(jnp.stack([gain_mixer, gain_mlp])),
        ],
        axis=0,
    )
    table = jnp.pad(table, ((0, shard - 3 * table_rows - 2), (0, 0)))

    masks = []
    for offset in range(1, taps):
        earlier = jnp.concatenate(
            [jnp.full((offset,), -1, segment_ids.dtype), segment_ids[: length - offset]]
        )
        masks.append((earlier == segment_ids).astype(f32))
    masks = jnp.stack([masks[0]] + masks, axis=1)
    masks = jnp.pad(masks, ((0, 0), (0, 128 - taps)))

    half = units // 2
    halves = (slice(0, half), slice(half, units))
    table_chain = Gather(ring, table, False, 0)
    pair_chains = [Gather(ring, branch_weight, True, 0), Gather(ring, input_weight, False, 0)]
    output_chain = Gather(ring, output_weight, True, 1)
    gated_chains = [
        Gather(
            ring,
            jnp.concatenate([gate_weight[:, at], up_weight[:, at]], axis=1),
            at.start == 0,
            0,
        )
        for at in halves
    ]
    down_chains = [Gather(ring, down_weight[at], at.start == 0, 1) for at in halves]
    lanes.now = 10.0
    input_rows = tensor_gather(inputs)
    lanes.add(pair_chains[0], table_chain, pair_chains[1], output_chain, *gated_chains, *down_chains)
    cotangent_rows = tensor_gather(cotangent)

    lanes.until(table_chain)
    gates, small, gains = unpack_tables(
        lanes.gate(*table_chain.blocks),
        ring.block_of,
        width,
        piece,
        block_width,
    )
    gain_one, gain_two = gains[0], gains[1]
    decay_full = small[7:8]
    small = jnp.concatenate([small[:7], -lru_scale * jax.nn.softplus(-decay_full)], axis=0)
    mixer_rows, tokens_low = ring.normal_in(input_rows, place, shard, gain_one)
    lanes.did(18.0, mixer_rows)
    lanes.until(*pair_chains)
    (mixer_rows,) = lanes.gate(mixer_rows)

    rows = inputs.shape[0]
    start = jnp.zeros((1,), jnp.int32)
    pair_weights = [chain.pieces() for chain in pair_chains]
    pre = collect(mixer_rows, pair_weights, width, False, "mixer_in")
    lanes.did(12.0, pre)
    (pre,) = lanes.gate(pre)
    mixer_low, mixed, rate, entry, state = core_forward(start, pre, masks, gates, small, tensor)
    lanes.did(21.0, mixer_low)
    lanes.until(output_chain)
    output_pieces = output_chain.pieces()
    (mixer_low,) = lanes.gate(mixer_low)
    mixer_out = spread([(mixer_low, 0, width)], [output_pieces], place, (), False, "mixer_out")
    lanes.did(9.0, mixer_out)
    mixer_sum = tensor_reduce(mixer_out)
    arrival = lanes.now + 46.0
    (cotangent_rows,) = lanes.gate(cotangent_rows)
    cotangent_rows = ring.columns_in([cotangent_rows], shard)
    lanes.did(5.0, cotangent_rows)
    lanes.catch_up(arrival)
    (mixer_sum,) = lanes.gate(mixer_sum)
    tokens = tokens_low.astype(f32)
    middle = tokens + mixer_sum.astype(f32)
    scale_two = row_scale(middle)
    mlp_own = (middle * scale_two * gain_two).astype(bf16)
    lanes.did(5.0, mlp_own)
    mlp_rows = tensor_gather(mlp_own)
    lanes.catch_up(lanes.now + 34.0)
    (mlp_rows,) = lanes.gate(mlp_rows)

    def columns_of(array, r):
        return lax.slice_in_dim(array, r * shard, (r + 1) * shard, axis=1)

    hidden, acts, slopes = [], [], []
    for h in range(2):
        lanes.until(gated_chains[h])
        (gated,) = lanes.gate(mlp_rows)
        one, two, three = gated_forward(gated, gated_chains[h].pieces())
        hidden.append(one)
        acts.append(two)
        slopes.append(three)
        lanes.did(13.5, one)
    lefts = lanes.gate(*hidden)
    down_scatters = [
        Scatter(ring, part, h == 1)
        for h, part in enumerate(weight_grads(lefts, cotangent_rows, dp, False, "down_grads"))
    ]
    lanes.did(13.5, down_scatters[0].part[0])
    lanes.add(*down_scatters)
    gated_lows, gated_scatters = [], []

    def gated_back(h):
        lanes.until(down_chains[h])
        (gated,) = lanes.gate(cotangent_rows)
        gated_lows.append(gated_backward(gated, down_chains[h].pieces(), acts[h], slopes[h]))
        lanes.did(8.5, gated_lows[h])

    def gated_grads(h):
        (gated,) = lanes.gate(gated_lows[h])
        (part,) = weight_grads([mlp_rows], gated, dp, True, "gated_grads")
        gated_scatters.append(Scatter(ring, part, h == 0))
        lanes.did(14.0, part[0])
        lanes.add(gated_scatters[h])

    gated_back(0)
    gated_back(1)
    mlp_in_grad = None
    for h in range(2):
        (gated,) = lanes.gate(gated_lows[h])
        mlp_in_grad = spread(
            [(gated, 0, 2 * half)],
            [gated_chains[h].pieces()],
            place,
            (),
            True,
            "mlp_in_grad",
            mlp_in_grad,
        )
        lanes.did(11.0, mlp_in_grad)
    mlp_in_grad = tensor_reduce(mlp_in_grad)
    arrival = lanes.now + 46.0
    gated_grads(0)
    gated_grads(1)
    lanes.catch_up(arrival)
    (mlp_in_grad,) = lanes.gate(mlp_in_grad)
    middle_norm_grad = norm_backward(middle, scale_two, gain_two, mlp_in_grad.astype(f32))
    middle_grad = (
        lax.dynamic_slice_in_dim(cotangent_rows, place[0] * rows, rows, axis=0).astype(f32)
        + middle_norm_grad
    )
    residual_own = middle_grad.astype(bf16)
    lanes.did(6.0, residual_own)
    residual_rows = tensor_gather(residual_own)
    arrival = lanes.now + 34.0
    late = [(low, 0, half) for low in lanes.gate(*hidden)]
    mlp_out = spread(
        late, [chain.pieces() for chain in down_chains], place, (), False, "mlp_out"
    )
    lanes.did(13.0, mlp_out)
    lanes.catch_up(arrival)
    mlp_out, residual_rows = lanes.gate(mlp_out, residual_rows)
    mlp_sum = tensor_reduce(mlp_out)

    state_grad, branch_low = mixer_back(residual_rows, output_pieces, pre, state)
    lanes.did(10.5, state_grad)
    (state_grad,) = lanes.gate(state_grad)
    entry_low, gate_grads, small_grads = core_backward(
        start, state_grad, pre, mixed, rate, entry, state, masks, gates, small, tensor
    )
    lanes.did(23.0, entry_low)
    (residual_rows,) = lanes.gate(residual_rows)
    (part,) = weight_grads([mixer_low], residual_rows, dp, False, "output_grads")
    output_scatter = Scatter(ring, part, True)
    lanes.did(9.5, part[0])
    lanes.add(output_scatter)
    (low,) = lanes.gate(branch_low)
    (part,) = weight_grads([mixer_rows], low, dp, True, "branch_grads")
    pair_scatters = [Scatter(ring, part, False)]
    lanes.did(8.0, part[0])
    lanes.add(pair_scatters[0])
    (late,) = lanes.gate(branch_low)
    mixer_in_grad = spread(
        [(late, 0, width)], pair_weights[:1], place, (), True, "mixer_in_grad"
    )
    lanes.did(6.5, mixer_in_grad)
    decay_grad = lru_scale * small_grads[7:8] * jax.nn.sigmoid(-decay_full)
    small_grads = jnp.concatenate([small_grads[:7], decay_grad], axis=0)
    (gate_grads,) = lanes.gate(gate_grads)
    grad_tables = pack_tables(
        gate_grads, small_grads, ring.block_of, dp, shard, piece, block_width
    )
    lanes.did(7.5, grad_tables)
    (low,) = lanes.gate(entry_low)
    (part,) = weight_grads([mixer_rows], low, dp, True, "input_grads", (grad_tables,))
    pair_scatters.append(Scatter(ring, part, True))
    lanes.did(9.0, part[0])
    lanes.add(pair_scatters[1])
    (late,) = lanes.gate(entry_low)
    mixer_in_grad = spread(
        [(late, 0, width)], pair_weights[1:], place, (), True, "mixer_in_grad", mixer_in_grad
    )
    lanes.did(7.5, mixer_in_grad)
    mixer_in_grad = tensor_reduce(mixer_in_grad)
    arrival = lanes.now + 50.0

    (mlp_sum,) = lanes.gate(mlp_sum)
    layer_out = ring.columns_out((middle + mlp_sum.astype(f32)).astype(bf16), shard)
    lanes.did(6.0, layer_out)
    lanes.until(*gated_scatters)
    gated_wgrads = [scatter.result(lanes.gate) for scatter in gated_scatters]
    lanes.catch_up(arrival)
    (mixer_in_grad,) = lanes.gate(mixer_in_grad)
    tokens_norm_grad = norm_backward(
        tokens, row_scale(tokens), gain_one, mixer_in_grad.astype(f32)
    )
    inputs_grad = ring.columns_out((middle_grad + tokens_norm_grad).astype(bf16), shard)
    lanes.did(9.0, inputs_grad)
    lanes.until(*down_scatters, *gated_scatters, output_scatter, *pair_scatters)

    free = lambda *values: values
    pair_wgrads = [scatter.result(free) for scatter in pair_scatters]
    table_grad = pair_wgrads[1][:, width:]
    pair_wgrads = [wgrad[:, :width] for wgrad in pair_wgrads]
    rate_wgrad, entry_wgrad, column_grads = [
        table_grad[k * table_rows : (k + 1) * table_rows].reshape(gate_blocks, piece, wide)
        for k in range(3)
    ]
    rate_wgrad = rate_wgrad[:, :, :block_width]
    entry_wgrad = entry_wgrad[:, :, :block_width]
    singles = [column_grads[:, :, k] for k in range(taps + 4)]

    def gain_grad(gain, own_weights, wgrads):
        total = sum(
            jnp.sum(weight[:, : wgrad.shape[1]].astype(f32) * wgrad, axis=1)
            for weight, wgrad in zip(own_weights, wgrads)
        )
        return total / gain.astype(f32)

    gain_grads = tensor_sum(
        jnp.stack(
            [
                gain_grad(
                    gain_mixer,
                    [branch_weight, input_weight],
                    pair_wgrads,
                ),
                gain_grad(gain_mlp, [chain.blocks[0] for chain in gated_chains], gated_wgrads),
            ]
        )
    )
    return (
        layer_out,
        inputs_grad,
        gain_grads[0],
        *pair_wgrads,
        jnp.stack(singles[:taps]),
        singles[taps],
        rate_wgrad,
        singles[taps + 1],
        entry_wgrad,
        singles[taps + 2],
        singles[taps + 3],
        output_scatter.result(free),
        gain_grads[1],
        jnp.concatenate([wgrad[:, :half] for wgrad in gated_wgrads], axis=1),
        jnp.concatenate([wgrad[:, half:] for wgrad in gated_wgrads], axis=1),
        jnp.concatenate([scatter.result(free) for scatter in down_scatters], axis=0),
    )


def solution(mesh):
    return jax.shard_map(
        functools.partial(body, dp=mesh.shape["dp"], tensor=mesh.shape["tensor"]),
        mesh=mesh,
        in_specs=(
            P(("dp", "tensor"), None),
            P("dp"),
            P("dp"),
            P("dp", "tensor"),
            P("dp", "tensor"),
            P(None, "tensor", "dp"),
            P("tensor", "dp"),
            P("tensor", "dp", None),
            P("tensor", "dp"),
            P("tensor", "dp", None),
            P("tensor", "dp"),
            P("tensor", "dp"),
            P("tensor", "dp"),
            P("dp"),
            P("dp", "tensor"),
            P("dp", "tensor"),
            P("tensor", "dp"),
            P(("dp", "tensor"), None),
        ),
        out_specs=(
            P(("dp", "tensor"), None),
            P(("dp", "tensor"), None),
            P("dp"),
            P("dp", "tensor"),
            P("dp", "tensor"),
            P(None, "tensor", "dp"),
            P("tensor", "dp"),
            P("tensor", "dp", None),
            P("tensor", "dp"),
            P("tensor", "dp", None),
            P("tensor", "dp"),
            P("tensor", "dp"),
            P("tensor", "dp"),
            P("dp"),
            P("dp", "tensor"),
            P("dp", "tensor"),
            P("tensor", "dp"),
        ),
        check_vma=False,
    )
```
